256 devices in a mesh: node: 64 (over z, y, core), head: 4 (over x).
Axes of the slice: x: 4, y: 4, z: 8, core: 2. Of those that a mesh axis runs over, the one named last changes fastest.
Arguments:
- features: bfloat16 [131072, 256], P(('node', 'head')), may hold values from -40 to 40
- in_weight: bfloat16 [256, 768], replicated, may hold values from -0.6 to 0.6
- out_weight: bfloat16 [256, 256], replicated, may hold values from -0.375 to 0.375
- cotangent: bfloat16 [131072, 256], P(('node', 'head')), may hold values from -6 to 6
- key_slots: int32 [1024, 12], P('node'), may hold values from 0 to 143, as said below
- block_count: int32 [1024], P('node'), may hold values from 1 to 12
- wanted: int32 [64, 64, 2], P('node'), may hold values from 0 to 15
Outputs:
- output: bfloat16 [131072, 256], P(('node', 'head'))
- feature_grad: bfloat16 [131072, 256], P(('node', 'head'))
- in_weight_grad: float32 [256, 768], P(None, 'head')
- out_weight_grad: float32 [256, 256], P('head')
The draws below stay inside these ranges and needn't reach their ends.
Inputs may be any that keep to these rules, and one draw needn't show every extreme that they name: `key_slots`: slot 0 of a query block names the block itself; the slots of one query block are distinct.
All inputs are finite; a program needn't handle non-finite values.
Results may differ from the reference program's by a relative error of at most 0.02.
The reference program's roundings to bfloat16 on the way count: a program that leaves them out, or rounds other values in their place, can miss the bound.
Values may be sent and summed in bfloat16 or wider, within the bound.
A program may use at most 128 MiB of HBM per device.

```python
import jax
import jax.numpy as jnp
from jax import lax

D = 256
HEADS = 4
HD = 64
BLOCK = 128
BLK = 16
PER = 12
CAP = 2
NODES = 131072
N_NODE = 64


def draw_features(key, part):
    key = jax.random.fold_in(key, 11)
    first = jax.random.fold_in(key, 0)
    base = jax.random.truncated_normal(first, -4.0, 4.0, (NODES, D), jnp.float32)
    return base.astype(jnp.bfloat16)


def draw_in_weight(key, part):
    key = jax.random.fold_in(key, 12)
    first = jax.random.fold_in(key, 0)
    deviation = D ** (-0.5)
    weights = jax.random.truncated_normal(first, -4.0, 4.0, (D, HEADS, 3, HD), jnp.float32) * deviation
    return weights.reshape(D, 3 * D).astype(jnp.bfloat16)


def draw_key_slots(key, part):
    key = jax.random.fold_in(key, 22)
    table_size = BLK + N_NODE * CAP
    row_total = N_NODE * BLK
    subkeys = jax.random.split(key, row_total)
    picks = jax.vmap(lambda subkey: jax.random.permutation(subkey, table_size - 1)[:PER - 1])(subkeys)
    leading = table_size - 2 - jnp.arange(PER - 1, dtype=jnp.int32)
    picks = picks.astype(jnp.int32).at[0].set(leading)
    own_block = (jnp.arange(row_total, dtype=jnp.int32) % BLK)[:, None]
    picks = picks + (picks >= own_block).astype(jnp.int32)
    return jnp.concatenate([own_block, picks], axis=1).astype(jnp.int32)


def draw_block_count(key, part):
    key = jax.random.fold_in(key, 23)
    first, second, third = jax.random.split(key, 3)
    loaded = jax.random.randint(first, (N_NODE, 1), 0, 4) == 0
    level = jnp.where(loaded, PER, jax.random.randint(second, (N_NODE, 1), 1, PER // 3 + 1))
    counts = jnp.clip(level - jax.random.randint(third, (N_NODE, BLK), 0, 2), 1, PER)
    counts = counts.reshape(-1).at[0].set(PER).at[1].set(1)
    return counts.astype(jnp.int32)


def plant(values, rng, low, largest):
    dims = values.shape
    place = [jax.random.randint(jax.random.fold_in(rng, axis), (), 0, dims[axis]) for axis in range(len(dims))]
    values = values.at[tuple(place)].set(low)
    longest = dims.index(max(dims))
    place[longest] = (place[longest] + 1) % dims[longest]
    return values.at[tuple(place)].set(largest)


def shard_levels(own_key, extent, pieces, smallest, top_value):
    level, own = 1.0, jax.random.fold_in(own_key, 6)
    for axis_at, parts in pieces:
        steps = jnp.exp(jax.random.uniform(jax.random.fold_in(own, axis_at), (parts,), jnp.float32, smallest / len(pieces), top_value / len(pieces)))
        level = level * jnp.repeat(steps, extent[axis_at] // parts).reshape([-1 if axis == axis_at else 1 for axis in range(len(extent))])
    return level


def noise(key, extent, scale, reach, shards=(), kind=jnp.bfloat16):
    array = scale * jax.random.normal(key, extent, jnp.float32)
    if shards:
        array = array * shard_levels(key, extent, shards, -0.22, 0.18)
    return jnp.clip(array, -reach, reach).astype(kind)


def setup_inputs(seed: int = 0) -> dict:
    seeds = jax.random.split(jax.random.key(seed), 8)
    return {
        "features": draw_features(jax.random.fold_in(seeds[7], 71), 0),
        "in_weight": draw_in_weight(jax.random.fold_in(seeds[7], 71), 0),
        "out_weight": noise(seeds[2], (D, D), D ** -0.5, 0.375),
        "cotangent": noise(seeds[3], (NODES, D), 1.0, 6.0, ((0, 256),)),
        "key_slots": draw_key_slots(jax.random.fold_in(seeds[7], 71), 0),
        "block_count": draw_block_count(jax.random.fold_in(seeds[7], 71), 0),
        "wanted": plant(jax.random.randint(seeds[6], (N_NODE, N_NODE, CAP), 0, BLK), jax.random.fold_in(seeds[6], 1), 0, BLK - 1).astype(jnp.int32),
    }


def block_attention(query_block, key_block, live_mask):
    score_scale = HD ** (-0.5)
    scores = jnp.einsum('qhd,pkhd->hqpk', query_block.astype(jnp.float32), key_block.astype(jnp.float32)) * score_scale
    scores = jnp.where(live_mask[None, None, :, None], scores, -1e+30)
    scores = scores.reshape(HEADS, BLOCK, PER * BLOCK)
    highest = lax.optimization_barrier(jnp.max(scores, axis=-1, keepdims=True))
    raised = jnp.exp(scores - highest)
    return raised / lax.optimization_barrier(jnp.sum(raised, axis=-1, keepdims=True))

def reference(features, in_weight, out_weight, cotangent, key_slots, block_count, wanted):
    block_total = N_NODE * BLK
    table_size = BLK + N_NODE * CAP
    score_scale = HD ** (-0.5)
    projected = jnp.dot(features, in_weight, preferred_element_type=jnp.float32).astype(jnp.bfloat16)
    projected = projected.reshape(block_total, BLOCK, HEADS, 3, HD)
    queries = projected[:, :, :, 0]
    keys_all = projected[:, :, :, 1]
    values_all = projected[:, :, :, 2]
    partition = (jnp.arange(block_total, dtype=jnp.int32) // BLK)[:, None]
    remote = jnp.maximum(key_slots - BLK, 0)
    owner = remote // CAP
    within = remote % CAP
    remote_block = owner * BLK + wanted[partition, owner, within]
    key_index = jnp.where(key_slots < BLK, partition * BLK + key_slots, remote_block).astype(jnp.int32)
    live = jnp.arange(PER, dtype=jnp.int32)[None, :] < block_count[:, None]

    def forward(index):
        chosen = key_index[index]
        attention = block_attention(queries[index], keys_all[chosen], live[index])
        attention_low = attention.astype(jnp.bfloat16).reshape(HEADS, BLOCK, PER, BLOCK)
        result = jnp.einsum('hqpk,pkhd->qhd', attention_low.astype(jnp.float32), values_all[chosen].astype(jnp.float32))
        return result.astype(jnp.bfloat16)
    attended = lax.map(forward, jnp.arange(block_total, dtype=jnp.int32)).reshape(NODES, D)
    summed = features.astype(jnp.float32) + jnp.dot(attended, out_weight, preferred_element_type=jnp.float32)
    root_mean = jnp.sqrt(lax.optimization_barrier(jnp.mean(summed * summed, axis=-1, keepdims=True)) + 1e-06)
    normed = summed / root_mean
    output = normed.astype(jnp.bfloat16)
    upstream = cotangent.astype(jnp.float32)
    norm_grad = (upstream - normed * lax.optimization_barrier(jnp.mean(upstream * normed, axis=-1, keepdims=True))) / root_mean
    norm_grad_low = norm_grad.astype(jnp.bfloat16)
    out_weight_grad = jnp.dot(attended.T, norm_grad_low, preferred_element_type=jnp.float32) * NODES ** (-0.5)
    attended_grad = jnp.dot(norm_grad_low, out_weight.T, preferred_element_type=jnp.float32).astype(jnp.bfloat16)
    grad_blocks = attended_grad.reshape(block_total, BLOCK, HEADS, HD)
    attended_blocks = attended.reshape(block_total, BLOCK, HEADS, HD)
    row_dots = lax.optimization_barrier(jnp.sum(grad_blocks.astype(jnp.float32) * attended_blocks.astype(jnp.float32), axis=-1))

    def block_backward(tables, index):
        key_table, value_table = tables
        chosen = key_index[index]
        slots = key_slots[index]
        key_block = keys_all[chosen]
        value_block = values_all[chosen]
        attention = block_attention(queries[index], key_block, live[index])
        attention_low = attention.astype(jnp.bfloat16).reshape(HEADS, BLOCK, PER, BLOCK)
        prob_grad = jnp.einsum('qhd,pkhd->hqpk', grad_blocks[index].astype(jnp.float32), value_block.astype(jnp.float32))
        prob_grad = prob_grad.reshape(HEADS, BLOCK, PER * BLOCK)
        score_grad = attention * (prob_grad - jnp.transpose(row_dots[index])[:, :, None]) * score_scale
        score_grad = score_grad.astype(jnp.bfloat16).reshape(HEADS, BLOCK, PER, BLOCK).astype(jnp.float32)
        query_grad = jnp.einsum('hqpk,pkhd->qhd', score_grad, key_block.astype(jnp.float32))
        key_grad = jnp.einsum('hqpk,qhd->pkhd', score_grad, queries[index].astype(jnp.float32))
        value_grad = jnp.einsum('hqpk,qhd->pkhd', attention_low.astype(jnp.float32), grad_blocks[index].astype(jnp.float32))
        return ((key_table.at[slots].add(key_grad), value_table.at[slots].add(value_grad)), query_grad.astype(jnp.bfloat16))

    def partition_backward(carry, rank):
        key_sums, value_sums = carry
        blank_table = jnp.zeros((table_size, BLOCK, HEADS, HD), jnp.float32)
        indices = rank * BLK + jnp.arange(BLK, dtype=jnp.int32)
        (key_table, value_table), query_grads = lax.scan(block_backward, (blank_table, blank_table), indices)
        remote_keys = lax.optimization_barrier(key_table[BLK:].astype(jnp.bfloat16)).astype(jnp.float32)
        remote_values = lax.optimization_barrier(value_table[BLK:].astype(jnp.bfloat16)).astype(jnp.float32)
        targets = (jnp.arange(N_NODE, dtype=jnp.int32)[:, None] * BLK + wanted[rank]).reshape(-1).astype(jnp.int32)
        key_sums = key_sums.at[indices].add(key_table[:BLK]).at[targets].add(remote_keys)
        value_sums = value_sums.at[indices].add(value_table[:BLK]).at[targets].add(remote_values)
        return ((key_sums, value_sums), query_grads)
    blank = jnp.zeros((block_total, BLOCK, HEADS, HD), jnp.float32)
    (key_sums, value_sums), query_grads = lax.scan(partition_backward, (blank, blank), jnp.arange(N_NODE, dtype=jnp.int32))
    query_grads = query_grads.reshape(block_total, BLOCK, HEADS, HD)
    projected_grad = jnp.stack([query_grads, key_sums.astype(jnp.bfloat16), value_sums.astype(jnp.bfloat16)], axis=3)
    projected_grad = projected_grad.reshape(NODES, 3 * D)
    feature_grad = (norm_grad + jnp.dot(projected_grad, in_weight.T, preferred_element_type=jnp.float32)).astype(jnp.bfloat16)
    in_weight_grad = jnp.dot(features.T, projected_grad, preferred_element_type=jnp.float32) * NODES ** (-0.5)
    return (output, feature_grad, in_weight_grad, out_weight_grad)
```

```python
import jax
import jax.numpy as jnp
from jax import lax
from jax.experimental import pallas as pl
from jax.experimental.pallas import tpu as pltpu
from jax.sharding import PartitionSpec as P

HEADS = 4
HD = 64
BLOCK = 128
BLK = 16
PER = 12
CAP = 2
PAIR = 2 * HD
SCALE = HD ** (-0.5)
NT = (((1,), (1,)), ((), ()))
TN = (((0,), (0,)), ((), ()))


def dot(a, b, dims=(((1,), (0,)), ((), ()))):
    return lax.dot_general(a, b, dims, preferred_element_type=jnp.float32)


def forward_kernel(slots_ref, count_ref, q_ref, table_ref, out_ref, stat_ref):
    b = pl.program_id(0)
    count = count_ref[b]
    query = q_ref[...]
    chosen = [table_ref[slots_ref[b * PER + j]] for j in range(PER)]
    scores = []
    for j in range(0, PER, 2):
        pair = dot(query, jnp.concatenate(chosen[j : j + 2], axis=0), NT)
        key = lax.broadcasted_iota(jnp.int32, pair.shape, 1) + j * BLOCK
        scores.append(jnp.where(key < count * BLOCK, pair, -1e30))
    highest = scores[0]
    for part in scores[1:]:
        highest = jnp.maximum(highest, part)
    highest = jnp.max(highest, axis=1, keepdims=True)
    total = jnp.zeros((BLOCK, 2 * BLOCK), jnp.float32)
    result = jnp.zeros((BLOCK, PAIR), jnp.float32)
    for j, part in enumerate(scores):
        raised = jnp.exp(part - highest)
        total = total + raised
        result = result + dot(
            raised.astype(jnp.bfloat16), jnp.concatenate(chosen[2 * j : 2 * j + 2], axis=0)
        )
    total = jnp.sum(total, axis=1, keepdims=True)
    out_ref[...] = (result / total).astype(jnp.bfloat16)
    lane = lax.broadcasted_iota(jnp.int32, stat_ref.shape, 1)
    stat_ref[...] = jnp.where(lane < HD, highest, 1.0 / total)


def forward(slots, count, query, table):
    rows = BLK * BLOCK
    grid_spec = pltpu.PrefetchScalarGridSpec(
        num_scalar_prefetch=2,
        grid=(BLK,),
        in_specs=[
            pl.BlockSpec((BLOCK, PAIR), lambda b, *_: (b, 0)),
            pl.BlockSpec(table.shape, lambda b, *_: (0, 0, 0)),
        ],
        out_specs=[
            pl.BlockSpec((BLOCK, PAIR), lambda b, *_: (b, 0)),
            pl.BlockSpec((BLOCK, PAIR), lambda b, *_: (b, 0)),
        ],
    )
    return pl.pallas_call(
        forward_kernel,
        grid_spec=grid_spec,
        out_shape=(
            jax.ShapeDtypeStruct((rows, PAIR), jnp.bfloat16),
            jax.ShapeDtypeStruct((rows, PAIR), jnp.float32),
        ),
        compiler_params=pltpu.CompilerParams(vmem_limit_bytes=40 << 20),
        cost_estimate=pl.CostEstimate(
            flops=4 * BLK * PER * BLOCK**3, bytes_accessed=8 << 20, transcendentals=BLK * PER * BLOCK**2
        ),
        name="attend",
    )(slots, count, query, table)


def backward_kernel(
    slots_ref, count_ref, qg_ref, att_ref, stat_ref, table_ref, dq_ref, own_ref, far_ref, acc_ref
):
    b = pl.program_id(0)
    own_slots = own_ref.shape[0]

    @pl.when(b == 0)
    def _():
        acc_ref[...] = jnp.zeros_like(acc_ref)

    count = count_ref[b]
    both = qg_ref[...]
    lane = lax.broadcasted_iota(jnp.int32, both.shape, 1)
    zero = jnp.zeros_like(both)
    stacked = jnp.concatenate(
        [jnp.where(lane < HD, both, zero), jnp.where(lane < HD, zero, both)], axis=0
    )
    dots = jnp.sum(
        jnp.where(lane < HD, 0.0, both.astype(jnp.float32) * att_ref[...].astype(jnp.float32)),
        axis=1,
        keepdims=True,
    )
    highest = stat_ref[:, 0:1]
    inverse = stat_ref[:, HD : HD + 1]
    dq = jnp.zeros((BLOCK, PAIR), jnp.float32)
    for j in range(0, PER, 2):
        slots = [slots_ref[b * PER + j + i] for i in range(2)]
        chosen = jnp.concatenate([table_ref[s] for s in slots], axis=0)
        products = dot(stacked, chosen, NT)
        key = lax.broadcasted_iota(jnp.int32, (BLOCK, 2 * BLOCK), 1) + j * BLOCK
        scores = jnp.where(key < count * BLOCK, products[:BLOCK], -1e30)
        attention = jnp.exp(scores - highest) * inverse
        score_grad = (attention * (products[BLOCK:] - dots)).astype(jnp.bfloat16)
        dq = dq + dot(score_grad, chosen)
        pair = jnp.concatenate([score_grad, attention.astype(jnp.bfloat16)], axis=0)
        grads = dot(pair, stacked, TN)
        for i in range(2):
            acc_ref[slots[i]] += grads[i * BLOCK : (i + 1) * BLOCK]
    dq_ref[...] = (dq * SCALE).astype(jnp.bfloat16)

    @pl.when(b == pl.num_programs(0) - 1)
    def _():
        own_ref[...] = acc_ref[:own_slots]
        far_ref[...] = acc_ref[own_slots:].astype(jnp.bfloat16)


def backward(slots, count, query_grad, attended, stat, table):
    rows = BLK * BLOCK
    far = table.shape[0] - BLK
    whole = lambda shape: pl.BlockSpec(shape, lambda b, *_: (0,) * len(shape))
    rowwise = pl.BlockSpec((BLOCK, PAIR), lambda b, *_: (b, 0))
    grid_spec = pltpu.PrefetchScalarGridSpec(
        num_scalar_prefetch=2,
        grid=(BLK,),
        in_specs=[rowwise, rowwise, rowwise, whole(table.shape)],
        out_specs=[rowwise, whole((BLK, BLOCK, PAIR)), whole((far, BLOCK, PAIR))],
        scratch_shapes=[pltpu.VMEM(table.shape, jnp.float32)],
    )
    return pl.pallas_call(
        backward_kernel,
        grid_spec=grid_spec,
        out_shape=(
            jax.ShapeDtypeStruct((rows, PAIR), jnp.bfloat16),
            jax.ShapeDtypeStruct((BLK, BLOCK, PAIR), jnp.float32),
            jax.ShapeDtypeStruct((far, BLOCK, PAIR), jnp.bfloat16),
        ),
        compiler_params=pltpu.CompilerParams(vmem_limit_bytes=56 << 20),
        cost_estimate=pl.CostEstimate(
            flops=10 * BLK * PER * BLOCK**3, bytes_accessed=16 << 20, transcendentals=BLK * PER * BLOCK**2
        ),
        name="attend_back",
    )(slots, count, query_grad, attended, stat, table)


def on_device(features, in_weight, out_weight, cotangent, key_slots, block_count, wanted):
    node_count = lax.axis_size("node")
    node_rows = BLK * BLOCK
    total_nodes = node_rows * node_count
    projected = jnp.dot(features, in_weight, preferred_element_type=jnp.float32).astype(
        jnp.bfloat16
    )
    projected = lax.all_to_all(projected, "head", split_axis=1, concat_axis=0, tiled=True)
    queries = projected[:, :HD] * jnp.bfloat16(SCALE)
    paired = projected[:, HD:].reshape(BLK, BLOCK, PAIR)
    requests = lax.all_to_all(wanted, "node", split_axis=1, concat_axis=0, tiled=True).reshape(-1)
    outgoing = paired[requests].reshape(node_count, CAP, BLOCK, PAIR)
    incoming = lax.all_to_all(outgoing, "node", split_axis=0, concat_axis=0, tiled=True)
    table = jnp.concatenate([paired, incoming.reshape(node_count * CAP, BLOCK, PAIR)], axis=0)
    slots = key_slots.reshape(-1)
    padded = jnp.concatenate([queries, jnp.zeros_like(queries)], axis=1)
    wide, stat = forward(slots, block_count, padded, table)
    attended = wide[:, HD:]
    attended_rows = lax.all_to_all(attended, "head", split_axis=0, concat_axis=1, tiled=True)
    summed = features.astype(jnp.float32) + jnp.dot(
        attended_rows, out_weight, preferred_element_type=jnp.float32
    )
    root_mean = jnp.sqrt(jnp.mean(summed * summed, axis=-1, keepdims=True) + 1e-06)
    normed = summed / root_mean
    output = normed.astype(jnp.bfloat16)
    upstream = cotangent.astype(jnp.float32)
    norm_grad = (
        upstream - normed * jnp.mean(upstream * normed, axis=-1, keepdims=True)
    ) / root_mean
    norm_grad_low = norm_grad.astype(jnp.bfloat16)
    out_weight_grad = jnp.dot(attended_rows.T, norm_grad_low, preferred_element_type=jnp.float32)
    attended_grad = jnp.dot(norm_grad_low, out_weight.T, preferred_element_type=jnp.float32).astype(
        jnp.bfloat16
    )
    attended_grad = lax.all_to_all(attended_grad, "head", split_axis=1, concat_axis=0, tiled=True)
    both = jnp.concatenate([queries, attended_grad], axis=1)
    dq, own, leaving = backward(slots, block_count, both, wide, stat, table)
    returned = lax.all_to_all(
        leaving.reshape(node_count, CAP, BLOCK, PAIR), "node", split_axis=0, concat_axis=0, tiled=True
    )
    returned = returned.astype(jnp.float32).reshape(node_count * CAP, BLOCK, PAIR)
    pair_grads = own.at[requests].add(returned).astype(jnp.bfloat16).reshape(node_rows, PAIR)
    projected_grad = jnp.concatenate([dq[:, :HD], pair_grads], axis=1)
    grad_rows_back = lax.all_to_all(projected_grad, "head", split_axis=0, concat_axis=1, tiled=True)
    feature_grad = norm_grad + jnp.dot(
        grad_rows_back, in_weight.T, preferred_element_type=jnp.float32
    )
    in_weight_grad = jnp.dot(features.T, grad_rows_back, preferred_element_type=jnp.float32)
    in_weight_grad, out_weight_grad = (
        lax.psum_scatter(in_weight_grad, "head", scatter_dimension=1, tiled=True),
        lax.psum_scatter(out_weight_grad, "head", scatter_dimension=0, tiled=True),
    )
    in_weight_grad, out_weight_grad = lax.psum((in_weight_grad, out_weight_grad), "node")
    grad_factor = total_nodes ** (-0.5)
    return (
        output,
        feature_grad.astype(jnp.bfloat16),
        in_weight_grad * grad_factor,
        out_weight_grad * grad_factor,
    )


def solution(mesh):
    placed = (
        P(("node", "head"), None),
        P(),
        P(),
        P(("node", "head"), None),
        P("node", None),
        P("node"),
        P("node", None, None),
    )
    return jax.shard_map(
        on_device,
        mesh=mesh,
        in_specs=placed,
        out_specs=(
            P(("node", "head"), None),
            P(("node", "head"), None),
            P(None, "head"),
            P("head", None),
        ),
        check_vma=False,
    )
```

```python
import functools

import jax
import jax.numpy as jnp
from jax import lax
from jax.experimental import pallas as pl
from jax.experimental.pallas import tpu as pltpu
from jax.sharding import PartitionSpec as P

HEADS = 4
HD = 64
BLOCK = 128
BLK = 16
PER = 12
CAP = 2
PAIR = 2 * HD
SCALE = HD ** (-0.5)
NT = (((1,), (1,)), ((), ()))
TN = (((0,), (0,)), ((), ()))
MESH = pl.DeviceIdType.MESH


def dot(a, b, dims=(((1,), (0,)), ((), ()))):
    return lax.dot_general(a, b, dims, preferred_element_type=jnp.float32)


def forward_kernel(slots_ref, count_ref, q_ref, table_ref, out_ref, stat_ref):
    b = pl.program_id(0)
    count = count_ref[b]
    query = q_ref[...]
    chosen = [table_ref[slots_ref[b * PER + j]] for j in range(PER)]
    scores = []
    for j in range(0, PER, 2):
        pair = dot(query, jnp.concatenate(chosen[j : j + 2], axis=0), NT)
        key = lax.broadcasted_iota(jnp.int32, pair.shape, 1) + j * BLOCK
        scores.append(jnp.where(key < count * BLOCK, pair, -1e30))
    highest = scores[0]
    for part in scores[1:]:
        highest = jnp.maximum(highest, part)
    highest = jnp.max(highest, axis=1, keepdims=True)
    total = jnp.zeros((BLOCK, 2 * BLOCK), jnp.float32)
    result = jnp.zeros((BLOCK, PAIR), jnp.float32)
    for j, part in enumerate(scores):
        raised = jnp.exp(part - highest)
        total = total + raised
        result = result + dot(
            raised.astype(jnp.bfloat16), jnp.concatenate(chosen[2 * j : 2 * j + 2], axis=0)
        )
    total = jnp.sum(total, axis=1, keepdims=True)
    out_ref[...] = (result / total).astype(jnp.bfloat16)
    lane = lax.broadcasted_iota(jnp.int32, stat_ref.shape, 1)
    stat_ref[...] = jnp.where(lane < HD, highest, 1.0 / total)


def forward(slots, count, query, table):
    rows = BLK * BLOCK
    grid_spec = pltpu.PrefetchScalarGridSpec(
        num_scalar_prefetch=2,
        grid=(BLK,),
        in_specs=[
            pl.BlockSpec((BLOCK, PAIR), lambda b, *_: (b, 0)),
            pl.BlockSpec(table.shape, lambda b, *_: (0, 0, 0)),
        ],
        out_specs=[
            pl.BlockSpec((BLOCK, PAIR), lambda b, *_: (b, 0)),
            pl.BlockSpec((BLOCK, PAIR), lambda b, *_: (b, 0)),
        ],
    )
    return pl.pallas_call(
        forward_kernel,
        grid_spec=grid_spec,
        out_shape=(
            jax.ShapeDtypeStruct((rows, PAIR), jnp.bfloat16),
            jax.ShapeDtypeStruct((rows, PAIR), jnp.float32),
        ),
        compiler_params=pltpu.CompilerParams(vmem_limit_bytes=40 << 20),
        cost_estimate=pl.CostEstimate(
            flops=4 * BLK * PER * BLOCK**3, bytes_accessed=8 << 20, transcendentals=BLK * PER * BLOCK**2
        ),
        name="attend",
    )(slots, count, query, table)


def backward_kernel(
    slots_ref, count_ref, qg_ref, att_ref, stat_ref, table_ref, dq_ref, own_ref, far_ref, acc_ref
):
    b = pl.program_id(0)
    own_slots = own_ref.shape[0]

    @pl.when(b == 0)
    def _():
        acc_ref[...] = jnp.zeros_like(acc_ref)

    count = count_ref[b]
    both = qg_ref[...]
    lane = lax.broadcasted_iota(jnp.int32, both.shape, 1)
    zero = jnp.zeros_like(both)
    stacked = jnp.concatenate(
        [jnp.where(lane < HD, both, zero), jnp.where(lane < HD, zero, both)], axis=0
    )
    dots = jnp.sum(
        jnp.where(lane < HD, 0.0, both.astype(jnp.float32) * att_ref[...].astype(jnp.float32)),
        axis=1,
        keepdims=True,
    )
    highest = stat_ref[:, 0:1]
    inverse = stat_ref[:, HD : HD + 1]
    dq = jnp.zeros((BLOCK, PAIR), jnp.float32)
    for j in range(0, PER, 2):
        slots = [slots_ref[b * PER + j + i] for i in range(2)]
        chosen = jnp.concatenate([table_ref[s] for s in slots], axis=0)
        products = dot(stacked, chosen, NT)
        key = lax.broadcasted_iota(jnp.int32, (BLOCK, 2 * BLOCK), 1) + j * BLOCK
        scores = jnp.where(key < count * BLOCK, products[:BLOCK], -1e30)
        attention = jnp.exp(scores - highest) * inverse
        score_grad = (attention * (products[BLOCK:] - dots)).astype(jnp.bfloat16)
        dq = dq + dot(score_grad, chosen)
        pair = jnp.concatenate([score_grad, attention.astype(jnp.bfloat16)], axis=0)
        grads = dot(pair, stacked, TN)
        for i in range(2):
            acc_ref[slots[i]] += grads[i * BLOCK : (i + 1) * BLOCK]
    dq_ref[...] = (dq * SCALE).astype(jnp.bfloat16)

    @pl.when(b == pl.num_programs(0) - 1)
    def _():
        own_ref[...] = acc_ref[:own_slots]
        far_ref[...] = acc_ref[own_slots:].astype(jnp.bfloat16)


def backward(slots, count, query_grad, attended, stat, table):
    rows = BLK * BLOCK
    far = table.shape[0] - BLK
    whole = lambda shape: pl.BlockSpec(shape, lambda b, *_: (0,) * len(shape))
    rowwise = pl.BlockSpec((BLOCK, PAIR), lambda b, *_: (b, 0))
    grid_spec = pltpu.PrefetchScalarGridSpec(
        num_scalar_prefetch=2,
        grid=(BLK,),
        in_specs=[rowwise, rowwise, rowwise, whole(table.shape)],
        out_specs=[rowwise, whole((BLK, BLOCK, PAIR)), whole((far, BLOCK, PAIR))],
        scratch_shapes=[pltpu.VMEM(table.shape, jnp.float32)],
    )
    return pl.pallas_call(
        backward_kernel,
        grid_spec=grid_spec,
        out_shape=(
            jax.ShapeDtypeStruct((rows, PAIR), jnp.bfloat16),
            jax.ShapeDtypeStruct((BLK, BLOCK, PAIR), jnp.float32),
            jax.ShapeDtypeStruct((far, BLOCK, PAIR), jnp.bfloat16),
        ),
        compiler_params=pltpu.CompilerParams(vmem_limit_bytes=56 << 20),
        cost_estimate=pl.CostEstimate(
            flops=10 * BLK * PER * BLOCK**3, bytes_accessed=16 << 20, transcendentals=BLK * PER * BLOCK**2
        ),
        name="attend_back",
    )(slots, count, query_grad, attended, stat, table)


def torus(node_count):
    rows = 4 if node_count >= 64 else 2
    return node_count // (2 * rows), rows * 2


def weights_kernel(
    planes, group, in_ref, out_ref, sum_ref,
    mine, x_in, x_sum, z_in, z_sum, g_in, piece,
    x_send, x_recv, z_send, z_recv, g_send, g_recv, p_send, p_recv, f_send, f_recv,
):
    node, head = lax.axis_index("node"), lax.axis_index("head")
    z, g = node // group, node % group
    rows = sum_ref.shape[2]
    x_peers = [(node, (head + d) % HEADS) for d in range(1, HEADS)]
    z_peers = [(((z + d) % planes) * group + g, head) for d in range(1, planes)]
    g_peers = [(z * group + (g + d) % group, head) for d in range(1, group)]
    barrier = pltpu.get_barrier_semaphore()
    for peer in x_peers + z_peers + g_peers:
        pl.semaphore_signal(barrier, inc=1, device_id=peer, device_id_type=MESH)

    for h in range(HEADS):
        chunk = jnp.concatenate(
            [in_ref[h * 3 * HD : (h + 1) * 3 * HD], out_ref[h * HD : (h + 1) * HD]], axis=0
        )
        chunk = jnp.concatenate([chunk[:, :128], chunk[:, 128:]], axis=0)
        mine[h] = chunk.reshape(planes, group, rows, 128)
    pl.semaphore_wait(barrier, len(x_peers + z_peers + g_peers))

    copies = [
        pltpu.make_async_remote_copy(
            mine.at[peer[1]], x_in.at[d], x_send.at[d], x_recv.at[d], device_id=peer, device_id_type=MESH
        )
        for d, peer in enumerate(x_peers)
    ]
    for copy in copies:
        copy.start()
    for copy in copies:
        copy.wait()
    x_sum[...] = mine[head] + x_in[0] + x_in[1] + x_in[2]

    copies = [
        pltpu.make_async_remote_copy(
            x_sum.at[(z + d + 1) % planes], z_in.at[d], z_send.at[d], z_recv.at[d],
            device_id=peer, device_id_type=MESH,
        )
        for d, peer in enumerate(z_peers)
    ]
    for copy in copies:
        copy.start()
    for copy in copies:
        copy.wait()
    total = x_sum[z]
    for d in range(planes - 1):
        total = total + z_in[d]
    z_sum[...] = total

    copies = [
        pltpu.make_async_remote_copy(
            z_sum.at[(g + d + 1) % group], g_in.at[d], g_send.at[d], g_recv.at[d],
            device_id=peer, device_id_type=MESH,
        )
        for d, peer in enumerate(g_peers)
    ]
    for copy in copies:
        copy.start()
    for copy in copies:
        copy.wait()
    total = z_sum[g]
    for d in range(group - 1):
        total = total + g_in[d]
    piece[...] = total

    copies = [
        pltpu.make_async_remote_copy(
            piece, sum_ref.at[z, g], p_send.at[d], p_recv.at[d], device_id=peer, device_id_type=MESH
        )
        for d, peer in enumerate(g_peers)
    ]
    for copy in copies:
        copy.start()
    sum_ref[z, g] = total
    for copy in copies:
        copy.wait()

    copies = [
        pltpu.make_async_remote_copy(
            sum_ref.at[z], sum_ref.at[z], f_send.at[d], f_recv.at[d], device_id=peer, device_id_type=MESH
        )
        for d, peer in enumerate(z_peers)
    ]
    for copy in copies:
        copy.start()
    for copy in copies:
        copy.wait()


def sum_weights(in_grad, out_grad, node_count):
    planes, group = torus(node_count)
    rows = 4 * HD * 2 // (planes * group)
    full = (planes, group, rows, 128)
    dma = lambda n: pltpu.SemaphoreType.DMA((n,))
    vmem = pl.BlockSpec(memory_space=pltpu.VMEM)
    total = pl.pallas_call(
        functools.partial(weights_kernel, planes, group),
        out_shape=jax.ShapeDtypeStruct(full, jnp.float32),
        in_specs=[vmem, vmem],
        out_specs=vmem,
        scratch_shapes=[
            pltpu.VMEM((HEADS,) + full, jnp.float32),
            pltpu.VMEM((HEADS - 1,) + full, jnp.float32),
            pltpu.VMEM(full, jnp.float32),
            pltpu.VMEM((planes - 1,) + full[1:], jnp.float32),
            pltpu.VMEM(full[1:], jnp.float32),
            pltpu.VMEM((group - 1,) + full[2:], jnp.float32),
            pltpu.VMEM(full[2:], jnp.float32),
            dma(HEADS - 1), dma(HEADS - 1),
            dma(planes - 1), dma(planes - 1),
            dma(group - 1), dma(group - 1),
            dma(group - 1), dma(group - 1),
            dma(planes - 1), dma(planes - 1),
        ],
        compiler_params=pltpu.CompilerParams(
            collective_id=1, has_side_effects=True, vmem_limit_bytes=32 << 20
        ),
        name="sum_weights",
    )(in_grad, out_grad)
    total = total.reshape(2, 4 * HD, 128).transpose(1, 0, 2).reshape(4 * HD, 2 * 128)
    return total[: 3 * HD].T, total[3 * HD :]


def on_device(features, in_weight, out_weight, cotangent, key_slots, block_count, wanted):
    node_count = lax.axis_size("node")
    node_rows = BLK * BLOCK
    total_nodes = node_rows * node_count
    projected = jnp.dot(features, in_weight, preferred_element_type=jnp.float32).astype(
        jnp.bfloat16
    )
    projected = lax.all_to_all(projected, "head", split_axis=1, concat_axis=0, tiled=True)
    queries = projected[:, :HD] * jnp.bfloat16(SCALE)
    paired = projected[:, HD:].reshape(BLK, BLOCK, PAIR)
    requests = lax.all_to_all(wanted, "node", split_axis=1, concat_axis=0, tiled=True).reshape(-1)
    outgoing = paired[requests].reshape(node_count, CAP, BLOCK, PAIR)
    incoming = lax.all_to_all(outgoing, "node", split_axis=0, concat_axis=0, tiled=True)
    table = jnp.concatenate([paired, incoming.reshape(node_count * CAP, BLOCK, PAIR)], axis=0)
    slots = key_slots.reshape(-1)
    padded = jnp.concatenate([queries, jnp.zeros_like(queries)], axis=1)
    wide, stat = forward(slots, block_count, padded, table)
    attended = wide[:, HD:]
    attended_rows = lax.all_to_all(attended, "head", split_axis=0, concat_axis=1, tiled=True)
    summed = features.astype(jnp.float32) + jnp.dot(
        attended_rows, out_weight, preferred_element_type=jnp.float32
    )
    root_mean = jnp.sqrt(jnp.mean(summed * summed, axis=-1, keepdims=True) + 1e-06)
    normed = summed / root_mean
    output = normed.astype(jnp.bfloat16)
    upstream = cotangent.astype(jnp.float32)
    norm_grad = (
        upstream - normed * jnp.mean(upstream * normed, axis=-1, keepdims=True)
    ) / root_mean
    norm_grad_low = norm_grad.astype(jnp.bfloat16)
    out_weight_grad = jnp.dot(attended_rows.T, norm_grad_low, preferred_element_type=jnp.float32)
    attended_grad = jnp.dot(norm_grad_low, out_weight.T, preferred_element_type=jnp.float32).astype(
        jnp.bfloat16
    )
    attended_grad = lax.all_to_all(attended_grad, "head", split_axis=1, concat_axis=0, tiled=True)
    both = jnp.concatenate([queries, attended_grad], axis=1)
    dq, own, leaving = backward(slots, block_count, both, wide, stat, table)
    returned = lax.all_to_all(
        leaving.reshape(node_count, CAP, BLOCK, PAIR), "node", split_axis=0, concat_axis=0, tiled=True
    )
    returned = returned.astype(jnp.float32).reshape(node_count * CAP, BLOCK, PAIR)
    pair_grads = own.at[requests].add(returned).astype(jnp.bfloat16).reshape(node_rows, PAIR)
    projected_grad = jnp.concatenate([dq[:, :HD], pair_grads], axis=1)
    grad_rows_back = lax.all_to_all(projected_grad, "head", split_axis=0, concat_axis=1, tiled=True)
    feature_grad = norm_grad + jnp.dot(
        grad_rows_back, in_weight.T, preferred_element_type=jnp.float32
    )
    in_weight_grad = lax.dot_general(
        grad_rows_back, features, TN, preferred_element_type=jnp.float32
    )
    in_weight_grad, out_weight_grad = sum_weights(in_weight_grad, out_weight_grad, node_count)
    grad_factor = total_nodes ** (-0.5)
    return (
        output,
        feature_grad.astype(jnp.bfloat16),
        in_weight_grad * grad_factor,
        out_weight_grad * grad_factor,
    )


def solution(mesh):
    placed = (
        P(("node", "head"), None),
        P(),
        P(),
        P(("node", "head"), None),
        P("node", None),
        P("node"),
        P("node", None, None),
    )
    return jax.shard_map(
        on_device,
        mesh=mesh,
        in_specs=placed,
        out_specs=(
            P(("node", "head"), None),
            P(("node", "head"), None),
            P(None, "head"),
            P("head", None),
        ),
        check_vma=False,
    )
```

```python
import functools

import jax
import jax.numpy as jnp
from jax import lax
from jax.experimental import pallas as pl
from jax.experimental.pallas import tpu as pltpu
from jax.sharding import PartitionSpec as P

HEADS = 4
HD = 64
BLOCK = 128
BLK = 16
PER = 12
CAP = 2
PAIR = 2 * HD
SCALE = HD ** (-0.5)
NT = (((1,), (1,)), ((), ()))
TN = (((0,), (0,)), ((), ()))
MESH = pl.DeviceIdType.MESH


def dot(a, b, dims=(((1,), (0,)), ((), ()))):
    return lax.dot_general(a, b, dims, preferred_element_type=jnp.float32)


def forward_kernel(slots_ref, count_ref, q_ref, table_ref, out_ref, stat_ref):
    b = pl.program_id(0)
    count = count_ref[b]
    query = q_ref[...]
    chosen = [table_ref[slots_ref[b * PER + j]] for j in range(PER)]
    scores = []
    for j in range(0, PER, 2):
        pair = dot(query, jnp.concatenate(chosen[j : j + 2], axis=0), NT)
        key = lax.broadcasted_iota(jnp.int32, pair.shape, 1) + j * BLOCK
        scores.append(jnp.where(key < count * BLOCK, pair, -1e30))
    highest = scores[0]
    for part in scores[1:]:
        highest = jnp.maximum(highest, part)
    highest = jnp.max(highest, axis=1, keepdims=True)
    total = jnp.zeros((BLOCK, 2 * BLOCK), jnp.float32)
    result = jnp.zeros((BLOCK, PAIR), jnp.float32)
    for j, part in enumerate(scores):
        raised = jnp.exp(part - highest)
        total = total + raised
        result = result + dot(
            raised.astype(jnp.bfloat16), jnp.concatenate(chosen[2 * j : 2 * j + 2], axis=0)
        )
    total = jnp.sum(total, axis=1, keepdims=True)
    out_ref[...] = (result / total).astype(jnp.bfloat16)
    lane = lax.broadcasted_iota(jnp.int32, stat_ref.shape, 1)
    stat_ref[...] = jnp.where(lane < HD, highest, 1.0 / total)


def forward(slots, count, query, table):
    rows = BLK * BLOCK
    grid_spec = pltpu.PrefetchScalarGridSpec(
        num_scalar_prefetch=2,
        grid=(BLK,),
        in_specs=[
            pl.BlockSpec((BLOCK, PAIR), lambda b, *_: (b, 0)),
            pl.BlockSpec(table.shape, lambda b, *_: (0, 0, 0)),
        ],
        out_specs=[
            pl.BlockSpec((BLOCK, PAIR), lambda b, *_: (b, 0)),
            pl.BlockSpec((BLOCK, PAIR), lambda b, *_: (b, 0)),
        ],
    )
    return pl.pallas_call(
        forward_kernel,
        grid_spec=grid_spec,
        out_shape=(
            jax.ShapeDtypeStruct((rows, PAIR), jnp.bfloat16),
            jax.ShapeDtypeStruct((rows, PAIR), jnp.float32),
        ),
        compiler_params=pltpu.CompilerParams(vmem_limit_bytes=40 << 20),
        cost_estimate=pl.CostEstimate(
            flops=4 * BLK * PER * BLOCK**3, bytes_accessed=8 << 20, transcendentals=BLK * PER * BLOCK**2
        ),
        name="attend",
    )(slots, count, query, table)


def backward_kernel(
    slots_ref, count_ref, qg_ref, att_ref, stat_ref, table_ref, dq_ref, own_ref, far_ref, acc_ref
):
    b = pl.program_id(0)
    own_slots = own_ref.shape[0]

    @pl.when(b == 0)
    def _():
        acc_ref[...] = jnp.zeros_like(acc_ref)

    count = count_ref[b]
    both = qg_ref[...]
    lane = lax.broadcasted_iota(jnp.int32, both.shape, 1)
    zero = jnp.zeros_like(both)
    stacked = jnp.concatenate(
        [jnp.where(lane < HD, both, zero), jnp.where(lane < HD, zero, both)], axis=0
    )
    dots = jnp.sum(
        jnp.where(lane < HD, 0.0, both.astype(jnp.float32) * att_ref[...].astype(jnp.float32)),
        axis=1,
        keepdims=True,
    )
    highest = stat_ref[:, 0:1]
    inverse = stat_ref[:, HD : HD + 1]
    dq = jnp.zeros((BLOCK, PAIR), jnp.float32)
    for j in range(0, PER, 2):
        slots = [slots_ref[b * PER + j + i] for i in range(2)]
        chosen = jnp.concatenate([table_ref[s] for s in slots], axis=0)
        products = dot(stacked, chosen, NT)
        key = lax.broadcasted_iota(jnp.int32, (BLOCK, 2 * BLOCK), 1) + j * BLOCK
        scores = jnp.where(key < count * BLOCK, products[:BLOCK], -1e30)
        attention = jnp.exp(scores - highest) * inverse
        score_grad = (attention * (products[BLOCK:] - dots)).astype(jnp.bfloat16)
        dq = dq + dot(score_grad, chosen)
        pair = jnp.concatenate([score_grad, attention.astype(jnp.bfloat16)], axis=0)
        grads = dot(pair, stacked, TN)
        for i in range(2):
            acc_ref[slots[i]] += grads[i * BLOCK : (i + 1) * BLOCK]
    dq_ref[...] = (dq * SCALE).astype(jnp.bfloat16)

    @pl.when(b == pl.num_programs(0) - 1)
    def _():
        own_ref[...] = acc_ref[:own_slots]
        far_ref[...] = acc_ref[own_slots:].astype(jnp.bfloat16)


def backward(slots, count, query_grad, attended, stat, table):
    rows = BLK * BLOCK
    far = table.shape[0] - BLK
    whole = lambda shape: pl.BlockSpec(shape, lambda b, *_: (0,) * len(shape))
    rowwise = pl.BlockSpec((BLOCK, PAIR), lambda b, *_: (b, 0))
    grid_spec = pltpu.PrefetchScalarGridSpec(
        num_scalar_prefetch=2,
        grid=(BLK,),
        in_specs=[rowwise, rowwise, rowwise, whole(table.shape)],
        out_specs=[rowwise, whole((BLK, BLOCK, PAIR)), whole((far, BLOCK, PAIR))],
        scratch_shapes=[pltpu.VMEM(table.shape, jnp.float32)],
    )
    return pl.pallas_call(
        backward_kernel,
        grid_spec=grid_spec,
        out_shape=(
            jax.ShapeDtypeStruct((rows, PAIR), jnp.bfloat16),
            jax.ShapeDtypeStruct((BLK, BLOCK, PAIR), jnp.float32),
            jax.ShapeDtypeStruct((far, BLOCK, PAIR), jnp.bfloat16),
        ),
        compiler_params=pltpu.CompilerParams(vmem_limit_bytes=56 << 20),
        cost_estimate=pl.CostEstimate(
            flops=10 * BLK * PER * BLOCK**3, bytes_accessed=16 << 20, transcendentals=BLK * PER * BLOCK**2
        ),
        name="attend_back",
    )(slots, count, query_grad, attended, stat, table)


def torus(node_count):
    rows = 4 if node_count >= 64 else 2
    return node_count // (2 * rows), rows * 2


def weights_kernel(
    planes, group, in_ref, out_ref, sum_ref,
    mine, x_in, x_sum, z_in, z_sum, g_in, piece,
    x_send, x_recv, z_send, z_recv, g_send, g_recv, p_send, p_recv, f_send, f_recv,
):
    node, head = lax.axis_index("node"), lax.axis_index("head")
    z, g = node // group, node % group
    rows = sum_ref.shape[2]
    x_peers = [(node, (head + d) % HEADS) for d in range(1, HEADS)]
    z_peers = [(((z + d) % planes) * group + g, head) for d in range(1, planes)]
    g_peers = [(z * group + (g + d) % group, head) for d in range(1, group)]
    barrier = pltpu.get_barrier_semaphore()
    for peer in x_peers + z_peers + g_peers:
        pl.semaphore_signal(barrier, inc=1, device_id=peer, device_id_type=MESH)

    for h in range(HEADS):
        chunk = jnp.concatenate(
            [in_ref[h * 3 * HD : (h + 1) * 3 * HD], out_ref[h * HD : (h + 1) * HD]], axis=0
        )
        chunk = jnp.concatenate([chunk[:, :128], chunk[:, 128:]], axis=0)
        mine[h] = chunk.reshape(planes, group, rows, 128)
    pl.semaphore_wait(barrier, len(x_peers + z_peers + g_peers))

    copies = [
        pltpu.make_async_remote_copy(
            mine.at[peer[1]], x_in.at[d], x_send.at[d], x_recv.at[d], device_id=peer, device_id_type=MESH
        )
        for d, peer in enumerate(x_peers)
    ]
    for copy in copies:
        copy.start()
    for copy in copies:
        copy.wait()
    x_sum[...] = mine[head] + x_in[0] + x_in[1] + x_in[2]

    copies = [
        pltpu.make_async_remote_copy(
            x_sum.at[(z + d + 1) % planes], z_in.at[d], z_send.at[d], z_recv.at[d],
            device_id=peer, device_id_type=MESH,
        )
        for d, peer in enumerate(z_peers)
    ]
    for copy in copies:
        copy.start()
    for copy in copies:
        copy.wait()
    total = x_sum[z]
    for d in range(planes - 1):
        total = total + z_in[d]
    z_sum[...] = total

    copies = [
        pltpu.make_async_remote_copy(
            z_sum.at[(g + d + 1) % group], g_in.at[d], g_send.at[d], g_recv.at[d],
            device_id=peer, device_id_type=MESH,
        )
        for d, peer in enumerate(g_peers)
    ]
    for copy in copies:
        copy.start()
    for copy in copies:
        copy.wait()
    total = z_sum[g]
    for d in range(group - 1):
        total = total + g_in[d]
    piece[...] = total

    copies = [
        pltpu.make_async_remote_copy(
            piece, sum_ref.at[z, g], p_send.at[d], p_recv.at[d], device_id=peer, device_id_type=MESH
        )
        for d, peer in enumerate(g_peers)
    ]
    for copy in copies:
        copy.start()
    sum_ref[z, g] = total
    for copy in copies:
        copy.wait()

    copies = [
        pltpu.make_async_remote_copy(
            sum_ref.at[z], sum_ref.at[z], f_send.at[d], f_recv.at[d], device_id=peer, device_id_type=MESH
        )
        for d, peer in enumerate(z_peers)
    ]
    for copy in copies:
        copy.start()
    for copy in copies:
        copy.wait()


def sum_weights(in_grad, out_grad, node_count):
    planes, group = torus(node_count)
    rows = 4 * HD * 2 // (planes * group)
    full = (planes, group, rows, 128)
    dma = lambda n: pltpu.SemaphoreType.DMA((n,))
    vmem = pl.BlockSpec(memory_space=pltpu.VMEM)
    total = pl.pallas_call(
        functools.partial(weights_kernel, planes, group),
        out_shape=jax.ShapeDtypeStruct(full, jnp.float32),
        in_specs=[vmem, vmem],
        out_specs=vmem,
        scratch_shapes=[
            pltpu.VMEM((HEADS,) + full, jnp.float32),
            pltpu.VMEM((HEADS - 1,) + full, jnp.float32),
            pltpu.VMEM(full, jnp.float32),
            pltpu.VMEM((planes - 1,) + full[1:], jnp.float32),
            pltpu.VMEM(full[1:], jnp.float32),
            pltpu.VMEM((group - 1,) + full[2:], jnp.float32),
            pltpu.VMEM(full[2:], jnp.float32),
            dma(HEADS - 1), dma(HEADS - 1),
            dma(planes - 1), dma(planes - 1),
            dma(group - 1), dma(group - 1),
            dma(group - 1), dma(group - 1),
            dma(planes - 1), dma(planes - 1),
        ],
        compiler_params=pltpu.CompilerParams(
            collective_id=1, has_side_effects=True, vmem_limit_bytes=32 << 20
        ),
        name="sum_weights",
    )(in_grad, out_grad)
    total = total.reshape(2, 4 * HD, 128).transpose(1, 0, 2).reshape(4 * HD, 2 * 128)
    return total[: 3 * HD].T, total[3 * HD :]


def ring_order(planes):
    half = planes // 2
    return [0] + [s * k for k in range(1, half) for s in (-1, 1)] + [half]


def fetch_kernel(
    planes, group, own_ref, asked_ref, pairs_ref, mine_ref, query_ref, table_ref, rows_ref, asks_ref,
    whole, ring, chunk, picked, made, asks,
    a_send, a_recv, b_send, b_recv, q_send, q_recv, r_send, r_recv, g_send, g_recv, x_send, x_recv, asks_sem,
):
    node, head = lax.axis_index("node"), lax.axis_index("head")
    z, g = node // group, node % group
    half = planes // 2
    part = BLOCK // HEADS
    x_peers = [(node, (head + d) % HEADS) for d in range(1, HEADS)]
    g_peers = [(z * group + (g + d) % group, head) for d in range(1, group)]
    right = (((z + 1) % planes) * group + g, head)
    left = (((z + planes - 1) % planes) * group + g, head)

    def remote(source, target, send, recv, peer):
        return pltpu.make_async_remote_copy(
            source, target, send, recv, device_id=peer, device_id_type=MESH
        )

    def quarter(h):
        return pl.ds(pl.multiple_of(h * part, part), part)

    barrier = pltpu.get_barrier_semaphore()
    for peer in x_peers + g_peers + [left, right]:
        pl.semaphore_signal(barrier, inc=1, device_id=peer, device_id_type=MESH)
    pl.semaphore_wait(barrier, len(x_peers + g_peers) + 2)

    own_blocks = pl.ds(head * HEADS, HEADS)
    first, rest = [], []
    for d, peer in enumerate(x_peers):
        rows = quarter(peer[1])
        first.append(
            remote(own_ref.at[:, rows], whole.at[own_blocks, rows], a_send.at[d], a_recv.at[d], peer)
        )
    for e in range(1, HEADS):
        for d, peer in enumerate(x_peers):
            rows = quarter((peer[1] + e) % HEADS)
            rest.append(
                remote(
                    own_ref.at[:, rows], whole.at[own_blocks, rows],
                    b_send.at[d, e - 1], b_recv.at[d, e - 1], peer,
                )
            )
    questions = [
        remote(asked_ref.at[peer[0] % group], asks_ref.at[g], q_send.at[d], q_recv.at[d], peer)
        for d, peer in enumerate(g_peers)
    ]
    for copy in first + questions + rest:
        copy.start()
    whole[own_blocks] = own_ref[...]
    asks_ref[g] = asked_ref[g]
    for copy in first:
        copy.wait_recv()
    ring[z] = whole[:, quarter(head)]

    def hop(way, k):
        at = (z - k + planes) % planes if way == 0 else (z + k) % planes
        view = ring.at[at]
        if k == half - 1:
            view = view.at[pl.ds(0, BLK // 2)] if way == 0 else view.at[pl.ds(BLK // 2, BLK // 2)]
        return remote(
            view, view, r_send.at[way, k], r_recv.at[way, k], right if way == 0 else left
        )

    hops = {(way, k): hop(way, k) for way in range(2) for k in range(half)}
    for way in range(2):
        hops[way, 0].start()
    for copy in questions:
        copy.wait_recv()
    answer = pltpu.make_async_copy(asks_ref, asks, asks_sem)
    answer.start()
    answer.wait()

    order = ring_order(planes)
    sent = []

    def bring(t):
        offset = order[t]
        at = (z + offset + planes) % planes
        if offset == half:
            hops[0, half - 1].wait_recv()
            hops[1, half - 1].wait_recv()
        elif offset:
            way, k = (0, -offset) if offset < 0 else (1, offset)
            hops[way, k - 1].wait_recv()
            hops[way, k].start()
        chunk[...] = ring[at]
        for d in range(group - 1, -1, -1):
            peer = (g + d) % group
            for c in range(CAP):
                block = chunk[asks[peer, 0, at * CAP + c]]
                if d:
                    picked[at, d - 1, c] = block
                else:
                    rows_ref[at, g, c] = block
            if d:
                copy = remote(
                    picked.at[at, d - 1], rows_ref.at[at, g], g_send.at[at, d - 1], g_recv.at[at, d - 1],
                    g_peers[d - 1],
                )
                copy.start()
                sent.append(copy)

    arriving = []

    def make(t):
        at = (z + order[t] + planes) % planes
        for d in range(1, group):
            remote(
                picked.at[at, d - 1], rows_ref.at[at, g], g_send.at[at, d - 1], g_recv.at[at, d - 1],
                g_peers[d - 1],
            ).wait_recv()
        rows = rows_ref[at].reshape(group * CAP * part, 2 * BLOCK)
        pairs = dot(rows, pairs_ref[...]).astype(jnp.bfloat16)
        for h in range(HEADS):
            made[at, h] = pairs[:, h * PAIR : (h + 1) * PAIR].reshape(group * CAP, part, PAIR)
        slots = pl.ds(BLK + at * group * CAP, group * CAP)
        for d, peer in enumerate(x_peers):
            copy = remote(
                made.at[at, peer[1]], table_ref.at[slots, quarter(head)], x_send.at[at, d], x_recv.at[at, d],
                peer,
            )
            copy.start()
            sent.append(copy)
            arriving.append(copy)
        table_ref[slots, quarter(head)] = made[at, head]

    bring(0)
    for copy in rest:
        copy.wait_recv()

    @pl.loop(0, BLK)
    def _(b):
        both = dot(whole[b], mine_ref[...])
        query_ref[b] = (both[:, :PAIR] * SCALE).astype(jnp.bfloat16)
        table_ref[b] = both[:, PAIR:].astype(jnp.bfloat16)

    for t in range(1, planes):
        bring(t)
        make(t - 1)
    make(planes - 1)
    for copy in arriving:
        copy.wait_recv()
    for copy in first + rest + questions + list(hops.values()) + sent:
        copy.wait_send()


def fetch(features, in_weight, wanted, node_count):
    planes, group = torus(node_count)
    part = BLOCK // HEADS
    head = lax.axis_index("head")
    own = features.reshape(HEADS, BLOCK, 2 * BLOCK)
    asked = wanted.reshape(planes, group, CAP).transpose(1, 0, 2).reshape(group, 1, planes * CAP)
    asked = jnp.pad(asked, ((0, 0), (0, 7), (0, 128 - planes * CAP)))
    columns = in_weight.reshape(2 * BLOCK, HEADS, 3 * HD)
    pairs = columns[:, :, HD:].reshape(2 * BLOCK, HEADS * PAIR)
    mine = lax.dynamic_index_in_dim(columns, head, axis=1, keepdims=False)
    mine = jnp.concatenate([mine[:, :HD], jnp.zeros_like(mine[:, :HD]), mine[:, HD:]], axis=1)
    dma = lambda *shape: pltpu.SemaphoreType.DMA(shape)
    vmem = pl.BlockSpec(memory_space=pltpu.VMEM)
    slots = BLK + planes * group * CAP
    return pl.pallas_call(
        functools.partial(fetch_kernel, planes, group),
        out_shape=(
            jax.ShapeDtypeStruct((BLK, BLOCK, PAIR), jnp.bfloat16),
            jax.ShapeDtypeStruct((slots, BLOCK, PAIR), jnp.bfloat16),
            jax.ShapeDtypeStruct((planes, group, CAP, part, 2 * BLOCK), jnp.bfloat16),
            jax.ShapeDtypeStruct((group, 8, 128), jnp.int32),
        ),
        in_specs=[vmem] * 4,
        out_specs=(vmem,) * 4,
        scratch_shapes=[
            pltpu.VMEM((BLK, BLOCK, 2 * BLOCK), jnp.bfloat16),
            pltpu.VMEM((planes, BLK, part, 2 * BLOCK), jnp.bfloat16),
            pltpu.VMEM((BLK, part, 2 * BLOCK), jnp.bfloat16),
            pltpu.VMEM((planes, group - 1, CAP, part, 2 * BLOCK), jnp.bfloat16),
            pltpu.VMEM((planes, HEADS, group * CAP, part, PAIR), jnp.bfloat16),
            pltpu.SMEM((group, 8, 128), jnp.int32),
            dma(3), dma(3), dma(3, 3), dma(3, 3), dma(group - 1), dma(group - 1),
            dma(2, planes // 2), dma(2, planes // 2),
            dma(planes, group - 1), dma(planes, group - 1), dma(planes, 3), dma(planes, 3),
            pltpu.SemaphoreType.DMA,
        ],
        compiler_params=pltpu.CompilerParams(
            collective_id=2, has_side_effects=True, vmem_limit_bytes=48 << 20
        ),
        name="fetch",
    )(own, asked, pairs, mine)


def on_device(features, in_weight, out_weight, cotangent, key_slots, block_count, wanted):
    node_count = lax.axis_size("node")
    node_rows = BLK * BLOCK
    total_nodes = node_rows * node_count
    queries, table, rows, asks = fetch(features, in_weight, wanted, node_count)
    queries = queries.reshape(node_rows, PAIR)
    requests = lax.all_to_all(wanted, "node", split_axis=1, concat_axis=0, tiled=True).reshape(-1)
    slots = key_slots.reshape(-1)
    wide, stat = forward(slots, block_count, queries, table)
    attended = wide[:, HD:]
    attended_rows = lax.all_to_all(attended, "head", split_axis=0, concat_axis=1, tiled=True)
    summed = features.astype(jnp.float32) + jnp.dot(
        attended_rows, out_weight, preferred_element_type=jnp.float32
    )
    root_mean = jnp.sqrt(jnp.mean(summed * summed, axis=-1, keepdims=True) + 1e-06)
    normed = summed / root_mean
    output = normed.astype(jnp.bfloat16)
    upstream = cotangent.astype(jnp.float32)
    norm_grad = (
        upstream - normed * jnp.mean(upstream * normed, axis=-1, keepdims=True)
    ) / root_mean
    norm_grad_low = norm_grad.astype(jnp.bfloat16)
    out_weight_grad = jnp.dot(attended_rows.T, norm_grad_low, preferred_element_type=jnp.float32)
    attended_grad = jnp.dot(norm_grad_low, out_weight.T, preferred_element_type=jnp.float32).astype(
        jnp.bfloat16
    )
    attended_grad = lax.all_to_all(attended_grad, "head", split_axis=1, concat_axis=0, tiled=True)
    both = jnp.concatenate([queries[:, :HD], attended_grad], axis=1)
    dq, own, leaving = backward(slots, block_count, both, wide, stat, table)
    returned = lax.all_to_all(
        leaving.reshape(node_count, CAP, BLOCK, PAIR), "node", split_axis=0, concat_axis=0, tiled=True
    )
    returned = returned.astype(jnp.float32).reshape(node_count * CAP, BLOCK, PAIR)
    pair_grads = own.at[requests].add(returned).astype(jnp.bfloat16).reshape(node_rows, PAIR)
    projected_grad = jnp.concatenate([dq[:, :HD], pair_grads], axis=1)
    grad_rows_back = lax.all_to_all(projected_grad, "head", split_axis=0, concat_axis=1, tiled=True)
    feature_grad = norm_grad + jnp.dot(
        grad_rows_back, in_weight.T, preferred_element_type=jnp.float32
    )
    in_weight_grad = lax.dot_general(
        grad_rows_back, features, TN, preferred_element_type=jnp.float32
    )
    in_weight_grad, out_weight_grad = sum_weights(in_weight_grad, out_weight_grad, node_count)
    grad_factor = total_nodes ** (-0.5)
    return (
        output,
        feature_grad.astype(jnp.bfloat16),
        in_weight_grad * grad_factor,
        out_weight_grad * grad_factor,
    )


def solution(mesh):
    placed = (
        P(("node", "head"), None),
        P(),
        P(),
        P(("node", "head"), None),
        P("node", None),
        P("node"),
        P("node", None, None),
    )
    return jax.shard_map(
        on_device,
        mesh=mesh,
        in_specs=placed,
        out_specs=(
            P(("node", "head"), None),
            P(("node", "head"), None),
            P(None, "head"),
            P("head", None),
        ),
        check_vma=False,
    )
```

```python
import functools

import jax
import jax.numpy as jnp
from jax import lax
from jax.experimental import pallas as pl
from jax.experimental.pallas import tpu as pltpu
from jax.sharding import PartitionSpec as P

HEADS = 4
HD = 64
BLOCK = 128
BLK = 16
PER = 12
CAP = 2
PAIR = 2 * HD
SCALE = HD ** (-0.5)
NT = (((1,), (1,)), ((), ()))
TN = (((0,), (0,)), ((), ()))
MESH = pl.DeviceIdType.MESH


def dot(a, b, dims=(((1,), (0,)), ((), ()))):
    return lax.dot_general(a, b, dims, preferred_element_type=jnp.float32)


def forward_kernel(slots_ref, count_ref, q_ref, table_ref, out_ref, stat_ref):
    b = pl.program_id(0)
    count = count_ref[b]
    query = q_ref[...]
    chosen = [table_ref[slots_ref[b * PER + j]] for j in range(PER)]
    scores = []
    for j in range(0, PER, 2):
        pair = dot(query, jnp.concatenate(chosen[j : j + 2], axis=0), NT)
        key = lax.broadcasted_iota(jnp.int32, pair.shape, 1) + j * BLOCK
        scores.append(jnp.where(key < count * BLOCK, pair, -1e30))
    highest = scores[0]
    for part in scores[1:]:
        highest = jnp.maximum(highest, part)
    highest = jnp.max(highest, axis=1, keepdims=True)
    total = jnp.zeros((BLOCK, 2 * BLOCK), jnp.float32)
    result = jnp.zeros((BLOCK, PAIR), jnp.float32)
    for j, part in enumerate(scores):
        raised = jnp.exp(part - highest)
        total = total + raised
        result = result + dot(
            raised.astype(jnp.bfloat16), jnp.concatenate(chosen[2 * j : 2 * j + 2], axis=0)
        )
    total = jnp.sum(total, axis=1, keepdims=True)
    out_ref[...] = (result / total).astype(jnp.bfloat16)
    lane = lax.broadcasted_iota(jnp.int32, stat_ref.shape, 1)
    stat_ref[...] = jnp.where(lane < HD, highest, 1.0 / total)


def forward(slots, count, query, table):
    rows = BLK * BLOCK
    grid_spec = pltpu.PrefetchScalarGridSpec(
        num_scalar_prefetch=2,
        grid=(BLK,),
        in_specs=[
            pl.BlockSpec((BLOCK, PAIR), lambda b, *_: (b, 0)),
            pl.BlockSpec(table.shape, lambda b, *_: (0, 0, 0)),
        ],
        out_specs=[
            pl.BlockSpec((BLOCK, PAIR), lambda b, *_: (b, 0)),
            pl.BlockSpec((BLOCK, PAIR), lambda b, *_: (b, 0)),
        ],
    )
    return pl.pallas_call(
        forward_kernel,
        grid_spec=grid_spec,
        out_shape=(
            jax.ShapeDtypeStruct((rows, PAIR), jnp.bfloat16),
            jax.ShapeDtypeStruct((rows, PAIR), jnp.float32),
        ),
        compiler_params=pltpu.CompilerParams(vmem_limit_bytes=40 << 20),
        cost_estimate=pl.CostEstimate(
            flops=4 * BLK * PER * BLOCK**3, bytes_accessed=8 << 20, transcendentals=BLK * PER * BLOCK**2
        ),
        name="attend",
    )(slots, count, query, table)


def backward_kernel(
    slots_ref, count_ref, qg_ref, att_ref, stat_ref, table_ref, dq_ref, grads_ref, acc_ref
):
    b = pl.program_id(0)

    @pl.when(b == 0)
    def _():
        acc_ref[...] = jnp.zeros_like(acc_ref)

    count = count_ref[b]
    both = qg_ref[...]
    lane = lax.broadcasted_iota(jnp.int32, both.shape, 1)
    zero = jnp.zeros_like(both)
    stacked = jnp.concatenate(
        [jnp.where(lane < HD, both, zero), jnp.where(lane < HD, zero, both)], axis=0
    )
    dots = jnp.sum(
        jnp.where(lane < HD, 0.0, both.astype(jnp.float32) * att_ref[...].astype(jnp.float32)),
        axis=1,
        keepdims=True,
    )
    highest = stat_ref[:, 0:1]
    inverse = stat_ref[:, HD : HD + 1]
    dq = jnp.zeros((BLOCK, PAIR), jnp.float32)
    for j in range(0, PER, 2):
        slots = [slots_ref[b * PER + j + i] for i in range(2)]
        chosen = jnp.concatenate([table_ref[s] for s in slots], axis=0)
        products = dot(stacked, chosen, NT)
        key = lax.broadcasted_iota(jnp.int32, (BLOCK, 2 * BLOCK), 1) + j * BLOCK
        scores = jnp.where(key < count * BLOCK, products[:BLOCK], -1e30)
        attention = jnp.exp(scores - highest) * inverse
        score_grad = (attention * (products[BLOCK:] - dots)).astype(jnp.bfloat16)
        dq = dq + dot(score_grad, chosen)
        pair = jnp.concatenate([score_grad, attention.astype(jnp.bfloat16)], axis=0)
        grads = dot(pair, stacked, TN)
        for i in range(2):
            acc_ref[slots[i]] += grads[i * BLOCK : (i + 1) * BLOCK]
    dq = (dq * SCALE).astype(jnp.bfloat16)
    dq_ref[0] = jnp.concatenate([dq[:HD, :HD], dq[HD:, :HD]], axis=1)

    @pl.when(b == pl.num_programs(0) - 1)
    def _():
        grads_ref[...] = acc_ref[...].astype(jnp.bfloat16)


def backward(slots, count, query_grad, attended, stat, table):
    whole = lambda shape: pl.BlockSpec(shape, lambda b, *_: (0,) * len(shape))
    rowwise = pl.BlockSpec((BLOCK, PAIR), lambda b, *_: (b, 0))
    grid_spec = pltpu.PrefetchScalarGridSpec(
        num_scalar_prefetch=2,
        grid=(BLK,),
        in_specs=[rowwise, rowwise, rowwise, whole(table.shape)],
        out_specs=[pl.BlockSpec((1, HD, PAIR), lambda b, *_: (b, 0, 0)), whole(table.shape)],
        scratch_shapes=[pltpu.VMEM(table.shape, jnp.float32)],
    )
    return pl.pallas_call(
        backward_kernel,
        grid_spec=grid_spec,
        out_shape=(
            jax.ShapeDtypeStruct((BLK, HD, PAIR), jnp.bfloat16),
            jax.ShapeDtypeStruct(table.shape, jnp.bfloat16),
        ),
        compiler_params=pltpu.CompilerParams(vmem_limit_bytes=56 << 20),
        cost_estimate=pl.CostEstimate(
            flops=10 * BLK * PER * BLOCK**3, bytes_accessed=16 << 20, transcendentals=BLK * PER * BLOCK**2
        ),
        name="attend_back",
    )(slots, count, query_grad, attended, stat, table)


def torus(node_count):
    rows = 4 if node_count >= 64 else 2
    return node_count // (2 * rows), rows * 2


def weights_kernel(
    planes, group, in_ref, out_ref, sum_ref,
    mine, x_in, x_sum, z_in, z_sum, g_in, piece,
    x_send, x_recv, z_send, z_recv, g_send, g_recv, p_send, p_recv, f_send, f_recv,
):
    node, head = lax.axis_index("node"), lax.axis_index("head")
    z, g = node // group, node % group
    rows = sum_ref.shape[2]
    x_peers = [(node, (head + d) % HEADS) for d in range(1, HEADS)]
    z_peers = [(((z + d) % planes) * group + g, head) for d in range(1, planes)]
    g_peers = [(z * group + (g + d) % group, head) for d in range(1, group)]
    barrier = pltpu.get_barrier_semaphore()
    for peer in x_peers + z_peers + g_peers:
        pl.semaphore_signal(barrier, inc=1, device_id=peer, device_id_type=MESH)

    for h in range(HEADS):
        chunk = jnp.concatenate(
            [in_ref[h * 3 * HD : (h + 1) * 3 * HD], out_ref[h * HD : (h + 1) * HD]], axis=0
        )
        chunk = jnp.concatenate([chunk[:, :128], chunk[:, 128:]], axis=0)
        mine[h] = chunk.reshape(planes, group, rows, 128)
    pl.semaphore_wait(barrier, len(x_peers + z_peers + g_peers))

    copies = [
        pltpu.make_async_remote_copy(
            mine.at[peer[1]], x_in.at[d], x_send.at[d], x_recv.at[d], device_id=peer, device_id_type=MESH
        )
        for d, peer in enumerate(x_peers)
    ]
    for copy in copies:
        copy.start()
    for copy in copies:
        copy.wait()
    x_sum[...] = mine[head] + x_in[0] + x_in[1] + x_in[2]

    copies = [
        pltpu.make_async_remote_copy(
            x_sum.at[(z + d + 1) % planes], z_in.at[d], z_send.at[d], z_recv.at[d],
            device_id=peer, device_id_type=MESH,
        )
        for d, peer in enumerate(z_peers)
    ]
    for copy in copies:
        copy.start()
    for copy in copies:
        copy.wait()
    total = x_sum[z]
    for d in range(planes - 1):
        total = total + z_in[d]
    z_sum[...] = total

    copies = [
        pltpu.make_async_remote_copy(
            z_sum.at[(g + d + 1) % group], g_in.at[d], g_send.at[d], g_recv.at[d],
            device_id=peer, device_id_type=MESH,
        )
        for d, peer in enumerate(g_peers)
    ]
    for copy in copies:
        copy.start()
    for copy in copies:
        copy.wait()
    total = z_sum[g]
    for d in range(group - 1):
        total = total + g_in[d]
    piece[...] = total

    copies = [
        pltpu.make_async_remote_copy(
            piece, sum_ref.at[z, g], p_send.at[d], p_recv.at[d], device_id=peer, device_id_type=MESH
        )
        for d, peer in enumerate(g_peers)
    ]
    for copy in copies:
        copy.start()
    sum_ref[z, g] = total
    for copy in copies:
        copy.wait()

    copies = [
        pltpu.make_async_remote_copy(
            sum_ref.at[z], sum_ref.at[z], f_send.at[d], f_recv.at[d], device_id=peer, device_id_type=MESH
        )
        for d, peer in enumerate(z_peers)
    ]
    for copy in copies:
        copy.start()
    for copy in copies:
        copy.wait()


def sum_weights(in_grad, out_grad, node_count):
    planes, group = torus(node_count)
    rows = 4 * HD * 2 // (planes * group)
    full = (planes, group, rows, 128)
    dma = lambda n: pltpu.SemaphoreType.DMA((n,))
    vmem = pl.BlockSpec(memory_space=pltpu.VMEM)
    total = pl.pallas_call(
        functools.partial(weights_kernel, planes, group),
        out_shape=jax.ShapeDtypeStruct(full, jnp.float32),
        in_specs=[vmem, vmem],
        out_specs=vmem,
        scratch_shapes=[
            pltpu.VMEM((HEADS,) + full, jnp.float32),
            pltpu.VMEM((HEADS - 1,) + full, jnp.float32),
            pltpu.VMEM(full, jnp.float32),
            pltpu.VMEM((planes - 1,) + full[1:], jnp.float32),
            pltpu.VMEM(full[1:], jnp.float32),
            pltpu.VMEM((group - 1,) + full[2:], jnp.float32),
            pltpu.VMEM(full[2:], jnp.float32),
            dma(HEADS - 1), dma(HEADS - 1),
            dma(planes - 1), dma(planes - 1),
            dma(group - 1), dma(group - 1),
            dma(group - 1), dma(group - 1),
            dma(planes - 1), dma(planes - 1),
        ],
        compiler_params=pltpu.CompilerParams(
            collective_id=1, has_side_effects=True, vmem_limit_bytes=32 << 20
        ),
        name="sum_weights",
    )(in_grad, out_grad)
    total = total.reshape(2, 4 * HD, 128).transpose(1, 0, 2).reshape(4 * HD, 2 * 128)
    return total[: 3 * HD].T, total[3 * HD :]


def ring_order(planes):
    half = planes // 2
    return [0] + [s * k for k in range(1, half) for s in (-1, 1)] + [half]


def fetch_kernel(
    planes, group, own_ref, asked_ref, pairs_ref, mine_ref, query_ref, table_ref, rows_ref, asks_ref,
    whole, ring, chunk, picked, made, asks,
    a_send, a_recv, b_send, b_recv, q_send, q_recv, r_send, r_recv, g_send, g_recv, x_send, x_recv, asks_sem,
):
    node, head = lax.axis_index("node"), lax.axis_index("head")
    z, g = node // group, node % group
    half = planes // 2
    part = BLOCK // HEADS
    x_peers = [(node, (head + d) % HEADS) for d in range(1, HEADS)]
    g_peers = [(z * group + (g + d) % group, head) for d in range(1, group)]
    right = (((z + 1) % planes) * group + g, head)
    left = (((z + planes - 1) % planes) * group + g, head)

    def remote(source, target, send, recv, peer):
        return pltpu.make_async_remote_copy(
            source, target, send, recv, device_id=peer, device_id_type=MESH
        )

    def quarter(h):
        return pl.ds(pl.multiple_of(h * part, part), part)

    barrier = pltpu.get_barrier_semaphore()
    for peer in x_peers + g_peers + [left, right]:
        pl.semaphore_signal(barrier, inc=1, device_id=peer, device_id_type=MESH)
    pl.semaphore_wait(barrier, len(x_peers + g_peers) + 2)

    own_blocks = pl.ds(head * HEADS, HEADS)
    first, rest = [], []
    for d, peer in enumerate(x_peers):
        rows = quarter(peer[1])
        first.append(
            remote(own_ref.at[:, rows], whole.at[own_blocks, rows], a_send.at[d], a_recv.at[d], peer)
        )
    for e in range(1, HEADS):
        for d, peer in enumerate(x_peers):
            rows = quarter((peer[1] + e) % HEADS)
            rest.append(
                remote(
                    own_ref.at[:, rows], whole.at[own_blocks, rows],
                    b_send.at[d, e - 1], b_recv.at[d, e - 1], peer,
                )
            )
    questions = [
        remote(asked_ref.at[peer[0] % group], asks_ref.at[g], q_send.at[d], q_recv.at[d], peer)
        for d, peer in enumerate(g_peers)
    ]
    for copy in first + questions + rest:
        copy.start()
    whole[own_blocks] = own_ref[...]
    asks_ref[g] = asked_ref[g]
    for copy in first:
        copy.wait_recv()
    ring[z] = whole[:, quarter(head)]

    def hop(way, k):
        at = (z - k + planes) % planes if way == 0 else (z + k) % planes
        view = ring.at[at]
        if k == half - 1:
            view = view.at[pl.ds(0, BLK // 2)] if way == 0 else view.at[pl.ds(BLK // 2, BLK // 2)]
        return remote(
            view, view, r_send.at[way, k], r_recv.at[way, k], right if way == 0 else left
        )

    hops = {(way, k): hop(way, k) for way in range(2) for k in range(half)}
    for way in range(2):
        hops[way, 0].start()
    for copy in questions:
        copy.wait_recv()
    answer = pltpu.make_async_copy(asks_ref, asks, asks_sem)
    answer.start()
    answer.wait()

    order = ring_order(planes)
    sent = []

    def bring(t):
        offset = order[t]
        at = (z + offset + planes) % planes
        if offset == half:
            hops[0, half - 1].wait_recv()
            hops[1, half - 1].wait_recv()
        elif offset:
            way, k = (0, -offset) if offset < 0 else (1, offset)
            hops[way, k - 1].wait_recv()
            hops[way, k].start()
        chunk[...] = ring[at]
        for d in range(group - 1, -1, -1):
            peer = (g + d) % group
            for c in range(CAP):
                block = chunk[asks[peer, 0, at * CAP + c]]
                if d:
                    picked[at, d - 1, c] = block
                else:
                    rows_ref[at, g, c] = block
            if d:
                copy = remote(
                    picked.at[at, d - 1], rows_ref.at[at, g], g_send.at[at, d - 1], g_recv.at[at, d - 1],
                    g_peers[d - 1],
                )
                copy.start()
                sent.append(copy)

    arriving = []

    def make(t):
        at = (z + order[t] + planes) % planes
        for d in range(1, group):
            remote(
                picked.at[at, d - 1], rows_ref.at[at, g], g_send.at[at, d - 1], g_recv.at[at, d - 1],
                g_peers[d - 1],
            ).wait_recv()
        rows = rows_ref[at].reshape(group * CAP * part, 2 * BLOCK)
        pairs = dot(rows, pairs_ref[...]).astype(jnp.bfloat16)
        for h in range(HEADS):
            made[at, h] = pairs[:, h * PAIR : (h + 1) * PAIR].reshape(group * CAP, part, PAIR)
        slots = pl.ds(BLK + at * group * CAP, group * CAP)
        for d, peer in enumerate(x_peers):
            copy = remote(
                made.at[at, peer[1]], table_ref.at[slots, quarter(head)], x_send.at[at, d], x_recv.at[at, d],
                peer,
            )
            copy.start()
            sent.append(copy)
            arriving.append(copy)
        table_ref[slots, quarter(head)] = made[at, head]

    bring(0)
    for copy in rest:
        copy.wait_recv()

    @pl.loop(0, BLK)
    def _(b):
        both = dot(whole[b], mine_ref[...])
        query_ref[b] = (both[:, :PAIR] * SCALE).astype(jnp.bfloat16)
        table_ref[b] = both[:, PAIR:].astype(jnp.bfloat16)

    for t in range(1, planes):
        bring(t)
        make(t - 1)
    make(planes - 1)
    for copy in arriving:
        copy.wait_recv()
    for copy in first + rest + questions + list(hops.values()) + sent:
        copy.wait_send()


def fetch(features, in_weight, wanted, node_count):
    planes, group = torus(node_count)
    part = BLOCK // HEADS
    head = lax.axis_index("head")
    own = features.reshape(HEADS, BLOCK, 2 * BLOCK)
    asked = wanted.reshape(planes, group, CAP).transpose(1, 0, 2).reshape(group, 1, planes * CAP)
    asked = jnp.pad(asked, ((0, 0), (0, 7), (0, 128 - planes * CAP)))
    columns = in_weight.reshape(2 * BLOCK, HEADS, 3 * HD)
    pairs = columns[:, :, HD:].reshape(2 * BLOCK, HEADS * PAIR)
    mine = lax.dynamic_index_in_dim(columns, head, axis=1, keepdims=False)
    mine = jnp.concatenate([mine[:, :HD], jnp.zeros_like(mine[:, :HD]), mine[:, HD:]], axis=1)
    dma = lambda *shape: pltpu.SemaphoreType.DMA(shape)
    vmem = pl.BlockSpec(memory_space=pltpu.VMEM)
    slots = BLK + planes * group * CAP
    return pl.pallas_call(
        functools.partial(fetch_kernel, planes, group),
        out_shape=(
            jax.ShapeDtypeStruct((BLK, BLOCK, PAIR), jnp.bfloat16),
            jax.ShapeDtypeStruct((slots, BLOCK, PAIR), jnp.bfloat16),
            jax.ShapeDtypeStruct((planes, group, CAP, part, 2 * BLOCK), jnp.bfloat16),
            jax.ShapeDtypeStruct((group, 8, 128), jnp.int32),
        ),
        in_specs=[vmem] * 4,
        out_specs=(vmem,) * 4,
        scratch_shapes=[
            pltpu.VMEM((BLK, BLOCK, 2 * BLOCK), jnp.bfloat16),
            pltpu.VMEM((planes, BLK, part, 2 * BLOCK), jnp.bfloat16),
            pltpu.VMEM((BLK, part, 2 * BLOCK), jnp.bfloat16),
            pltpu.VMEM((planes, group - 1, CAP, part, 2 * BLOCK), jnp.bfloat16),
            pltpu.VMEM((planes, HEADS, group * CAP, part, PAIR), jnp.bfloat16),
            pltpu.SMEM((group, 8, 128), jnp.int32),
            dma(3), dma(3), dma(3, 3), dma(3, 3), dma(group - 1), dma(group - 1),
            dma(2, planes // 2), dma(2, planes // 2),
            dma(planes, group - 1), dma(planes, group - 1), dma(planes, 3), dma(planes, 3),
            pltpu.SemaphoreType.DMA,
        ],
        compiler_params=pltpu.CompilerParams(
            collective_id=2, has_side_effects=True, vmem_limit_bytes=48 << 20
        ),
        name="fetch",
    )(own, asked, pairs, mine)


def return_kernel(
    planes, group, grads_ref, dq_ref, rows_ref, features_ref, norm_ref, pair_ref, single_ref, asks_ref,
    feature_ref, weight_ref,
    own_pairs, own_queries, heads, leaving, answers, partial, ring, summed, quarters, acc,
    o_send, o_recv, q_send, q_recv, x_send, x_recv, g_send, g_recv, r_send, r_recv, f_send, f_recv,
):
    node, head = lax.axis_index("node"), lax.axis_index("head")
    z, g = node // group, node % group
    half = planes // 2
    part = BLOCK // HEADS
    width = group * CAP
    x_peers = [(node, (head + d) % HEADS) for d in range(1, HEADS)]
    g_peers = [(z * group + (g + d) % group, head) for d in range(1, group)]
    right = (((z + 1) % planes) * group + g, head)
    left = (((z + planes - 1) % planes) * group + g, head)

    def remote(source, target, send, recv, peer):
        return pltpu.make_async_remote_copy(
            source, target, send, recv, device_id=peer, device_id_type=MESH
        )

    def quarter(h):
        return pl.ds(pl.multiple_of(h * part, part), part)

    barrier = pltpu.get_barrier_semaphore()
    for peer in x_peers + g_peers + [left, right]:
        pl.semaphore_signal(barrier, inc=1, device_id=peer, device_id_type=MESH)
    pl.semaphore_wait(barrier, len(x_peers + g_peers) + 2)

    order = list(reversed(ring_order(planes)))
    planes_in_order = [(z + offset + planes) % planes for offset in order]
    sent = []
    far = [
        [
            remote(
                grads_ref.at[pl.ds(BLK + at * width, width), quarter(peer[1])], heads.at[at, head],
                x_send.at[at, d], x_recv.at[at, d], peer,
            )
            for d, peer in enumerate(x_peers)
        ]
        for at in planes_in_order
    ]
    own = []
    for d, peer in enumerate(x_peers):
        blocks = pl.ds(peer[1] * HEADS, HEADS)
        own.append(remote(grads_ref.at[blocks], own_pairs.at[head], o_send.at[d], o_recv.at[d], peer))
        own.append(remote(dq_ref.at[blocks], own_queries.at[head], q_send.at[d], q_recv.at[d], peer))

    def begin(copies):
        for copy in copies:
            copy.start()
            sent.append(copy)

    for t in range(min(3, planes)):
        begin(far[t])
    acc[...] = jnp.zeros_like(acc)
    own_blocks = pl.ds(head * HEADS, HEADS)
    own_pairs[head] = grads_ref[own_blocks]
    own_queries[head] = dq_ref[own_blocks]

    def spread(t):
        at = planes_in_order[t]
        heads[at, head] = grads_ref[pl.ds(BLK + at * width, width), quarter(head)]
        for copy in far[t]:
            copy.wait_recv()
        if t + 3 < planes:
            begin(far[t + 3])
        if t == max(planes - 4, 0):
            begin(own)
        pairs = jnp.concatenate(
            [heads[at, h].reshape(width * part, PAIR) for h in range(HEADS)], axis=1
        )
        back = dot(pairs, pair_ref[...]).astype(jnp.bfloat16)
        leaving[at] = back.reshape(group, CAP, part, 2 * BLOCK)
        copies = [
            remote(
                leaving.at[at, peer[0] % group], answers.at[at, g], g_send.at[at, d], g_recv.at[at, d], peer
            )
            for d, peer in enumerate(g_peers)
        ]
        begin(copies)
        answers[at, g] = leaving[at, g]
        acc[...] += dot(pairs, rows_ref[at].reshape(width * part, 2 * BLOCK), TN)
        return copies

    def hop(way, step, at):
        source, target = partial.at[at], ring.at[way, step]
        if step == 0:
            blocks = pl.ds(way * (BLK // 2), BLK // 2)
            source, target = source.at[blocks], target.at[blocks]
        return remote(
            source, target, r_send.at[way, step], r_recv.at[way, step], left if way else right
        )

    def gather(t, copies):
        at, offset = planes_in_order[t], order[t]
        for copy in copies:
            copy.wait_recv()
        side = width * part
        column = lax.broadcasted_iota(jnp.int32, (1, side), 1)
        target = column % part
        for j in range(width):
            block = asks_ref[j // CAP, 0, at * CAP + j % CAP]
            target = target + jnp.where(column // part == j, block * part, 0)
        row = lax.broadcasted_iota(jnp.int32, (BLK * part, side), 0)
        chosen = jnp.where(row == target, 1.0, 0.0).astype(jnp.bfloat16)
        total = dot(chosen, answers[at].reshape(side, 2 * BLOCK)).reshape(BLK, part, 2 * BLOCK)
        if offset == half:
            partial[at] = total.astype(jnp.bfloat16)
            for way in range(2):
                begin([hop(way, 0, at)])
            return
        step = half - 1 - abs(offset)
        ways = [0] if offset > 0 else [1] if offset < 0 else [0, 1]
        for way in ways:
            hop(way, step, at).wait_recv()
            if step == 0:
                mid = BLK // 2
                if way == 0:
                    total = jnp.concatenate(
                        [total[:mid] + ring[way, step, :mid].astype(jnp.float32), total[mid:]], axis=0
                    )
                else:
                    total = jnp.concatenate(
                        [total[:mid], total[mid:] + ring[way, step, mid:].astype(jnp.float32)], axis=0
                    )
            else:
                total = total + ring[way, step].astype(jnp.float32)
        if offset:
            partial[at] = total.astype(jnp.bfloat16)
            begin([hop(ways[0], step + 1, at)])
        else:
            summed[...] = total.astype(jnp.bfloat16)

    waiting = None
    for t in range(planes):
        copies = spread(t)
        if t:
            gather(t - 1, waiting)
        waiting = copies
    gather(planes - 1, waiting)
    final = [
        remote(
            summed.at[pl.ds(peer[1] * HEADS, HEADS)], quarters.at[head], f_send.at[d], f_recv.at[d], peer
        )
        for d, peer in enumerate(x_peers)
    ]
    begin(final)
    quarters[head] = summed[own_blocks]

    for copy in own:
        copy.wait_recv()
    rows = HEADS * BLOCK
    pairs = jnp.concatenate([own_pairs[h].reshape(rows, PAIR) for h in range(HEADS)], axis=1)
    queries = jnp.concatenate(
        [
            jnp.concatenate(
                [own_queries[h, :, :, :HD], own_queries[h, :, :, HD:]], axis=1
            ).reshape(rows, HD)
            for h in range(HEADS)
        ],
        axis=1,
    )
    features = features_ref[...]
    pair_weight = acc[...] + dot(pairs, features, TN)
    single_weight = dot(queries, features, TN)
    for h in range(HEADS):
        weight_ref[h, :HD] = single_weight[h * HD : (h + 1) * HD]
        weight_ref[h, HD:] = pair_weight[h * PAIR : (h + 1) * PAIR]
    base = norm_ref[...] + dot(pairs, pair_ref[...]) + dot(queries, single_ref[...])
    base = base.reshape(HEADS, HEADS, part, 2 * BLOCK)
    for copy in final:
        copy.wait_recv()
    for h in range(HEADS):
        feature_ref[:, h] = (base[:, h] + quarters[h].astype(jnp.float32)).astype(jnp.bfloat16)
    for copy in sent:
        copy.wait_send()


def give_back(grads, dq, rows, features, norm_grad, in_weight, asks, node_count):
    planes, group = torus(node_count)
    part = BLOCK // HEADS
    wide = 2 * BLOCK
    columns = in_weight.T.reshape(HEADS, 3 * HD, wide)
    pair = columns[:, HD:].reshape(HEADS * PAIR, wide)
    single = columns[:, :HD].reshape(HEADS * HD, wide)
    dma = lambda *shape: pltpu.SemaphoreType.DMA(shape)
    vmem = pl.BlockSpec(memory_space=pltpu.VMEM)
    low = lambda *shape: pltpu.VMEM(shape, jnp.bfloat16)
    feature_grad, weight = pl.pallas_call(
        functools.partial(return_kernel, planes, group),
        out_shape=(
            jax.ShapeDtypeStruct((HEADS, HEADS, part, wide), jnp.bfloat16),
            jax.ShapeDtypeStruct((HEADS, 3 * HD, wide), jnp.float32),
        ),
        in_specs=[vmem] * 7 + [pl.BlockSpec(memory_space=pltpu.SMEM)],
        out_specs=(vmem,) * 2,
        scratch_shapes=[
            low(HEADS, HEADS, BLOCK, PAIR),
            low(HEADS, HEADS, HD, PAIR),
            low(planes, HEADS, group * CAP, part, PAIR),
            low(planes, group, CAP, part, wide),
            low(planes, group, CAP, part, wide),
            low(planes, BLK, part, wide),
            low(2, planes // 2, BLK, part, wide),
            low(BLK, part, wide),
            low(HEADS, HEADS, part, wide),
            pltpu.VMEM((HEADS * PAIR, wide), jnp.float32),
            dma(3), dma(3), dma(3), dma(3), dma(planes, 3), dma(planes, 3),
            dma(planes, group - 1), dma(planes, group - 1),
            dma(2, planes // 2), dma(2, planes // 2), dma(3), dma(3),
        ],
        compiler_params=pltpu.CompilerParams(
            collective_id=3, has_side_effects=True, vmem_limit_bytes=56 << 20
        ),
        name="give_back",
    )(grads, dq, rows, features, norm_grad, pair, single, asks)
    return feature_grad.reshape(HEADS * BLOCK, wide), weight.reshape(HEADS * 3 * HD, wide)


def on_device(features, in_weight, out_weight, cotangent, key_slots, block_count, wanted):
    node_count = lax.axis_size("node")
    node_rows = BLK * BLOCK
    total_nodes = node_rows * node_count
    queries, table, rows, asks = fetch(features, in_weight, wanted, node_count)
    queries = queries.reshape(node_rows, PAIR)
    slots = key_slots.reshape(-1)
    wide, stat = forward(slots, block_count, queries, table)
    attended = wide[:, HD:]
    attended_rows = lax.all_to_all(attended, "head", split_axis=0, concat_axis=1, tiled=True)
    summed = features.astype(jnp.float32) + jnp.dot(
        attended_rows, out_weight, preferred_element_type=jnp.float32
    )
    root_mean = jnp.sqrt(jnp.mean(summed * summed, axis=-1, keepdims=True) + 1e-06)
    normed = summed / root_mean
    output = normed.astype(jnp.bfloat16)
    upstream = cotangent.astype(jnp.float32)
    norm_grad = (
        upstream - normed * jnp.mean(upstream * normed, axis=-1, keepdims=True)
    ) / root_mean
    norm_grad_low = norm_grad.astype(jnp.bfloat16)
    out_weight_grad = jnp.dot(attended_rows.T, norm_grad_low, preferred_element_type=jnp.float32)
    attended_grad = jnp.dot(norm_grad_low, out_weight.T, preferred_element_type=jnp.float32).astype(
        jnp.bfloat16
    )
    attended_grad = lax.all_to_all(attended_grad, "head", split_axis=1, concat_axis=0, tiled=True)
    both = jnp.concatenate([queries[:, :HD], attended_grad], axis=1)
    dq, grads = backward(slots, block_count, both, wide, stat, table)
    feature_grad, in_weight_grad = give_back(
        grads, dq, rows, features, norm_grad, in_weight, asks, node_count
    )
    in_weight_grad, out_weight_grad = sum_weights(in_weight_grad, out_weight_grad, node_count)
    grad_factor = total_nodes ** (-0.5)
    return (
        output,
        feature_grad,
        in_weight_grad * grad_factor,
        out_weight_grad * grad_factor,
    )


def solution(mesh):
    placed = (
        P(("node", "head"), None),
        P(),
        P(),
        P(("node", "head"), None),
        P("node", None),
        P("node"),
        P("node", None, None),
    )
    return jax.shard_map(
        on_device,
        mesh=mesh,
        in_specs=placed,
        out_specs=(
            P(("node", "head"), None),
            P(("node", "head"), None),
            P(None, "head"),
            P("head", None),
        ),
        check_vma=False,
    )
```

```python
import functools

import jax
import jax.numpy as jnp
from jax import lax
from jax.experimental import pallas as pl
from jax.experimental.pallas import tpu as pltpu
from jax.sharding import PartitionSpec as P

HEADS = 4
HD = 64
BLOCK = 128
BLK = 16
PER = 12
CAP = 2
PAIR = 2 * HD
SCALE = HD ** (-0.5)
NT = (((1,), (1,)), ((), ()))
TN = (((0,), (0,)), ((), ()))
MESH = pl.DeviceIdType.MESH


def dot(a, b, dims=(((1,), (0,)), ((), ()))):
    return lax.dot_general(a, b, dims, preferred_element_type=jnp.float32)


def forward_kernel(slots_ref, count_ref, q_ref, table_ref, out_ref, stat_ref):
    b = pl.program_id(0)
    count = count_ref[b]
    query = q_ref[...]
    chosen = [table_ref[slots_ref[b * PER + j]] for j in range(PER)]
    scores = []
    for j in range(0, PER, 2):
        pair = dot(query, jnp.concatenate(chosen[j : j + 2], axis=0), NT)
        for i in range(2):
            dead = jnp.where(j + i < count, 0.0, -1e30)
            scores.append(pair[:, i * BLOCK : (i + 1) * BLOCK] + dead)
    highest = scores[0]
    for part in scores[1:]:
        highest = jnp.maximum(highest, part)
    highest = jnp.max(highest, axis=1, keepdims=True)
    total = jnp.zeros((BLOCK, BLOCK), jnp.float32)
    result = jnp.zeros((BLOCK, PAIR), jnp.float32)
    for j in range(0, PER, 2):
        raised = [jnp.exp(part - highest) for part in scores[j : j + 2]]
        total = total + raised[0] + raised[1]
        result = result + dot(
            jnp.concatenate([x.astype(jnp.bfloat16) for x in raised], axis=1),
            jnp.concatenate(chosen[j : j + 2], axis=0),
        )
    total = jnp.sum(total, axis=1, keepdims=True)
    out_ref[...] = (result / total).astype(jnp.bfloat16)
    lane = lax.broadcasted_iota(jnp.int32, stat_ref.shape, 1)
    stat_ref[...] = jnp.where(lane < HD, highest, 1.0 / total)


def forward(slots, count, query, table):
    rows = BLK * BLOCK
    grid_spec = pltpu.PrefetchScalarGridSpec(
        num_scalar_prefetch=2,
        grid=(BLK,),
        in_specs=[
            pl.BlockSpec((BLOCK, PAIR), lambda b, *_: (b, 0)),
            pl.BlockSpec(table.shape, lambda b, *_: (0, 0, 0)),
        ],
        out_specs=[
            pl.BlockSpec((BLOCK, PAIR), lambda b, *_: (b, 0)),
            pl.BlockSpec((BLOCK, PAIR), lambda b, *_: (b, 0)),
        ],
    )
    return pl.pallas_call(
        forward_kernel,
        grid_spec=grid_spec,
        out_shape=(
            jax.ShapeDtypeStruct((rows, PAIR), jnp.bfloat16),
            jax.ShapeDtypeStruct((rows, PAIR), jnp.float32),
        ),
        compiler_params=pltpu.CompilerParams(vmem_limit_bytes=40 << 20),
        cost_estimate=pl.CostEstimate(
            flops=4 * BLK * PER * BLOCK**3, bytes_accessed=8 << 20, transcendentals=BLK * PER * BLOCK**2
        ),
        name="attend",
    )(slots, count, query, table)


def backward_kernel(
    slots_ref, count_ref, qg_ref, att_ref, stat_ref, table_ref, dq_ref, grads_ref, acc_ref
):
    b = pl.program_id(0)

    @pl.when(b == 0)
    def _():
        acc_ref[...] = jnp.zeros_like(acc_ref)

    count = count_ref[b]
    both = qg_ref[...]
    lane = lax.broadcasted_iota(jnp.int32, both.shape, 1)
    zero = jnp.zeros_like(both)
    stacked = jnp.concatenate(
        [jnp.where(lane < HD, both, zero), jnp.where(lane < HD, zero, both)], axis=0
    )
    dots = jnp.sum(
        jnp.where(lane < HD, 0.0, both.astype(jnp.float32) * att_ref[...].astype(jnp.float32)),
        axis=1,
        keepdims=True,
    )
    flipped = jnp.where((lane >= 32) & (lane < HD), dots, stat_ref[...]).T
    highest, dots, inverse = flipped[0:1], flipped[32:33], flipped[HD : HD + 1]
    dq = jnp.zeros((PAIR, BLOCK), jnp.float32)
    for j in range(0, PER, 2):
        slots = [slots_ref[b * PER + j + i] for i in range(2)]
        chosen = jnp.concatenate([table_ref[s] for s in slots], axis=0)
        products = dot(chosen, stacked, NT)
        terms = []
        for i in range(2):
            rows = slice(i * BLOCK, (i + 1) * BLOCK)
            top = highest + jnp.where(j + i < count, 0.0, 1e30)
            attention = jnp.exp(products[rows, :BLOCK] - top) * inverse
            terms.append((attention * (products[rows, BLOCK:] - dots), attention))
        score_grad, attention = [
            jnp.concatenate([x.astype(jnp.bfloat16) for x in pair], axis=0) for pair in zip(*terms)
        ]
        dq = dq + dot(chosen, score_grad, TN)
        grads = dot(jnp.concatenate([score_grad, attention], axis=1), stacked)
        for i in range(2):
            acc_ref[slots[i]] += grads[i * BLOCK : (i + 1) * BLOCK]
    dq = (dq.T * SCALE).astype(jnp.bfloat16)
    dq_ref[0] = jnp.concatenate([dq[:HD, :HD], dq[HD:, :HD]], axis=1)

    @pl.when(b == pl.num_programs(0) - 1)
    def _():
        grads_ref[...] = acc_ref[...].astype(jnp.bfloat16)


def backward(slots, count, query_grad, attended, stat, table):
    whole = lambda shape: pl.BlockSpec(shape, lambda b, *_: (0,) * len(shape))
    rowwise = pl.BlockSpec((BLOCK, PAIR), lambda b, *_: (b, 0))
    grid_spec = pltpu.PrefetchScalarGridSpec(
        num_scalar_prefetch=2,
        grid=(BLK,),
        in_specs=[rowwise, rowwise, rowwise, whole(table.shape)],
        out_specs=[pl.BlockSpec((1, HD, PAIR), lambda b, *_: (b, 0, 0)), whole(table.shape)],
        scratch_shapes=[pltpu.VMEM(table.shape, jnp.float32)],
    )
    return pl.pallas_call(
        backward_kernel,
        grid_spec=grid_spec,
        out_shape=(
            jax.ShapeDtypeStruct((BLK, HD, PAIR), jnp.bfloat16),
            jax.ShapeDtypeStruct(table.shape, jnp.bfloat16),
        ),
        compiler_params=pltpu.CompilerParams(vmem_limit_bytes=56 << 20),
        cost_estimate=pl.CostEstimate(
            flops=10 * BLK * PER * BLOCK**3, bytes_accessed=16 << 20, transcendentals=BLK * PER * BLOCK**2
        ),
        name="attend_back",
    )(slots, count, query_grad, attended, stat, table)


def torus(node_count):
    rows = 4 if node_count >= 64 else 2
    return node_count // (2 * rows), rows * 2


def weights_kernel(
    planes, group, in_ref, out_ref, sum_ref,
    mine, x_in, x_sum, z_in, z_sum, g_in, piece,
    x_send, x_recv, z_send, z_recv, g_send, g_recv, p_send, p_recv, f_send, f_recv,
):
    node, head = lax.axis_index("node"), lax.axis_index("head")
    z, g = node // group, node % group
    rows = sum_ref.shape[2]
    x_peers = [(node, (head + d) % HEADS) for d in range(1, HEADS)]
    z_peers = [(((z + d) % planes) * group + g, head) for d in range(1, planes)]
    g_peers = [(z * group + (g + d) % group, head) for d in range(1, group)]
    barrier = pltpu.get_barrier_semaphore()
    for peer in x_peers + z_peers + g_peers:
        pl.semaphore_signal(barrier, inc=1, device_id=peer, device_id_type=MESH)

    for h in range(HEADS):
        chunk = jnp.concatenate(
            [in_ref[h * 3 * HD : (h + 1) * 3 * HD], out_ref[h * HD : (h + 1) * HD]], axis=0
        )
        chunk = jnp.concatenate([chunk[:, :128], chunk[:, 128:]], axis=0)
        mine[h] = chunk.reshape(planes, group, rows, 128)
    pl.semaphore_wait(barrier, len(x_peers + z_peers + g_peers))

    copies = [
        pltpu.make_async_remote_copy(
            mine.at[peer[1]], x_in.at[d], x_send.at[d], x_recv.at[d], device_id=peer, device_id_type=MESH
        )
        for d, peer in enumerate(x_peers)
    ]
    for copy in copies:
        copy.start()
    for copy in copies:
        copy.wait()
    x_sum[...] = mine[head] + x_in[0] + x_in[1] + x_in[2]

    copies = [
        pltpu.make_async_remote_copy(
            x_sum.at[(z + d + 1) % planes], z_in.at[d], z_send.at[d], z_recv.at[d],
            device_id=peer, device_id_type=MESH,
        )
        for d, peer in enumerate(z_peers)
    ]
    for copy in copies:
        copy.start()
    for copy in copies:
        copy.wait()
    total = x_sum[z]
    for d in range(planes - 1):
        total = total + z_in[d]
    z_sum[...] = total

    copies = [
        pltpu.make_async_remote_copy(
            z_sum.at[(g + d + 1) % group], g_in.at[d], g_send.at[d], g_recv.at[d],
            device_id=peer, device_id_type=MESH,
        )
        for d, peer in enumerate(g_peers)
    ]
    for copy in copies:
        copy.start()
    for copy in copies:
        copy.wait()
    total = z_sum[g]
    for d in range(group - 1):
        total = total + g_in[d]
    piece[...] = total

    copies = [
        pltpu.make_async_remote_copy(
            piece, sum_ref.at[z, g], p_send.at[d], p_recv.at[d], device_id=peer, device_id_type=MESH
        )
        for d, peer in enumerate(g_peers)
    ]
    for copy in copies:
        copy.start()
    sum_ref[z, g] = total
    for copy in copies:
        copy.wait()

    copies = [
        pltpu.make_async_remote_copy(
            sum_ref.at[z], sum_ref.at[z], f_send.at[d], f_recv.at[d], device_id=peer, device_id_type=MESH
        )
        for d, peer in enumerate(z_peers)
    ]
    for copy in copies:
        copy.start()
    for copy in copies:
        copy.wait()


def sum_weights(in_grad, out_grad, node_count):
    planes, group = torus(node_count)
    rows = 4 * HD * 2 // (planes * group)
    full = (planes, group, rows, 128)
    dma = lambda n: pltpu.SemaphoreType.DMA((n,))
    vmem = pl.BlockSpec(memory_space=pltpu.VMEM)
    total = pl.pallas_call(
        functools.partial(weights_kernel, planes, group),
        out_shape=jax.ShapeDtypeStruct(full, jnp.float32),
        in_specs=[vmem, vmem],
        out_specs=vmem,
        scratch_shapes=[
            pltpu.VMEM((HEADS,) + full, jnp.float32),
            pltpu.VMEM((HEADS - 1,) + full, jnp.float32),
            pltpu.VMEM(full, jnp.float32),
            pltpu.VMEM((planes - 1,) + full[1:], jnp.float32),
            pltpu.VMEM(full[1:], jnp.float32),
            pltpu.VMEM((group - 1,) + full[2:], jnp.float32),
            pltpu.VMEM(full[2:], jnp.float32),
            dma(HEADS - 1), dma(HEADS - 1),
            dma(planes - 1), dma(planes - 1),
            dma(group - 1), dma(group - 1),
            dma(group - 1), dma(group - 1),
            dma(planes - 1), dma(planes - 1),
        ],
        compiler_params=pltpu.CompilerParams(
            collective_id=1, has_side_effects=True, vmem_limit_bytes=32 << 20
        ),
        name="sum_weights",
    )(in_grad, out_grad)
    total = total.reshape(2, 4 * HD, 128).transpose(1, 0, 2).reshape(4 * HD, 2 * 128)
    return total[: 3 * HD].T, total[3 * HD :]


def ring_order(planes):
    half = planes // 2
    return [0] + [s * k for k in range(1, half) for s in (-1, 1)] + [half]


def fetch_kernel(
    planes, group, own_ref, asked_ref, pairs_ref, mine_ref, query_ref, table_ref, rows_ref, asks_ref,
    whole, ring, chunk, picked, made, asks,
    a_send, a_recv, b_send, b_recv, q_send, q_recv, r_send, r_recv, g_send, g_recv, x_send, x_recv, asks_sem,
):
    node, head = lax.axis_index("node"), lax.axis_index("head")
    z, g = node // group, node % group
    half = planes // 2
    part = BLOCK // HEADS
    x_peers = [(node, (head + d) % HEADS) for d in range(1, HEADS)]
    g_peers = [(z * group + (g + d) % group, head) for d in range(1, group)]
    right = (((z + 1) % planes) * group + g, head)
    left = (((z + planes - 1) % planes) * group + g, head)

    def remote(source, target, send, recv, peer):
        return pltpu.make_async_remote_copy(
            source, target, send, recv, device_id=peer, device_id_type=MESH
        )

    def quarter(h):
        return pl.ds(pl.multiple_of(h * part, part), part)

    barrier = pltpu.get_barrier_semaphore()
    for peer in x_peers + g_peers + [left, right]:
        pl.semaphore_signal(barrier, inc=1, device_id=peer, device_id_type=MESH)
    pl.semaphore_wait(barrier, len(x_peers + g_peers) + 2)

    own_blocks = pl.ds(head * HEADS, HEADS)
    first, rest = [], []
    for d, peer in enumerate(x_peers):
        rows = quarter(peer[1])
        first.append(
            remote(own_ref.at[:, rows], whole.at[own_blocks, rows], a_send.at[d], a_recv.at[d], peer)
        )
    for e in range(1, HEADS):
        for d, peer in enumerate(x_peers):
            rows = quarter((peer[1] + e) % HEADS)
            rest.append(
                remote(
                    own_ref.at[:, rows], whole.at[own_blocks, rows],
                    b_send.at[d, e - 1], b_recv.at[d, e - 1], peer,
                )
            )
    questions = [
        remote(asked_ref.at[peer[0] % group], asks_ref.at[g], q_send.at[d], q_recv.at[d], peer)
        for d, peer in enumerate(g_peers)
    ]
    for copy in first + questions + rest:
        copy.start()
    whole[own_blocks] = own_ref[...]
    asks_ref[g] = asked_ref[g]
    for copy in first:
        copy.wait_recv()
    ring[z] = whole[:, quarter(head)]

    def hop(way, k):
        at = (z - k + planes) % planes if way == 0 else (z + k) % planes
        view = ring.at[at]
        if k == half - 1:
            view = view.at[pl.ds(0, BLK // 2)] if way == 0 else view.at[pl.ds(BLK // 2, BLK // 2)]
        return remote(
            view, view, r_send.at[way, k], r_recv.at[way, k], right if way == 0 else left
        )

    hops = {(way, k): hop(way, k) for way in range(2) for k in range(half)}
    for way in range(2):
        hops[way, 0].start()
    for copy in questions:
        copy.wait_recv()
    answer = pltpu.make_async_copy(asks_ref, asks, asks_sem)
    answer.start()
    answer.wait()

    order = ring_order(planes)
    sent = []

    def bring(t):
        offset = order[t]
        at = (z + offset + planes) % planes
        if offset == half:
            hops[0, half - 1].wait_recv()
            hops[1, half - 1].wait_recv()
        elif offset:
            way, k = (0, -offset) if offset < 0 else (1, offset)
            hops[way, k - 1].wait_recv()
            hops[way, k].start()
        chunk[...] = ring[at]
        for d in range(group - 1, -1, -1):
            peer = (g + d) % group
            for c in range(CAP):
                block = chunk[asks[peer, 0, at * CAP + c]]
                if d:
                    picked[at, d - 1, c] = block
                else:
                    rows_ref[at, g, c] = block
            if d:
                copy = remote(
                    picked.at[at, d - 1], rows_ref.at[at, g], g_send.at[at, d - 1], g_recv.at[at, d - 1],
                    g_peers[d - 1],
                )
                copy.start()
                sent.append(copy)

    arriving = []

    def make(t):
        at = (z + order[t] + planes) % planes
        for d in range(1, group):
            remote(
                picked.at[at, d - 1], rows_ref.at[at, g], g_send.at[at, d - 1], g_recv.at[at, d - 1],
                g_peers[d - 1],
            ).wait_recv()
        rows = rows_ref[at].reshape(group * CAP * part, 2 * BLOCK)
        pairs = dot(rows, pairs_ref[...]).astype(jnp.bfloat16)
        for h in range(HEADS):
            made[at, h] = pairs[:, h * PAIR : (h + 1) * PAIR].reshape(group * CAP, part, PAIR)
        slots = pl.ds(BLK + at * group * CAP, group * CAP)
        for d, peer in enumerate(x_peers):
            copy = remote(
                made.at[at, peer[1]], table_ref.at[slots, quarter(head)], x_send.at[at, d], x_recv.at[at, d],
                peer,
            )
            copy.start()
            sent.append(copy)
            arriving.append(copy)
        table_ref[slots, quarter(head)] = made[at, head]

    bring(0)
    for copy in rest:
        copy.wait_recv()

    @pl.loop(0, BLK)
    def _(b):
        both = dot(whole[b], mine_ref[...])
        query_ref[b] = (both[:, :PAIR] * SCALE).astype(jnp.bfloat16)
        table_ref[b] = both[:, PAIR:].astype(jnp.bfloat16)

    for t in range(1, planes):
        bring(t)
        make(t - 1)
    make(planes - 1)
    for copy in arriving:
        copy.wait_recv()
    for copy in first + rest + questions + list(hops.values()) + sent:
        copy.wait_send()


def fetch(features, in_weight, wanted, node_count):
    planes, group = torus(node_count)
    part = BLOCK // HEADS
    head = lax.axis_index("head")
    own = features.reshape(HEADS, BLOCK, 2 * BLOCK)
    asked = wanted.reshape(planes, group, CAP).transpose(1, 0, 2).reshape(group, 1, planes * CAP)
    asked = jnp.pad(asked, ((0, 0), (0, 7), (0, 128 - planes * CAP)))
    columns = in_weight.reshape(2 * BLOCK, HEADS, 3 * HD)
    pairs = columns[:, :, HD:].reshape(2 * BLOCK, HEADS * PAIR)
    mine = lax.dynamic_index_in_dim(columns, head, axis=1, keepdims=False)
    mine = jnp.concatenate([mine[:, :HD], jnp.zeros_like(mine[:, :HD]), mine[:, HD:]], axis=1)
    dma = lambda *shape: pltpu.SemaphoreType.DMA(shape)
    vmem = pl.BlockSpec(memory_space=pltpu.VMEM)
    slots = BLK + planes * group * CAP
    return pl.pallas_call(
        functools.partial(fetch_kernel, planes, group),
        out_shape=(
            jax.ShapeDtypeStruct((BLK, BLOCK, PAIR), jnp.bfloat16),
            jax.ShapeDtypeStruct((slots, BLOCK, PAIR), jnp.bfloat16),
            jax.ShapeDtypeStruct((planes, group, CAP, part, 2 * BLOCK), jnp.bfloat16),
            jax.ShapeDtypeStruct((group, 8, 128), jnp.int32),
        ),
        in_specs=[vmem] * 4,
        out_specs=(vmem,) * 4,
        scratch_shapes=[
            pltpu.VMEM((BLK, BLOCK, 2 * BLOCK), jnp.bfloat16),
            pltpu.VMEM((planes, BLK, part, 2 * BLOCK), jnp.bfloat16),
            pltpu.VMEM((BLK, part, 2 * BLOCK), jnp.bfloat16),
            pltpu.VMEM((planes, group - 1, CAP, part, 2 * BLOCK), jnp.bfloat16),
            pltpu.VMEM((planes, HEADS, group * CAP, part, PAIR), jnp.bfloat16),
            pltpu.SMEM((group, 8, 128), jnp.int32),
            dma(3), dma(3), dma(3, 3), dma(3, 3), dma(group - 1), dma(group - 1),
            dma(2, planes // 2), dma(2, planes // 2),
            dma(planes, group - 1), dma(planes, group - 1), dma(planes, 3), dma(planes, 3),
            pltpu.SemaphoreType.DMA,
        ],
        compiler_params=pltpu.CompilerParams(
            collective_id=2, has_side_effects=True, vmem_limit_bytes=48 << 20
        ),
        name="fetch",
    )(own, asked, pairs, mine)


def return_kernel(
    planes, group, grads_ref, dq_ref, rows_ref, features_ref, norm_ref, pair_ref, single_ref, asks_ref,
    feature_ref, weight_ref,
    own_pairs, own_queries, heads, leaving, answers, partial, ring, summed, quarters, acc,
    o_send, o_recv, q_send, q_recv, x_send, x_recv, g_send, g_recv, r_send, r_recv, f_send, f_recv,
):
    node, head = lax.axis_index("node"), lax.axis_index("head")
    z, g = node // group, node % group
    half = planes // 2
    part = BLOCK // HEADS
    width = group * CAP
    x_peers = [(node, (head + d) % HEADS) for d in range(1, HEADS)]
    g_peers = [(z * group + (g + d) % group, head) for d in range(1, group)]
    right = (((z + 1) % planes) * group + g, head)
    left = (((z + planes - 1) % planes) * group + g, head)

    def remote(source, target, send, recv, peer):
        return pltpu.make_async_remote_copy(
            source, target, send, recv, device_id=peer, device_id_type=MESH
        )

    def quarter(h):
        return pl.ds(pl.multiple_of(h * part, part), part)

    barrier = pltpu.get_barrier_semaphore()
    for peer in x_peers + g_peers + [left, right]:
        pl.semaphore_signal(barrier, inc=1, device_id=peer, device_id_type=MESH)
    pl.semaphore_wait(barrier, len(x_peers + g_peers) + 2)

    order = list(reversed(ring_order(planes)))
    planes_in_order = [(z + offset + planes) % planes for offset in order]
    sent = []
    far = [
        [
            remote(
                grads_ref.at[pl.ds(BLK + at * width, width), quarter(peer[1])], heads.at[at, head],
                x_send.at[at, d], x_recv.at[at, d], peer,
            )
            for d, peer in enumerate(x_peers)
        ]
        for at in planes_in_order
    ]
    own = []
    for d, peer in enumerate(x_peers):
        blocks = pl.ds(peer[1] * HEADS, HEADS)
        own.append(remote(grads_ref.at[blocks], own_pairs.at[head], o_send.at[d], o_recv.at[d], peer))
        own.append(remote(dq_ref.at[blocks], own_queries.at[head], q_send.at[d], q_recv.at[d], peer))

    def begin(copies):
        for copy in copies:
            copy.start()
            sent.append(copy)

    for t in range(min(3, planes)):
        begin(far[t])
    acc[...] = jnp.zeros_like(acc)
    own_blocks = pl.ds(head * HEADS, HEADS)
    own_pairs[head] = grads_ref[own_blocks]
    own_queries[head] = dq_ref[own_blocks]

    def spread(t):
        at = planes_in_order[t]
        heads[at, head] = grads_ref[pl.ds(BLK + at * width, width), quarter(head)]
        for copy in far[t]:
            copy.wait_recv()
        if t + 3 < planes:
            begin(far[t + 3])
        if t == max(planes - 4, 0):
            begin(own)
        pairs = jnp.concatenate(
            [heads[at, h].reshape(width * part, PAIR) for h in range(HEADS)], axis=1
        )
        back = dot(pairs, pair_ref[...]).astype(jnp.bfloat16)
        leaving[at] = back.reshape(group, CAP, part, 2 * BLOCK)
        copies = [
            remote(
                leaving.at[at, peer[0] % group], answers.at[at, g], g_send.at[at, d], g_recv.at[at, d], peer
            )
            for d, peer in enumerate(g_peers)
        ]
        begin(copies)
        answers[at, g] = leaving[at, g]
        acc[...] += dot(pairs, rows_ref[at].reshape(width * part, 2 * BLOCK), TN)
        return copies

    def hop(way, step, at):
        source, target = partial.at[at], ring.at[way, step]
        if step == 0:
            blocks = pl.ds(way * (BLK // 2), BLK // 2)
            source, target = source.at[blocks], target.at[blocks]
        return remote(
            source, target, r_send.at[way, step], r_recv.at[way, step], left if way else right
        )

    def gather(t, copies):
        at, offset = planes_in_order[t], order[t]
        for copy in copies:
            copy.wait_recv()
        side = width * part
        column = lax.broadcasted_iota(jnp.int32, (1, side), 1)
        target = column % part
        for j in range(width):
            block = asks_ref[j // CAP, 0, at * CAP + j % CAP]
            target = target + jnp.where(column // part == j, block * part, 0)
        row = lax.broadcasted_iota(jnp.int32, (BLK * part, side), 0)
        chosen = jnp.where(row == target, 1.0, 0.0).astype(jnp.bfloat16)
        total = dot(chosen, answers[at].reshape(side, 2 * BLOCK)).reshape(BLK, part, 2 * BLOCK)
        if offset == half:
            partial[at] = total.astype(jnp.bfloat16)
            for way in range(2):
                begin([hop(way, 0, at)])
            return
        step = half - 1 - abs(offset)
        ways = [0] if offset > 0 else [1] if offset < 0 else [0, 1]
        for way in ways:
            hop(way, step, at).wait_recv()
            if step == 0:
                mid = BLK // 2
                if way == 0:
                    total = jnp.concatenate(
                        [total[:mid] + ring[way, step, :mid].astype(jnp.float32), total[mid:]], axis=0
                    )
                else:
                    total = jnp.concatenate(
                        [total[:mid], total[mid:] + ring[way, step, mid:].astype(jnp.float32)], axis=0
                    )
            else:
                total = total + ring[way, step].astype(jnp.float32)
        if offset:
            partial[at] = total.astype(jnp.bfloat16)
            begin([hop(ways[0], step + 1, at)])
        else:
            summed[...] = total.astype(jnp.bfloat16)

    waiting = None
    for t in range(planes):
        copies = spread(t)
        if t:
            gather(t - 1, waiting)
        waiting = copies
    gather(planes - 1, waiting)
    final = [
        remote(
            summed.at[pl.ds(peer[1] * HEADS, HEADS)], quarters.at[head], f_send.at[d], f_recv.at[d], peer
        )
        for d, peer in enumerate(x_peers)
    ]
    begin(final)
    quarters[head] = summed[own_blocks]

    for copy in own:
        copy.wait_recv()
    rows = HEADS * BLOCK
    pairs = jnp.concatenate([own_pairs[h].reshape(rows, PAIR) for h in range(HEADS)], axis=1)
    queries = jnp.concatenate(
        [
            jnp.concatenate(
                [own_queries[h, :, :, :HD], own_queries[h, :, :, HD:]], axis=1
            ).reshape(rows, HD)
            for h in range(HEADS)
        ],
        axis=1,
    )
    features = features_ref[...]
    pair_weight = acc[...] + dot(pairs, features, TN)
    single_weight = dot(queries, features, TN)
    for h in range(HEADS):
        weight_ref[h, :HD] = single_weight[h * HD : (h + 1) * HD]
        weight_ref[h, HD:] = pair_weight[h * PAIR : (h + 1) * PAIR]
    base = norm_ref[...] + dot(pairs, pair_ref[...]) + dot(queries, single_ref[...])
    base = base.reshape(HEADS, HEADS, part, 2 * BLOCK)
    for copy in final:
        copy.wait_recv()
    for h in range(HEADS):
        feature_ref[:, h] = (base[:, h] + quarters[h].astype(jnp.float32)).astype(jnp.bfloat16)
    for copy in sent:
        copy.wait_send()


def give_back(grads, dq, rows, features, norm_grad, in_weight, asks, node_count):
    planes, group = torus(node_count)
    part = BLOCK // HEADS
    wide = 2 * BLOCK
    columns = in_weight.T.reshape(HEADS, 3 * HD, wide)
    pair = columns[:, HD:].reshape(HEADS * PAIR, wide)
    single = columns[:, :HD].reshape(HEADS * HD, wide)
    dma = lambda *shape: pltpu.SemaphoreType.DMA(shape)
    vmem = pl.BlockSpec(memory_space=pltpu.VMEM)
    low = lambda *shape: pltpu.VMEM(shape, jnp.bfloat16)
    feature_grad, weight = pl.pallas_call(
        functools.partial(return_kernel, planes, group),
        out_shape=(
            jax.ShapeDtypeStruct((HEADS, HEADS, part, wide), jnp.bfloat16),
            jax.ShapeDtypeStruct((HEADS, 3 * HD, wide), jnp.float32),
        ),
        in_specs=[vmem] * 7 + [pl.BlockSpec(memory_space=pltpu.SMEM)],
        out_specs=(vmem,) * 2,
        scratch_shapes=[
            low(HEADS, HEADS, BLOCK, PAIR),
            low(HEADS, HEADS, HD, PAIR),
            low(planes, HEADS, group * CAP, part, PAIR),
            low(planes, group, CAP, part, wide),
            low(planes, group, CAP, part, wide),
            low(planes, BLK, part, wide),
            low(2, planes // 2, BLK, part, wide),
            low(BLK, part, wide),
            low(HEADS, HEADS, part, wide),
            pltpu.VMEM((HEADS * PAIR, wide), jnp.float32),
            dma(3), dma(3), dma(3), dma(3), dma(planes, 3), dma(planes, 3),
            dma(planes, group - 1), dma(planes, group - 1),
            dma(2, planes // 2), dma(2, planes // 2), dma(3), dma(3),
        ],
        compiler_params=pltpu.CompilerParams(
            collective_id=3, has_side_effects=True, vmem_limit_bytes=56 << 20
        ),
        name="give_back",
    )(grads, dq, rows, features, norm_grad, pair, single, asks)
    return feature_grad.reshape(HEADS * BLOCK, wide), weight.reshape(HEADS * 3 * HD, wide)


def on_device(features, in_weight, out_weight, cotangent, key_slots, block_count, wanted):
    node_count = lax.axis_size("node")
    node_rows = BLK * BLOCK
    total_nodes = node_rows * node_count
    queries, table, rows, asks = fetch(features, in_weight, wanted, node_count)
    queries = queries.reshape(node_rows, PAIR)
    slots = key_slots.reshape(-1)
    wide, stat = forward(slots, block_count, queries, table)
    attended = wide[:, HD:]
    attended_rows = lax.all_to_all(attended, "head", split_axis=0, concat_axis=1, tiled=True)
    summed = features.astype(jnp.float32) + jnp.dot(
        attended_rows, out_weight, preferred_element_type=jnp.float32
    )
    root_mean = jnp.sqrt(jnp.mean(summed * summed, axis=-1, keepdims=True) + 1e-06)
    normed = summed / root_mean
    output = normed.astype(jnp.bfloat16)
    upstream = cotangent.astype(jnp.float32)
    norm_grad = (
        upstream - normed * jnp.mean(upstream * normed, axis=-1, keepdims=True)
    ) / root_mean
    norm_grad_low = norm_grad.astype(jnp.bfloat16)
    out_weight_grad = jnp.dot(attended_rows.T, norm_grad_low, preferred_element_type=jnp.float32)
    attended_grad = jnp.dot(norm_grad_low, out_weight.T, preferred_element_type=jnp.float32).astype(
        jnp.bfloat16
    )
    attended_grad = lax.all_to_all(attended_grad, "head", split_axis=1, concat_axis=0, tiled=True)
    both = jnp.concatenate([queries[:, :HD], attended_grad], axis=1)
    dq, grads = backward(slots, block_count, both, wide, stat, table)
    feature_grad, in_weight_grad = give_back(
        grads, dq, rows, features, norm_grad, in_weight, asks, node_count
    )
    in_weight_grad, out_weight_grad = sum_weights(in_weight_grad, out_weight_grad, node_count)
    grad_factor = total_nodes ** (-0.5)
    return (
        output,
        feature_grad,
        in_weight_grad * grad_factor,
        out_weight_grad * grad_factor,
    )


def solution(mesh):
    placed = (
        P(("node", "head"), None),
        P(),
        P(),
        P(("node", "head"), None),
        P("node", None),
        P("node"),
        P("node", None, None),
    )
    return jax.shard_map(
        on_device,
        mesh=mesh,
        in_specs=placed,
        out_specs=(
            P(("node", "head"), None),
            P(("node", "head"), None),
            P(None, "head"),
            P("head", None),
        ),
        check_vma=False,
    )
```

```python
import functools

import jax
import jax.numpy as jnp
from jax import lax
from jax.experimental import pallas as pl
from jax.experimental.pallas import tpu as pltpu
from jax.sharding import PartitionSpec as P

HEADS = 4
HD = 64
BLOCK = 128
BLK = 16
PER = 12
CAP = 2
PAIR = 2 * HD
WIDE = 2 * BLOCK
SHARED = BLOCK // 2
PART = SHARED // HEADS
LUMP = PART + (BLOCK - SHARED) // 2
SCALE = HD ** (-0.5)
NT = (((1,), (1,)), ((), ()))
TN = (((0,), (0,)), ((), ()))
MESH = pl.DeviceIdType.MESH


def dot(a, b, dims=(((1,), (0,)), ((), ()))):
    return lax.dot_general(a, b, dims, preferred_element_type=jnp.float32)


def forward_kernel(slots_ref, count_ref, q_ref, table_ref, out_ref, stat_ref):
    b = pl.program_id(0)
    count = count_ref[b]
    query = q_ref[...]
    chosen = [table_ref[slots_ref[b * PER + j]] for j in range(PER)]
    scores = []
    for j in range(0, PER, 2):
        pair = dot(query, jnp.concatenate(chosen[j : j + 2], axis=0), NT)
        for i in range(2):
            dead = jnp.where(j + i < count, 0.0, -1e30)
            scores.append(pair[:, i * BLOCK : (i + 1) * BLOCK] + dead)
    highest = scores[0]
    for part in scores[1:]:
        highest = jnp.maximum(highest, part)
    highest = jnp.max(highest, axis=1, keepdims=True)
    total = jnp.zeros((BLOCK, BLOCK), jnp.float32)
    result = jnp.zeros((BLOCK, PAIR), jnp.float32)
    for j in range(0, PER, 2):
        raised = [jnp.exp(part - highest) for part in scores[j : j + 2]]
        total = total + raised[0] + raised[1]
        result = result + dot(
            jnp.concatenate([x.astype(jnp.bfloat16) for x in raised], axis=1),
            jnp.concatenate(chosen[j : j + 2], axis=0),
        )
    total = jnp.sum(total, axis=1, keepdims=True)
    out_ref[...] = (result / total).astype(jnp.bfloat16)
    lane = lax.broadcasted_iota(jnp.int32, stat_ref.shape, 1)
    stat_ref[...] = jnp.where(lane < HD, highest, 1.0 / total)


def forward(slots, count, query, table):
    rows = BLK * BLOCK
    grid_spec = pltpu.PrefetchScalarGridSpec(
        num_scalar_prefetch=2,
        grid=(BLK,),
        in_specs=[
            pl.BlockSpec((BLOCK, PAIR), lambda b, *_: (b, 0)),
            pl.BlockSpec(table.shape, lambda b, *_: (0, 0, 0)),
        ],
        out_specs=[
            pl.BlockSpec((BLOCK, PAIR), lambda b, *_: (b, 0)),
            pl.BlockSpec((BLOCK, PAIR), lambda b, *_: (b, 0)),
        ],
    )
    return pl.pallas_call(
        forward_kernel,
        grid_spec=grid_spec,
        out_shape=(
            jax.ShapeDtypeStruct((rows, PAIR), jnp.bfloat16),
            jax.ShapeDtypeStruct((rows, PAIR), jnp.float32),
        ),
        compiler_params=pltpu.CompilerParams(vmem_limit_bytes=40 << 20),
        cost_estimate=pl.CostEstimate(
            flops=4 * BLK * PER * BLOCK**3, bytes_accessed=8 << 20, transcendentals=BLK * PER * BLOCK**2
        ),
        name="attend",
    )(slots, count, query, table)


def backward_kernel(
    slots_ref, count_ref, qg_ref, att_ref, stat_ref, table_ref, dq_ref, grads_ref, acc_ref, keys_ref, terms_ref
):
    b = pl.program_id(0)

    @pl.when(b == 0)
    def _():
        acc_ref[...] = jnp.zeros_like(acc_ref)

    count = count_ref[b]
    both = qg_ref[...]
    lane = lax.broadcasted_iota(jnp.int32, both.shape, 1)
    zero = jnp.zeros_like(both)
    stacked = jnp.concatenate(
        [jnp.where(lane < HD, both, zero), jnp.where(lane < HD, zero, both)], axis=0
    )
    dots = jnp.sum(
        jnp.where(lane < HD, 0.0, both.astype(jnp.float32) * att_ref[...].astype(jnp.float32)),
        axis=1,
        keepdims=True,
    )
    flipped = jnp.where((lane >= 32) & (lane < HD), dots, stat_ref[...]).T
    highest, dots, inverse = flipped[0:1], flipped[32:33], flipped[HD : HD + 1]
    slots = [slots_ref[b * PER + j] for j in range(PER)]
    for j in range(PER):
        keys_ref[j * BLOCK : (j + 1) * BLOCK] = table_ref[slots[j]]
    for j in range(0, PER, 2):
        products = dot(keys_ref[j * BLOCK : (j + 2) * BLOCK], stacked, NT)
        for i in range(2):
            rows = slice(i * BLOCK, (i + 1) * BLOCK)
            top = highest + jnp.where(j + i < count, 0.0, 1e30)
            attention = jnp.exp(products[rows, :BLOCK] - top) * inverse
            score_grad = attention * (products[rows, BLOCK:] - dots)
            terms_ref[(j + i) * BLOCK : (j + i + 1) * BLOCK] = jnp.concatenate(
                [score_grad.astype(jnp.bfloat16), attention.astype(jnp.bfloat16)], axis=1
            )
    dq = dot(keys_ref[...], terms_ref[:, :BLOCK], TN)
    for j in range(0, PER, 2):
        grads = dot(terms_ref[j * BLOCK : (j + 2) * BLOCK], stacked)
        for i in range(2):
            acc_ref[slots[j + i]] += grads[i * BLOCK : (i + 1) * BLOCK]
    dq = (dq.T * SCALE).astype(jnp.bfloat16)
    dq_ref[0] = jnp.concatenate([dq[:HD, :HD], dq[HD:, :HD]], axis=1)

    @pl.when(b == pl.num_programs(0) - 1)
    def _():
        grads_ref[...] = acc_ref[...].astype(jnp.bfloat16)


def backward(slots, count, query_grad, attended, stat, table):
    whole = lambda shape: pl.BlockSpec(shape, lambda b, *_: (0,) * len(shape))
    rowwise = pl.BlockSpec((BLOCK, PAIR), lambda b, *_: (b, 0))
    grid_spec = pltpu.PrefetchScalarGridSpec(
        num_scalar_prefetch=2,
        grid=(BLK,),
        in_specs=[rowwise, rowwise, rowwise, whole(table.shape)],
        out_specs=[pl.BlockSpec((1, HD, PAIR), lambda b, *_: (b, 0, 0)), whole(table.shape)],
        scratch_shapes=[
            pltpu.VMEM(table.shape, jnp.float32),
            pltpu.VMEM((PER * BLOCK, PAIR), jnp.bfloat16),
            pltpu.VMEM((PER * BLOCK, 2 * BLOCK), jnp.bfloat16),
        ],
    )
    return pl.pallas_call(
        backward_kernel,
        grid_spec=grid_spec,
        out_shape=(
            jax.ShapeDtypeStruct((BLK, HD, PAIR), jnp.bfloat16),
            jax.ShapeDtypeStruct(table.shape, jnp.bfloat16),
        ),
        compiler_params=pltpu.CompilerParams(vmem_limit_bytes=56 << 20),
        cost_estimate=pl.CostEstimate(
            flops=10 * BLK * PER * BLOCK**3, bytes_accessed=16 << 20, transcendentals=BLK * PER * BLOCK**2
        ),
        name="attend_back",
    )(slots, count, query_grad, attended, stat, table)


def torus(node_count):
    rows = 4 if node_count >= 64 else 2
    return node_count // (2 * rows), rows * 2


def weights_kernel(
    planes, group, in_ref, out_ref, sum_ref,
    mine, x_in, x_sum, z_in, z_sum, g_in, piece,
    x_send, x_recv, z_send, z_recv, g_send, g_recv, p_send, p_recv, f_send, f_recv,
):
    node, head = lax.axis_index("node"), lax.axis_index("head")
    z, g = node // group, node % group
    rows = sum_ref.shape[2]
    x_peers = [(node, (head + d) % HEADS) for d in range(1, HEADS)]
    z_peers = [(((z + d) % planes) * group + g, head) for d in range(1, planes)]
    g_peers = [(z * group + (g + d) % group, head) for d in range(1, group)]
    barrier = pltpu.get_barrier_semaphore()
    for peer in x_peers + z_peers + g_peers:
        pl.semaphore_signal(barrier, inc=1, device_id=peer, device_id_type=MESH)

    for h in range(HEADS):
        chunk = jnp.concatenate(
            [in_ref[h * 3 * HD : (h + 1) * 3 * HD], out_ref[h * HD : (h + 1) * HD]], axis=0
        )
        chunk = jnp.concatenate([chunk[:, :128], chunk[:, 128:]], axis=0)
        mine[h] = chunk.reshape(planes, group, rows, 128)
    pl.semaphore_wait(barrier, len(x_peers + z_peers + g_peers))

    copies = [
        pltpu.make_async_remote_copy(
            mine.at[peer[1]], x_in.at[d], x_send.at[d], x_recv.at[d], device_id=peer, device_id_type=MESH
        )
        for d, peer in enumerate(x_peers)
    ]
    for copy in copies:
        copy.start()
    for copy in copies:
        copy.wait()
    x_sum[...] = mine[head] + x_in[0] + x_in[1] + x_in[2]

    copies = [
        pltpu.make_async_remote_copy(
            x_sum.at[(z + d + 1) % planes], z_in.at[d], z_send.at[d], z_recv.at[d],
            device_id=peer, device_id_type=MESH,
        )
        for d, peer in enumerate(z_peers)
    ]
    for copy in copies:
        copy.start()
    for copy in copies:
        copy.wait()
    total = x_sum[z]
    for d in range(planes - 1):
        total = total + z_in[d]
    z_sum[...] = total

    copies = [
        pltpu.make_async_remote_copy(
            z_sum.at[(g + d + 1) % group], g_in.at[d], g_send.at[d], g_recv.at[d],
            device_id=peer, device_id_type=MESH,
        )
        for d, peer in enumerate(g_peers)
    ]
    for copy in copies:
        copy.start()
    for copy in copies:
        copy.wait()
    total = z_sum[g]
    for d in range(group - 1):
        total = total + g_in[d]
    piece[...] = total

    copies = [
        pltpu.make_async_remote_copy(
            piece, sum_ref.at[z, g], p_send.at[d], p_recv.at[d], device_id=peer, device_id_type=MESH
        )
        for d, peer in enumerate(g_peers)
    ]
    for copy in copies:
        copy.start()
    sum_ref[z, g] = total
    for copy in copies:
        copy.wait()

    copies = [
        pltpu.make_async_remote_copy(
            sum_ref.at[z], sum_ref.at[z], f_send.at[d], f_recv.at[d], device_id=peer, device_id_type=MESH
        )
        for d, peer in enumerate(z_peers)
    ]
    for copy in copies:
        copy.start()
    for copy in copies:
        copy.wait()


def sum_weights(in_grad, out_grad, node_count):
    planes, group = torus(node_count)
    rows = 4 * HD * 2 // (planes * group)
    full = (planes, group, rows, 128)
    dma = lambda n: pltpu.SemaphoreType.DMA((n,))
    vmem = pl.BlockSpec(memory_space=pltpu.VMEM)
    total = pl.pallas_call(
        functools.partial(weights_kernel, planes, group),
        out_shape=jax.ShapeDtypeStruct(full, jnp.float32),
        in_specs=[vmem, vmem],
        out_specs=vmem,
        scratch_shapes=[
            pltpu.VMEM((HEADS,) + full, jnp.float32),
            pltpu.VMEM((HEADS - 1,) + full, jnp.float32),
            pltpu.VMEM(full, jnp.float32),
            pltpu.VMEM((planes - 1,) + full[1:], jnp.float32),
            pltpu.VMEM(full[1:], jnp.float32),
            pltpu.VMEM((group - 1,) + full[2:], jnp.float32),
            pltpu.VMEM(full[2:], jnp.float32),
            dma(HEADS - 1), dma(HEADS - 1),
            dma(planes - 1), dma(planes - 1),
            dma(group - 1), dma(group - 1),
            dma(group - 1), dma(group - 1),
            dma(planes - 1), dma(planes - 1),
        ],
        compiler_params=pltpu.CompilerParams(
            collective_id=1, has_side_effects=True, vmem_limit_bytes=32 << 20
        ),
        name="sum_weights",
    )(in_grad, out_grad)
    total = total.reshape(2, 4 * HD, 128).transpose(1, 0, 2).reshape(4 * HD, 2 * 128)
    return total[: 3 * HD].T, total[3 * HD :]


def ring_order(planes):
    half = planes // 2
    return [0] + [s * k for k in range(1, half) for s in (-1, 1)] + [half]


def fetch_kernel(
    planes, group, own_ref, asked_ref, pairs_ref, mine_ref, query_ref, table_ref, shared_ref, asks_ref,
    whole, ring, chunk, picked, landed, made, asks,
    b_send, b_recv, q_send, q_recv, r_send, r_recv, g_send, g_recv, x_send, x_recv, asks_sem,
):
    node, head = lax.axis_index("node"), lax.axis_index("head")
    z, g = node // group, node % group
    half = planes // 2
    part = PART
    x_peers = [(node, (head + d) % HEADS) for d in range(1, HEADS)]
    g_peers = [(z * group + (g + d) % group, head) for d in range(1, group)]
    right = (((z + 1) % planes) * group + g, head)
    left = (((z + planes - 1) % planes) * group + g, head)

    def remote(source, target, send, recv, peer):
        return pltpu.make_async_remote_copy(
            source, target, send, recv, device_id=peer, device_id_type=MESH
        )

    def quarter(h):
        return pl.ds(pl.multiple_of(h * part, part), part)

    barrier = pltpu.get_barrier_semaphore()
    for peer in x_peers + g_peers + [left, right]:
        pl.semaphore_signal(barrier, inc=1, device_id=peer, device_id_type=MESH)
    pl.semaphore_wait(barrier, len(x_peers + g_peers) + 2)

    own_blocks = pl.ds(head * HEADS, HEADS)
    first, rest = [], []
    for d, peer in enumerate(x_peers):
        for e in range(HEADS + 1):
            rows = pl.ds(SHARED, BLOCK - SHARED) if e == 1 else quarter((peer[1] + max(e - 1, 0)) % HEADS)
            (first if e < 2 else rest).append(
                remote(
                    own_ref.at[:, rows], whole.at[own_blocks, rows], b_send.at[d, e], b_recv.at[d, e], peer
                )
            )
    questions = [
        remote(asked_ref.at[peer[0] % group], asks_ref.at[g], q_send.at[d], q_recv.at[d], peer)
        for d, peer in enumerate(g_peers)
    ]
    for copy in first + questions + rest:
        copy.start()
    whole[own_blocks] = own_ref[...]
    asks_ref[g] = asked_ref[g]
    for copy in first:
        copy.wait_recv()
    ring[z, :, :PART] = whole[:, quarter(head)]
    low = (BLOCK - SHARED) // 2

    @pl.loop(0, BLK)
    def _(b):
        pairs = dot(whole[b, SHARED:], mine_ref[:, PAIR:]).astype(jnp.bfloat16)
        table_ref[b, SHARED:] = pairs
        ring[z, b, PART:] = jnp.concatenate([pairs[:low], pairs[low:]], axis=1)


    def hop(way, k):
        at = (z - k + planes) % planes if way == 0 else (z + k) % planes
        view = ring.at[at]
        if k == half - 1:
            view = view.at[pl.ds(0, BLK // 2)] if way == 0 else view.at[pl.ds(BLK // 2, BLK // 2)]
        return remote(
            view, view, r_send.at[way, k], r_recv.at[way, k], right if way == 0 else left
        )

    hops = {(way, k): hop(way, k) for way in range(2) for k in range(half)}
    for way in range(2):
        hops[way, 0].start()
    for copy in questions:
        copy.wait_recv()
    answer = pltpu.make_async_copy(asks_ref, asks, asks_sem)
    answer.start()
    answer.wait()

    order = ring_order(planes)
    sent = []

    def bring(t):
        offset = order[t]
        at = (z + offset + planes) % planes
        if offset == half:
            hops[0, half - 1].wait_recv()
            hops[1, half - 1].wait_recv()
        elif offset:
            way, k = (0, -offset) if offset < 0 else (1, offset)
            hops[way, k - 1].wait_recv()
            hops[way, k].start()
        chunk[...] = ring[at]
        for d in range(group - 1, -1, -1):
            peer = (g + d) % group
            for c in range(CAP):
                block = chunk[asks[peer, 0, at * CAP + c]]
                if d:
                    picked[at, d - 1, c] = block
                else:
                    landed[at, g, c] = block
            if d:
                copy = remote(
                    picked.at[at, d - 1], landed.at[at, g], g_send.at[at, d - 1], g_recv.at[at, d - 1],
                    g_peers[d - 1],
                )
                copy.start()
                sent.append(copy)

    arriving = []

    def make(t):
        at = (z + order[t] + planes) % planes
        for d in range(1, group):
            remote(
                picked.at[at, d - 1], landed.at[at, g], g_send.at[at, d - 1], g_recv.at[at, d - 1],
                g_peers[d - 1],
            ).wait_recv()
        rows = landed[at].reshape(group * CAP, LUMP, WIDE)
        shared = rows[:, :PART].reshape(group * CAP * PART, WIDE)
        shared_ref[at] = shared
        pairs = dot(shared, pairs_ref[...]).astype(jnp.bfloat16)
        for h in range(HEADS):
            made[at, h] = pairs[:, h * PAIR : (h + 1) * PAIR].reshape(group * CAP, part, PAIR)
        slots = pl.ds(BLK + at * group * CAP, group * CAP)
        for d, peer in enumerate(x_peers):
            copy = remote(
                made.at[at, peer[1]], table_ref.at[slots, quarter(head)], x_send.at[at, d], x_recv.at[at, d],
                peer,
            )
            copy.start()
            sent.append(copy)
            arriving.append(copy)
        table_ref[slots, quarter(head)] = made[at, head]
        table_ref[slots, SHARED : SHARED + low] = rows[:, PART:, :PAIR]
        table_ref[slots, SHARED + low :] = rows[:, PART:, PAIR:]

    bring(0)
    for copy in rest:
        copy.wait_recv()

    @pl.loop(0, BLK)
    def _(b):
        both = dot(whole[b], mine_ref[...])
        query_ref[b] = (both[:, :PAIR] * SCALE).astype(jnp.bfloat16)
        table_ref[b, :SHARED] = both[:SHARED, PAIR:].astype(jnp.bfloat16)

    for t in range(1, planes):
        bring(t)
        make(t - 1)
    make(planes - 1)
    for copy in arriving:
        copy.wait_recv()
    for copy in first + rest + questions + list(hops.values()) + sent:
        copy.wait_send()


def fetch(features, in_weight, wanted, node_count):
    planes, group = torus(node_count)
    part = PART
    head = lax.axis_index("head")
    own = features.reshape(HEADS, BLOCK, 2 * BLOCK)
    asked = wanted.reshape(planes, group, CAP).transpose(1, 0, 2).reshape(group, 1, planes * CAP)
    asked = jnp.pad(asked, ((0, 0), (0, 7), (0, 128 - planes * CAP)))
    columns = in_weight.reshape(2 * BLOCK, HEADS, 3 * HD)
    pairs = columns[:, :, HD:].reshape(2 * BLOCK, HEADS * PAIR)
    mine = lax.dynamic_index_in_dim(columns, head, axis=1, keepdims=False)
    mine = jnp.concatenate([mine[:, :HD], jnp.zeros_like(mine[:, :HD]), mine[:, HD:]], axis=1)
    dma = lambda *shape: pltpu.SemaphoreType.DMA(shape)
    vmem = pl.BlockSpec(memory_space=pltpu.VMEM)
    slots = BLK + planes * group * CAP
    return pl.pallas_call(
        functools.partial(fetch_kernel, planes, group),
        out_shape=(
            jax.ShapeDtypeStruct((BLK, BLOCK, PAIR), jnp.bfloat16),
            jax.ShapeDtypeStruct((slots, BLOCK, PAIR), jnp.bfloat16),
            jax.ShapeDtypeStruct((planes, group * CAP * PART, WIDE), jnp.bfloat16),
            jax.ShapeDtypeStruct((group, 8, 128), jnp.int32),
        ),
        in_specs=[vmem] * 4,
        out_specs=(vmem,) * 4,
        scratch_shapes=[
            pltpu.VMEM((BLK, BLOCK, 2 * BLOCK), jnp.bfloat16),
            pltpu.VMEM((planes, BLK, LUMP, WIDE), jnp.bfloat16),
            pltpu.VMEM((BLK, LUMP, WIDE), jnp.bfloat16),
            pltpu.VMEM((planes, group - 1, CAP, LUMP, WIDE), jnp.bfloat16),
            pltpu.VMEM((planes, group, CAP, LUMP, WIDE), jnp.bfloat16),
            pltpu.VMEM((planes, HEADS, group * CAP, part, PAIR), jnp.bfloat16),
            pltpu.SMEM((group, 8, 128), jnp.int32),
            dma(3, HEADS + 1), dma(3, HEADS + 1), dma(group - 1), dma(group - 1),
            dma(2, planes // 2), dma(2, planes // 2),
            dma(planes, group - 1), dma(planes, group - 1), dma(planes, 3), dma(planes, 3),
            pltpu.SemaphoreType.DMA,
        ],
        compiler_params=pltpu.CompilerParams(
            collective_id=2, has_side_effects=True, vmem_limit_bytes=48 << 20
        ),
        name="fetch",
    )(own, asked, pairs, mine)


def return_kernel(
    planes, group, grads_ref, dq_ref, shared_ref, features_ref, norm_ref, pair_ref, single_ref, asks_ref,
    feature_ref, weight_ref,
    own_pairs, own_queries, heads, leaving, answers, partial, ring, summed, late, quarters, acc,
    o_send, o_recv, l_send, l_recv, q_send, q_recv, x_send, x_recv, g_send, g_recv, r_send, r_recv, f_send, f_recv,
):
    node, head = lax.axis_index("node"), lax.axis_index("head")
    z, g = node // group, node % group
    half = planes // 2
    part = PART
    low = (BLOCK - SHARED) // 2
    width = group * CAP
    x_peers = [(node, (head + d) % HEADS) for d in range(1, HEADS)]
    g_peers = [(z * group + (g + d) % group, head) for d in range(1, group)]
    right = (((z + 1) % planes) * group + g, head)
    left = (((z + planes - 1) % planes) * group + g, head)

    def remote(source, target, send, recv, peer):
        return pltpu.make_async_remote_copy(
            source, target, send, recv, device_id=peer, device_id_type=MESH
        )

    def quarter(h):
        return pl.ds(pl.multiple_of(h * part, part), part)

    barrier = pltpu.get_barrier_semaphore()
    for peer in x_peers + g_peers + [left, right]:
        pl.semaphore_signal(barrier, inc=1, device_id=peer, device_id_type=MESH)
    pl.semaphore_wait(barrier, len(x_peers + g_peers) + 2)

    order = list(reversed(ring_order(planes)))
    planes_in_order = [(z + offset + planes) % planes for offset in order]
    sent = []
    far = [
        [
            remote(
                grads_ref.at[pl.ds(BLK + at * width, width), quarter(peer[1])], heads.at[at, head],
                x_send.at[at, d], x_recv.at[at, d], peer,
            )
            for d, peer in enumerate(x_peers)
        ]
        for at in planes_in_order
    ]
    own = []
    for d, peer in enumerate(x_peers):
        blocks = pl.ds(peer[1] * HEADS, HEADS)
        own.append(
            remote(
                grads_ref.at[blocks, pl.ds(0, SHARED)], own_pairs.at[head, :, pl.ds(0, SHARED)],
                o_send.at[d], o_recv.at[d], peer,
            )
        )
        own.append(remote(dq_ref.at[blocks], own_queries.at[head], q_send.at[d], q_recv.at[d], peer))

    def begin(copies):
        for copy in copies:
            copy.start()
            sent.append(copy)

    for t in range(min(3, planes)):
        begin(far[t])
    acc[...] = jnp.zeros_like(acc)
    own_blocks = pl.ds(head * HEADS, HEADS)
    own_pairs[head, :, :SHARED] = grads_ref[own_blocks, :SHARED]
    own_queries[head] = dq_ref[own_blocks]

    def spread(t):
        at = planes_in_order[t]
        slots = pl.ds(BLK + at * width, width)
        heads[at, head] = grads_ref[slots, quarter(head)]
        for copy in far[t]:
            copy.wait_recv()
        if t + 3 < planes:
            begin(far[t + 3])
        if t == max(planes - 4, 0):
            begin(own)
        pairs = jnp.concatenate(
            [heads[at, h].reshape(width * part, PAIR) for h in range(HEADS)], axis=1
        )
        back = dot(pairs, pair_ref[...]).astype(jnp.bfloat16)
        leaving[at, :, :, :PART] = back.reshape(group, CAP, part, WIDE)
        for i in range(2):
            some = grads_ref[slots, SHARED + i * low : SHARED + (i + 1) * low]
            leaving[at, :, :, PART:, i * PAIR : (i + 1) * PAIR] = some.reshape(group, CAP, low, PAIR)
        copies = [
            remote(
                leaving.at[at, peer[0] % group], answers.at[at, g], g_send.at[at, d], g_recv.at[at, d], peer
            )
            for d, peer in enumerate(g_peers)
        ]
        begin(copies)
        answers[at, g] = leaving[at, g]
        acc[...] += dot(pairs, shared_ref[at], TN)
        return copies

    def hop(way, step, at):
        source, target = partial.at[at], ring.at[way, step]
        if step == 0:
            blocks = pl.ds(way * (BLK // 2), BLK // 2)
            source, target = source.at[blocks], target.at[blocks]
        return remote(
            source, target, r_send.at[way, step], r_recv.at[way, step], left if way else right
        )

    def gather(t, copies):
        at, offset = planes_in_order[t], order[t]
        for copy in copies:
            copy.wait_recv()
        side = width * part
        column = lax.broadcasted_iota(jnp.int32, (1, side), 1)
        target = column % part
        for j in range(width):
            block = asks_ref[j // CAP, 0, at * CAP + j % CAP]
            target = target + jnp.where(column // part == j, block * part, 0)
        row = lax.broadcasted_iota(jnp.int32, (BLK * part, side), 0)
        chosen = jnp.where(row == target, 1.0, 0.0).astype(jnp.bfloat16)
        total = jnp.concatenate(
            [
                dot(
                    chosen, answers[at, :, :, i * part : (i + 1) * part].reshape(side, WIDE)
                ).reshape(BLK, part, WIDE)
                for i in range(LUMP // part)
            ],
            axis=1,
        )
        if offset == half:
            partial[at] = total.astype(jnp.bfloat16)
            for way in range(2):
                begin([hop(way, 0, at)])
            return
        step = half - 1 - abs(offset)
        ways = [0] if offset > 0 else [1] if offset < 0 else [0, 1]
        for way in ways:
            hop(way, step, at).wait_recv()
            if step == 0:
                mid = BLK // 2
                if way == 0:
                    total = jnp.concatenate(
                        [total[:mid] + ring[way, step, :mid].astype(jnp.float32), total[mid:]], axis=0
                    )
                else:
                    total = jnp.concatenate(
                        [total[:mid], total[mid:] + ring[way, step, mid:].astype(jnp.float32)], axis=0
                    )
            else:
                total = total + ring[way, step].astype(jnp.float32)
        if offset:
            partial[at] = total.astype(jnp.bfloat16)
            begin([hop(ways[0], step + 1, at)])
        else:
            summed[...] = total[:, :PART].astype(jnp.bfloat16)
            for i in range(2):
                rows = slice(SHARED + i * low, SHARED + (i + 1) * low)
                fetched = total[:, PART:, i * PAIR : (i + 1) * PAIR]
                late[:, i * low : (i + 1) * low] = (
                    grads_ref[:BLK, rows].astype(jnp.float32) + fetched
                ).astype(jnp.bfloat16)

    waiting = None
    for t in range(planes):
        copies = spread(t)
        if t:
            gather(t - 1, waiting)
        waiting = copies
    gather(planes - 1, waiting)
    final = [
        remote(
            summed.at[pl.ds(peer[1] * HEADS, HEADS)], quarters.at[head], f_send.at[d], f_recv.at[d], peer
        )
        for d, peer in enumerate(x_peers)
    ]
    tail = [
        remote(
            late.at[pl.ds(peer[1] * HEADS, HEADS)], own_pairs.at[head, :, pl.ds(SHARED, BLOCK - SHARED)],
            l_send.at[d], l_recv.at[d], peer,
        )
        for d, peer in enumerate(x_peers)
    ]
    begin(tail + final)
    own_pairs[head, :, SHARED:] = late[own_blocks]
    quarters[head] = summed[own_blocks]

    for copy in own + tail:
        copy.wait_recv()
    rows = HEADS * BLOCK
    pairs = jnp.concatenate([own_pairs[h].reshape(rows, PAIR) for h in range(HEADS)], axis=1)
    queries = jnp.concatenate(
        [
            jnp.concatenate(
                [own_queries[h, :, :, :HD], own_queries[h, :, :, HD:]], axis=1
            ).reshape(rows, HD)
            for h in range(HEADS)
        ],
        axis=1,
    )
    features = features_ref[...]
    pair_weight = acc[...] + dot(pairs, features, TN)
    single_weight = dot(queries, features, TN)
    for h in range(HEADS):
        weight_ref[h, :HD] = single_weight[h * HD : (h + 1) * HD]
        weight_ref[h, HD:] = pair_weight[h * PAIR : (h + 1) * PAIR]
    base = norm_ref[...] + dot(pairs, pair_ref[...]) + dot(queries, single_ref[...])
    base = base.reshape(HEADS, BLOCK, WIDE)
    feature_ref[:, SHARED:] = base[:, SHARED:].astype(jnp.bfloat16)
    for copy in final:
        copy.wait_recv()
    for h in range(HEADS):
        rows = slice(h * part, (h + 1) * part)
        feature_ref[:, rows] = (base[:, rows] + quarters[h].astype(jnp.float32)).astype(jnp.bfloat16)
    for copy in sent:
        copy.wait_send()


def give_back(grads, dq, shared, features, norm_grad, in_weight, asks, node_count):
    planes, group = torus(node_count)
    part = PART
    wide = 2 * BLOCK
    columns = in_weight.T.reshape(HEADS, 3 * HD, wide)
    pair = columns[:, HD:].reshape(HEADS * PAIR, wide)
    single = columns[:, :HD].reshape(HEADS * HD, wide)
    dma = lambda *shape: pltpu.SemaphoreType.DMA(shape)
    vmem = pl.BlockSpec(memory_space=pltpu.VMEM)
    low = lambda *shape: pltpu.VMEM(shape, jnp.bfloat16)
    feature_grad, weight = pl.pallas_call(
        functools.partial(return_kernel, planes, group),
        out_shape=(
            jax.ShapeDtypeStruct((HEADS, BLOCK, wide), jnp.bfloat16),
            jax.ShapeDtypeStruct((HEADS, 3 * HD, wide), jnp.float32),
        ),
        in_specs=[vmem] * 7 + [pl.BlockSpec(memory_space=pltpu.SMEM)],
        out_specs=(vmem,) * 2,
        scratch_shapes=[
            low(HEADS, HEADS, BLOCK, PAIR),
            low(HEADS, HEADS, HD, PAIR),
            low(planes, HEADS, group * CAP, part, PAIR),
            low(planes, group, CAP, LUMP, wide),
            low(planes, group, CAP, LUMP, wide),
            low(planes, BLK, LUMP, wide),
            low(2, planes // 2, BLK, LUMP, wide),
            low(BLK, part, wide),
            low(BLK, BLOCK - SHARED, PAIR),
            low(HEADS, HEADS, part, wide),
            pltpu.VMEM((HEADS * PAIR, wide), jnp.float32),
            dma(3), dma(3), dma(3), dma(3), dma(3), dma(3), dma(planes, 3), dma(planes, 3),
            dma(planes, group - 1), dma(planes, group - 1),
            dma(2, planes // 2), dma(2, planes // 2), dma(3), dma(3),
        ],
        compiler_params=pltpu.CompilerParams(
            collective_id=3, has_side_effects=True, vmem_limit_bytes=56 << 20
        ),
        name="give_back",
    )(grads, dq, shared, features, norm_grad, pair, single, asks)
    return feature_grad.reshape(HEADS * BLOCK, wide), weight.reshape(HEADS * 3 * HD, wide)


def on_device(features, in_weight, out_weight, cotangent, key_slots, block_count, wanted):
    node_count = lax.axis_size("node")
    node_rows = BLK * BLOCK
    total_nodes = node_rows * node_count
    queries, table, shared, asks = fetch(features, in_weight, wanted, node_count)
    queries = queries.reshape(node_rows, PAIR)
    slots = key_slots.reshape(-1)
    wide, stat = forward(slots, block_count, queries, table)
    attended = wide[:, HD:]
    attended_rows = lax.all_to_all(attended, "head", split_axis=0, concat_axis=1, tiled=True)
    summed = features.astype(jnp.float32) + jnp.dot(
        attended_rows, out_weight, preferred_element_type=jnp.float32
    )
    root_mean = jnp.sqrt(jnp.mean(summed * summed, axis=-1, keepdims=True) + 1e-06)
    normed = summed / root_mean
    output = normed.astype(jnp.bfloat16)
    upstream = cotangent.astype(jnp.float32)
    norm_grad = (
        upstream - normed * jnp.mean(upstream * normed, axis=-1, keepdims=True)
    ) / root_mean
    norm_grad_low = norm_grad.astype(jnp.bfloat16)
    out_weight_grad = jnp.dot(attended_rows.T, norm_grad_low, preferred_element_type=jnp.float32)
    attended_grad = jnp.dot(norm_grad_low, out_weight.T, preferred_element_type=jnp.float32).astype(
        jnp.bfloat16
    )
    attended_grad = lax.all_to_all(attended_grad, "head", split_axis=1, concat_axis=0, tiled=True)
    both = jnp.concatenate([queries[:, :HD], attended_grad], axis=1)
    dq, grads = backward(slots, block_count, both, wide, stat, table)
    feature_grad, in_weight_grad = give_back(
        grads, dq, shared, features, norm_grad, in_weight, asks, node_count
    )
    in_weight_grad, out_weight_grad = sum_weights(in_weight_grad, out_weight_grad, node_count)
    grad_factor = total_nodes ** (-0.5)
    return (
        output,
        feature_grad,
        in_weight_grad * grad_factor,
        out_weight_grad * grad_factor,
    )


def solution(mesh):
    placed = (
        P(("node", "head"), None),
        P(),
        P(),
        P(("node", "head"), None),
        P("node", None),
        P("node"),
        P("node", None, None),
    )
    return jax.shard_map(
        on_device,
        mesh=mesh,
        in_specs=placed,
        out_specs=(
            P(("node", "head"), None),
            P(("node", "head"), None),
            P(None, "head"),
            P("head", None),
        ),
        check_vma=False,
    )
```

```python
import functools

import jax
import jax.numpy as jnp
from jax import lax
from jax.experimental import pallas as pl
from jax.experimental.pallas import tpu as pltpu
from jax.sharding import PartitionSpec as P

HEADS = 4
HD = 64
BLOCK = 128
BLK = 16
PER = 12
CAP = 2
PAIR = 2 * HD
WIDE = 2 * BLOCK
SHARED = BLOCK // 2
PART = SHARED // HEADS
LUMP = PART + (BLOCK - SHARED) // 2
SCALE = HD ** (-0.5)
NT = (((1,), (1,)), ((), ()))
TN = (((0,), (0,)), ((), ()))
MESH = pl.DeviceIdType.MESH


def dot(a, b, dims=(((1,), (0,)), ((), ()))):
    return lax.dot_general(a, b, dims, preferred_element_type=jnp.float32)


def forward_kernel(slots_ref, count_ref, q_ref, table_ref, out_ref, stat_ref):
    b = pl.program_id(0)
    count = count_ref[b]
    packed = q_ref[0]
    query = jnp.concatenate([packed[:, :HD], packed[:, HD:]], axis=0)
    query = jnp.concatenate([query, jnp.zeros_like(query)], axis=1)
    chosen = [table_ref[slots_ref[b * PER + j]] for j in range(PER)]
    scores = []
    for j in range(0, PER, 2):
        pair = dot(query, jnp.concatenate(chosen[j : j + 2], axis=0), NT)
        for i in range(2):
            dead = jnp.where(j + i < count, 0.0, -1e30)
            scores.append(pair[:, i * BLOCK : (i + 1) * BLOCK] + dead)
    highest = scores[0]
    for part in scores[1:]:
        highest = jnp.maximum(highest, part)
    highest = jnp.max(highest, axis=1, keepdims=True)
    total = jnp.zeros((BLOCK, BLOCK), jnp.float32)
    result = jnp.zeros((BLOCK, PAIR), jnp.float32)
    for j in range(0, PER, 2):
        raised = [jnp.exp(part - highest) for part in scores[j : j + 2]]
        total = total + raised[0] + raised[1]
        result = result + dot(
            jnp.concatenate([x.astype(jnp.bfloat16) for x in raised], axis=1),
            jnp.concatenate(chosen[j : j + 2], axis=0),
        )
    total = jnp.sum(total, axis=1, keepdims=True)
    out_ref[...] = (result / total).astype(jnp.bfloat16)
    lane = lax.broadcasted_iota(jnp.int32, stat_ref.shape, 1)
    stat_ref[...] = jnp.where(lane < HD, highest, 1.0 / total)


def forward(slots, count, query, table):
    rows = BLK * BLOCK
    grid_spec = pltpu.PrefetchScalarGridSpec(
        num_scalar_prefetch=2,
        grid=(BLK,),
        in_specs=[
            pl.BlockSpec((1, HD, PAIR), lambda b, *_: (b, 0, 0)),
            pl.BlockSpec(table.shape, lambda b, *_: (0, 0, 0)),
        ],
        out_specs=[
            pl.BlockSpec((BLOCK, PAIR), lambda b, *_: (b, 0)),
            pl.BlockSpec((BLOCK, PAIR), lambda b, *_: (b, 0)),
        ],
    )
    return pl.pallas_call(
        forward_kernel,
        grid_spec=grid_spec,
        out_shape=(
            jax.ShapeDtypeStruct((rows, PAIR), jnp.bfloat16),
            jax.ShapeDtypeStruct((rows, PAIR), jnp.float32),
        ),
        compiler_params=pltpu.CompilerParams(vmem_limit_bytes=40 << 20),
        cost_estimate=pl.CostEstimate(
            flops=4 * BLK * PER * BLOCK**3, bytes_accessed=8 << 20, transcendentals=BLK * PER * BLOCK**2
        ),
        name="attend",
    )(slots, count, query, table)


def backward_kernel(
    slots_ref, count_ref, q_ref, grad_ref, att_ref, stat_ref, table_ref, dq_ref, grads_ref, acc_ref, keys_ref, terms_ref
):
    b = pl.program_id(0)

    @pl.when(b == 0)
    def _():
        acc_ref[...] = jnp.zeros_like(acc_ref)

    count = count_ref[b]
    packed = q_ref[0]
    query = jnp.concatenate([packed[:, :HD], packed[:, HD:]], axis=0)
    both = jnp.concatenate([query, grad_ref[...]], axis=1)
    lane = lax.broadcasted_iota(jnp.int32, both.shape, 1)
    zero = jnp.zeros_like(both)
    stacked = jnp.concatenate(
        [jnp.where(lane < HD, both, zero), jnp.where(lane < HD, zero, both)], axis=0
    )
    dots = jnp.sum(
        jnp.where(lane < HD, 0.0, both.astype(jnp.float32) * att_ref[...].astype(jnp.float32)),
        axis=1,
        keepdims=True,
    )
    flipped = jnp.where((lane >= 32) & (lane < HD), dots, stat_ref[...]).T
    highest, dots, inverse = flipped[0:1], flipped[32:33], flipped[HD : HD + 1]
    slots = [slots_ref[b * PER + j] for j in range(PER)]
    for j in range(PER):
        keys_ref[j * BLOCK : (j + 1) * BLOCK] = table_ref[slots[j]]
    for j in range(0, PER, 2):
        products = dot(keys_ref[j * BLOCK : (j + 2) * BLOCK], stacked, NT)
        for i in range(2):
            rows = slice(i * BLOCK, (i + 1) * BLOCK)
            top = highest + jnp.where(j + i < count, 0.0, 1e30)
            attention = jnp.exp(products[rows, :BLOCK] - top) * inverse
            score_grad = attention * (products[rows, BLOCK:] - dots)
            terms_ref[(j + i) * BLOCK : (j + i + 1) * BLOCK] = jnp.concatenate(
                [score_grad.astype(jnp.bfloat16), attention.astype(jnp.bfloat16)], axis=1
            )
    dq = dot(keys_ref[...], terms_ref[:, :BLOCK], TN)
    for j in range(0, PER, 2):
        grads = dot(terms_ref[j * BLOCK : (j + 2) * BLOCK], stacked)
        for i in range(2):
            acc_ref[slots[j + i]] += grads[i * BLOCK : (i + 1) * BLOCK]
    dq = (dq.T * SCALE).astype(jnp.bfloat16)
    dq_ref[0] = jnp.concatenate([dq[:HD, :HD], dq[HD:, :HD]], axis=1)

    @pl.when(b == pl.num_programs(0) - 1)
    def _():
        grads_ref[...] = acc_ref[...].astype(jnp.bfloat16)


def backward(slots, count, query, grad, attended, stat, table):
    whole = lambda shape: pl.BlockSpec(shape, lambda b, *_: (0,) * len(shape))
    packed = pl.BlockSpec((1, HD, PAIR), lambda b, *_: (b, 0, 0))
    rowwise = pl.BlockSpec((BLOCK, PAIR), lambda b, *_: (b, 0))
    grid_spec = pltpu.PrefetchScalarGridSpec(
        num_scalar_prefetch=2,
        grid=(BLK,),
        in_specs=[
            packed, pl.BlockSpec((BLOCK, HD), lambda b, *_: (b, 0)), rowwise, rowwise, whole(table.shape)
        ],
        out_specs=[packed, whole(table.shape)],
        scratch_shapes=[
            pltpu.VMEM(table.shape, jnp.float32),
            pltpu.VMEM((PER * BLOCK, PAIR), jnp.bfloat16),
            pltpu.VMEM((PER * BLOCK, 2 * BLOCK), jnp.bfloat16),
        ],
    )
    return pl.pallas_call(
        backward_kernel,
        grid_spec=grid_spec,
        out_shape=(
            jax.ShapeDtypeStruct((BLK, HD, PAIR), jnp.bfloat16),
            jax.ShapeDtypeStruct(table.shape, jnp.bfloat16),
        ),
        compiler_params=pltpu.CompilerParams(vmem_limit_bytes=56 << 20),
        cost_estimate=pl.CostEstimate(
            flops=10 * BLK * PER * BLOCK**3, bytes_accessed=16 << 20, transcendentals=BLK * PER * BLOCK**2
        ),
        name="attend_back",
    )(slots, count, query, grad, attended, stat, table)


def torus(node_count):
    rows = 4 if node_count >= 64 else 2
    return node_count // (2 * rows), rows * 2


def ring_order(planes):
    half = planes // 2
    return [0] + [s * k for k in range(1, half) for s in (-1, 1)] + [half]


def quarter(h):
    return pl.ds(pl.multiple_of(h * PART, PART), PART)


def remote(source, target, send, recv, peer):
    return pltpu.make_async_remote_copy(
        source, target, send, recv, device_id=peer, device_id_type=MESH
    )


def neighbours(planes, group):
    node, head = lax.axis_index("node"), lax.axis_index("head")
    z, g = node // group, node % group
    x_peers = [(node, (head + d) % HEADS) for d in range(1, HEADS)]
    g_peers = [(z * group + (g + d) % group, head) for d in range(1, group)]
    right = (((z + 1) % planes) * group + g, head)
    left = (((z + planes - 1) % planes) * group + g, head)
    return head, z, g, x_peers, g_peers, right, left


def greet(peers):
    barrier = pltpu.get_barrier_semaphore()
    for peer in peers:
        pl.semaphore_signal(barrier, inc=1, device_id=peer, device_id_type=MESH)
    return lambda: pl.semaphore_wait(barrier, len(peers))


def fetch_kernel(
    planes, group, own_ref, asked_ref, weight_ref, query_ref, table_ref, shared_ref, asks_ref,
    pairs, my_pairs, my_queries, ring_a, ring_b, chunk_a, chunk_b, picked_a, picked_b, landed, made, asks,
    o_send, o_recv, q_send, q_recv, ra_send, ra_recv, rb_send, rb_recv,
    ga_send, ga_recv, gb_send, gb_recv, x_send, x_recv, asks_sem,
):
    head, z, g, x_peers, g_peers, right, left = neighbours(planes, group)
    half = planes // 2
    width = group * CAP
    rows = HEADS * BLOCK
    late = pl.ds(SHARED, BLOCK - SHARED)
    own_blocks = pl.ds(head * HEADS, HEADS)
    arrive = greet(x_peers + g_peers + [right, left])

    ring_a[z, own_blocks] = own_ref[:, quarter(head)]
    weight = weight_ref[...]
    step = 3 * HD
    for h in range(HEADS):
        pairs[:, h * PAIR : (h + 1) * PAIR] = weight[:, h * step + HD : (h + 1) * step]
    own = own_ref[...].reshape(rows, WIDE)
    for h in range(HEADS):
        both = dot(own, pairs[:, h * PAIR : (h + 1) * PAIR]).astype(jnp.bfloat16)
        my_pairs[h] = both.reshape(HEADS, BLOCK, PAIR)
        queries = (dot(own, weight[:, h * step : h * step + HD]) * SCALE).astype(jnp.bfloat16)
        queries = queries.reshape(HEADS, BLOCK, HD)
        my_queries[h] = jnp.concatenate([queries[:, :HD], queries[:, HD:]], axis=2)
    arrive()

    def own_copies(kind, source, target):
        return [
            remote(source(peer[1]), target, o_send.at[kind, d], o_recv.at[kind, d], peer)
            for d, peer in enumerate(x_peers)
        ]

    early = pl.ds(0, SHARED)
    corner = own_copies(0, lambda h: own_ref.at[:, quarter(h)], ring_a.at[z, own_blocks])
    lower = own_copies(1, lambda h: my_pairs.at[h, :, late], table_ref.at[own_blocks, late])
    upper = own_copies(2, lambda h: my_pairs.at[h, :, early], table_ref.at[own_blocks, early])
    asking = own_copies(3, lambda h: my_queries.at[h], query_ref.at[own_blocks])
    questions = [
        remote(asked_ref.at[peer[0] % group], asks_ref.at[g], q_send.at[d], q_recv.at[d], peer)
        for d, peer in enumerate(g_peers)
    ]
    sent = []

    def begin(copies):
        for copy in copies:
            copy.start()
            sent.append(copy)

    begin(corner + questions + lower + upper + asking)
    table_ref[own_blocks] = my_pairs[head]
    query_ref[own_blocks] = my_queries[head]
    asks_ref[g] = asked_ref[g]

    def hop(ring, send, recv, way, k):
        at = (z - k + planes) % planes if way == 0 else (z + k) % planes
        view = ring.at[at]
        if k == half - 1:
            view = view.at[pl.ds(way * (BLK // 2), BLK // 2)]
        return remote(view, view, send.at[way, k], recv.at[way, k], left if way else right)

    def hops(ring, send, recv):
        return {(way, k): hop(ring, send, recv, way, k) for way in range(2) for k in range(half)}

    hops_a = hops(ring_a, ra_send, ra_recv)
    hops_b = hops(ring_b, rb_send, rb_recv)
    order = ring_order(planes)
    place = lambda t: (z + order[t] + planes) % planes

    def bring(hops, t):
        offset = order[t]
        if offset == 0:
            begin([hops[0, 0], hops[1, 0]])
        elif offset == half:
            hops[0, half - 1].wait_recv()
            hops[1, half - 1].wait_recv()
        else:
            way, k = (0, -offset) if offset < 0 else (1, offset)
            hops[way, k - 1].wait_recv()
            begin([hops[way, k]])

    def spot(at, owner):
        return pl.ds(BLK + (at * group + owner) * CAP, CAP)

    def copies_a(at):
        return [
            remote(picked_a.at[at, d], landed.at[at, g], ga_send.at[at, d], ga_recv.at[at, d], peer)
            for d, peer in enumerate(g_peers)
        ]

    def copies_b(at):
        return [
            remote(
                picked_b.at[at, d], table_ref.at[spot(at, g), late], gb_send.at[at, d], gb_recv.at[at, d], peer
            )
            for d, peer in enumerate(g_peers)
        ]

    def bring_a(t):
        at = place(t)
        bring(hops_a, t)
        chunk_a[...] = ring_a[at]
        copies = copies_a(at)
        for d, peer in enumerate(g_peers):
            for c in range(CAP):
                picked_a[at, d, c] = chunk_a[asks[peer[0] % group, 0, at * CAP + c]]
            begin([copies[d]])
        for c in range(CAP):
            landed[at, g, c] = chunk_a[asks[g, 0, at * CAP + c]]

    def bring_b(t):
        at = place(t)
        bring(hops_b, t)
        chunk_b[...] = ring_b[at]
        copies = copies_b(at)
        for d, peer in enumerate(g_peers):
            for c in range(CAP):
                picked_b[at, d, c] = chunk_b[asks[peer[0] % group, 0, at * CAP + c]]
            begin([copies[d]])
        for c in range(CAP):
            table_ref[BLK + (at * group + g) * CAP + c, SHARED:] = chunk_b[asks[g, 0, at * CAP + c]]

    arriving = []

    def make(t):
        at = place(t)
        for copy in copies_a(at):
            copy.wait_recv()
        shared = landed[at].reshape(width * PART, WIDE)
        shared_ref[at] = shared
        both = dot(shared, pairs[...]).astype(jnp.bfloat16)
        for h in range(HEADS):
            made[at, h] = both[:, h * PAIR : (h + 1) * PAIR].reshape(width, PART, PAIR)
        slots = pl.ds(BLK + at * width, width)
        copies = [
            remote(
                made.at[at, peer[1]], table_ref.at[slots, quarter(head)], x_send.at[at, d], x_recv.at[at, d],
                peer,
            )
            for d, peer in enumerate(x_peers)
        ]
        begin(copies)
        arriving.extend(copies)
        table_ref[slots, quarter(head)] = made[at, head]

    for copy in corner:
        copy.wait_recv()
    for copy in questions:
        copy.wait_recv()
    answer = pltpu.make_async_copy(asks_ref, asks, asks_sem)
    answer.start()
    answer.wait()
    bring_a(0)
    for copy in lower:
        copy.wait_recv()
    ring_b[z] = table_ref[:BLK, SHARED:]
    bring_b(0)
    pairs_of = [[t, t + 1] for t in range(1, planes - 1, 2)] + [[planes - 1]]
    before = [0]
    for now in pairs_of:
        for t in now:
            bring_a(t)
        for t in before:
            make(t)
        for t in now:
            bring_b(t)
        before = now
    for t in before:
        make(t)
    for copy in upper + asking + arriving:
        copy.wait_recv()
    for t in range(planes):
        for copy in copies_b(place(t)):
            copy.wait_recv()
    for copy in sent:
        copy.wait_send()


def fetch(features, in_weight, wanted, node_count):
    planes, group = torus(node_count)
    own = features.reshape(HEADS, BLOCK, WIDE)
    asked = wanted.reshape(planes, group, CAP).transpose(1, 0, 2).reshape(group, 1, planes * CAP)
    asked = jnp.pad(asked, ((0, 0), (0, 7), (0, 128 - planes * CAP)))
    dma = lambda *shape: pltpu.SemaphoreType.DMA(shape)
    vmem = pl.BlockSpec(memory_space=pltpu.VMEM)
    low = lambda *shape: pltpu.VMEM(shape, jnp.bfloat16)
    late = BLOCK - SHARED
    slots = BLK + planes * group * CAP
    return pl.pallas_call(
        functools.partial(fetch_kernel, planes, group),
        out_shape=(
            jax.ShapeDtypeStruct((BLK, HD, PAIR), jnp.bfloat16),
            jax.ShapeDtypeStruct((slots, BLOCK, PAIR), jnp.bfloat16),
            jax.ShapeDtypeStruct((planes, group * CAP * PART, WIDE), jnp.bfloat16),
            jax.ShapeDtypeStruct((group, 8, 128), jnp.int32),
        ),
        in_specs=[vmem] * 3,
        out_specs=(vmem,) * 4,
        scratch_shapes=[
            low(WIDE, HEADS * PAIR),
            low(HEADS, HEADS, BLOCK, PAIR),
            low(HEADS, HEADS, HD, PAIR),
            low(planes, BLK, PART, WIDE),
            low(planes, BLK, late, PAIR),
            low(BLK, PART, WIDE),
            low(BLK, late, PAIR),
            low(planes, group - 1, CAP, PART, WIDE),
            low(planes, group - 1, CAP, late, PAIR),
            low(planes, group, CAP, PART, WIDE),
            low(planes, HEADS, group * CAP, PART, PAIR),
            pltpu.SMEM((group, 8, 128), jnp.int32),
            dma(4, 3), dma(4, 3), dma(group - 1), dma(group - 1),
            dma(2, planes // 2), dma(2, planes // 2), dma(2, planes // 2), dma(2, planes // 2),
            dma(planes, group - 1), dma(planes, group - 1), dma(planes, group - 1), dma(planes, group - 1),
            dma(planes, 3), dma(planes, 3),
            pltpu.SemaphoreType.DMA,
        ],
        compiler_params=pltpu.CompilerParams(
            collective_id=2, has_side_effects=True, vmem_limit_bytes=48 << 20
        ),
        name="fetch",
    )(own, asked, in_weight)


def return_kernel(
    planes, group, grads_ref, dq_ref, shared_ref, features_ref, norm_ref, weight_ref, out_ref, asks_ref,
    feature_ref, sum_ref,
    pairs, singles, own_pairs, own_queries, heads, leaving, answers_a, answers_b, partial_a, partial_b,
    ring_a, ring_b, summed, late_sums, quarters, acc, base,
    out_mine, out_in, in_mine, in_in, x_sum, g_in, g_sum, z_in, piece,
    o_send, o_recv, x_send, x_recv, ga_send, ga_recv, gb_send, gb_recv, ra_send, ra_recv, rb_send, rb_recv,
    wg_send, wg_recv, wz_send, wz_recv, bz_send, bz_recv, bg_send, bg_recv,
):
    head, z, g, x_peers, g_peers, right, left = neighbours(planes, group)
    z_peers = [(((z + d) % planes) * group + g, head) for d in range(1, planes)]
    half = planes // 2
    width = group * CAP
    low = BLOCK - SHARED
    early, late = pl.ds(0, SHARED), pl.ds(SHARED, low)
    own_blocks = pl.ds(head * HEADS, HEADS)
    arrive = greet(x_peers + g_peers + z_peers)

    weight = weight_ref[...]
    step = 3 * HD
    for h in range(HEADS):
        pairs[:, h * PAIR : (h + 1) * PAIR] = weight[:, h * step + HD : (h + 1) * step]
    singles[...] = jnp.concatenate(
        [weight[:, h * step : h * step + HD] for h in range(HEADS)], axis=1
    )
    for h in range(HEADS):
        some = out_ref[h * HD : (h + 1) * HD]
        out_mine[h] = jnp.concatenate([some[:, :BLOCK], some[:, BLOCK:]], axis=0)
    arrive()

    order = list(reversed(ring_order(planes)))
    places = [(z + offset + planes) % planes for offset in order]
    spot = lambda at, owner: pl.ds(BLK + (at * group + owner) * CAP, CAP)
    slots = lambda at: pl.ds(BLK + at * width, width)
    sent = []

    def begin(copies):
        for copy in copies:
            copy.start()
            sent.append(copy)

    def to_heads(kind, source, target):
        return [
            remote(source(peer[1]), target, o_send.at[kind, d], o_recv.at[kind, d], peer)
            for d, peer in enumerate(x_peers)
        ]

    blocks_of = lambda h: pl.ds(h * HEADS, HEADS)
    own = to_heads(0, lambda h: grads_ref.at[blocks_of(h), early], own_pairs.at[head, :, early])
    own += to_heads(1, lambda h: dq_ref.at[blocks_of(h)], own_queries.at[head])
    out_copies = to_heads(2, lambda h: out_mine.at[h], out_in.at[head])
    far = [
        [
            remote(
                grads_ref.at[slots(at), quarter(peer[1])], heads.at[at, head],
                x_send.at[at, d], x_recv.at[at, d], peer,
            )
            for d, peer in enumerate(x_peers)
        ]
        for at in places
    ]
    far_late = [
        [
            remote(
                grads_ref.at[spot(at, peer[0] % group), late], answers_b.at[at, g],
                gb_send.at[at, d], gb_recv.at[at, d], peer,
            )
            for d, peer in enumerate(g_peers)
        ]
        for at in places
    ]
    ahead = 3
    for t in range(min(ahead, planes)):
        begin(far[t])
        begin(far_late[t])
    acc[...] = jnp.zeros_like(acc)
    own_pairs[head, :, :SHARED] = grads_ref[own_blocks, :SHARED]
    own_queries[head] = dq_ref[own_blocks]

    def spread(t):
        at = places[t]
        heads[at, head] = grads_ref[slots(at), quarter(head)]
        for copy in far[t]:
            copy.wait_recv()
        if t + ahead < planes:
            begin(far[t + ahead])
            begin(far_late[t + ahead])
        if t + ahead == planes - 1:
            begin(own + out_copies)
        some = jnp.concatenate([heads[at, h].reshape(width * PART, PAIR) for h in range(HEADS)], axis=1)
        back = dot(some, pairs[...], NT).astype(jnp.bfloat16)
        leaving[at] = back.reshape(group, CAP, PART, WIDE)
        copies = [
            remote(
                leaving.at[at, peer[0] % group], answers_a.at[at, g], ga_send.at[at, d], ga_recv.at[at, d], peer
            )
            for d, peer in enumerate(g_peers)
        ]
        begin(copies)
        answers_a[at, g] = leaving[at, g]
        acc[...] += dot(some, shared_ref[at], TN)
        return copies

    def choose(t):
        at = places[t]
        side = width * PART
        column = lax.broadcasted_iota(jnp.int32, (1, side), 1)
        target = column % PART
        for j in range(width):
            block = asks_ref[j // CAP, 0, at * CAP + j % CAP]
            target = target + jnp.where(column // PART == j, block * PART, 0)
        row = lax.broadcasted_iota(jnp.int32, (BLK * PART, side), 0)
        return jnp.where(row == target, 1.0, 0.0).astype(jnp.bfloat16)

    def pass_on(t, total, partial, ring, send, recv):
        at, offset = places[t], order[t]
        mid = BLK // 2

        def hop(way, k):
            source, target = partial.at[at], ring.at[way, k]
            if k == 0:
                blocks = pl.ds(way * mid, mid)
                source, target = source.at[blocks], target.at[blocks]
            return remote(source, target, send.at[way, k], recv.at[way, k], left if way else right)

        if offset == half:
            partial[at] = total.astype(jnp.bfloat16)
            begin([hop(0, 0), hop(1, 0)])
            return None
        k = half - 1 - abs(offset)
        ways = [0] if offset > 0 else [1] if offset < 0 else [0, 1]
        for way in ways:
            hop(way, k).wait_recv()
            if k:
                total = total + ring[way, k].astype(jnp.float32)
            elif way:
                total = jnp.concatenate([total[:mid], total[mid:] + ring[way, k, mid:].astype(jnp.float32)], axis=0)
            else:
                total = jnp.concatenate([total[:mid] + ring[way, k, :mid].astype(jnp.float32), total[mid:]], axis=0)
        if offset:
            partial[at] = total.astype(jnp.bfloat16)
            begin([hop(ways[0], k + 1)])
            return None
        return total

    def gather_late(t, chosen):
        at = places[t]
        for copy in far_late[t]:
            copy.wait_recv()
        answers_b[at, g] = grads_ref[spot(at, g), SHARED:]
        total = [
            dot(chosen, answers_b[at, :, :, i * PART : (i + 1) * PART].reshape(width * PART, PAIR))
            for i in range(low // PART)
        ]
        total = jnp.concatenate([x.reshape(BLK, PART, PAIR) for x in total], axis=1)
        return pass_on(t, total, partial_b, ring_b, rb_send, rb_recv)

    def gather(t, chosen, copies):
        for copy in copies:
            copy.wait_recv()
        total = dot(chosen, answers_a[places[t]].reshape(width * PART, WIDE)).reshape(BLK, PART, WIDE)
        return pass_on(t, total, partial_a, ring_a, ra_send, ra_recv)

    before = None
    for t in range(planes):
        copies = spread(t)
        chosen = choose(t)
        if t == planes - 1:
            for copy in own:
                copy.wait_recv()
            some = jnp.concatenate(
                [own_pairs[h, :, :SHARED].reshape(HEADS * SHARED, PAIR) for h in range(HEADS)], axis=1
            )
            queries = jnp.concatenate(
                [
                    jnp.concatenate(
                        [own_queries[h, :, :, :HD], own_queries[h, :, :, HD:]], axis=1
                    ).reshape(HEADS * BLOCK, HD)
                    for h in range(HEADS)
                ],
                axis=1,
            )
            everything = features_ref[...].reshape(HEADS * BLOCK, WIDE)
            acc[...] += dot(some, features_ref[:, :SHARED].reshape(HEADS * SHARED, WIDE), TN)
            single_weight = dot(queries, everything, TN)
            base[...] = (norm_ref[...] + dot(queries, singles[...], NT)).reshape(HEADS, BLOCK, WIDE)
            base[:, :SHARED] += dot(some, pairs[...], NT).reshape(HEADS, SHARED, WIDE)
        total = gather_late(t, chosen)
        if t == planes - 1:
            late_sums[...] = (grads_ref[:BLK, SHARED:].astype(jnp.float32) + total).astype(jnp.bfloat16)
            tail = to_heads(3, lambda h: late_sums.at[blocks_of(h)], own_pairs.at[head, :, late])
            begin(tail)
            own_pairs[head, :, SHARED:] = late_sums[own_blocks]
        if t:
            gather(t - 1, *before)
        before = (chosen, copies)
    summed[...] = gather(planes - 1, *before).astype(jnp.bfloat16)
    final = to_heads(4, lambda h: summed.at[blocks_of(h)], quarters.at[head])
    begin(final)
    quarters[head] = summed[own_blocks]

    for copy in tail:
        copy.wait_recv()
    some = jnp.concatenate(
        [own_pairs[h, :, SHARED:].reshape(HEADS * low, PAIR) for h in range(HEADS)], axis=1
    )
    pair_weight = acc[...] + dot(some, features_ref[:, SHARED:].reshape(HEADS * low, WIDE), TN)
    for h in range(HEADS):
        terms = jnp.concatenate(
            [single_weight[h * HD : (h + 1) * HD], pair_weight[h * PAIR : (h + 1) * PAIR]], axis=0
        )
        terms = jnp.concatenate([terms[:, :BLOCK], terms[:, BLOCK:]], axis=0)
        in_mine[h] = terms.astype(jnp.bfloat16)
        if h == 0:
            in_own = jnp.where(head == 0, terms, 0.0)
        else:
            in_own = in_own + jnp.where(head == h, terms, 0.0)
    in_low = to_heads(5, lambda h: in_mine.at[h], in_in.at[head])
    begin(in_low)

    base[:, SHARED:] += dot(some, pairs[...], NT).reshape(HEADS, low, WIDE)
    feature_ref[:, SHARED:] = base[:, SHARED:].astype(jnp.bfloat16)
    for copy in final:
        copy.wait_recv()
    for h in range(HEADS):
        rows = slice(h * PART, (h + 1) * PART)
        feature_ref[:, rows] = (base[:, rows] + quarters[h].astype(jnp.float32)).astype(jnp.bfloat16)

    def exchange(peers, source, target, send, recv):
        copies = [
            remote(source(d, peer), target(d), send.at[d], recv.at[d], peer) for d, peer in enumerate(peers)
        ]
        begin(copies)
        return copies

    for copy in out_copies + in_low:
        copy.wait_recv()
    out_in[head] = out_mine[head]
    in_total = in_own
    for _, h in x_peers:
        in_total = in_total + in_in[h].astype(jnp.float32)
    out_total = out_in[0] + out_in[1] + out_in[2] + out_in[3]
    x_sum[...] = jnp.concatenate([in_total, out_total], axis=0).reshape(x_sum.shape)
    for copy in exchange(
        g_peers, lambda d, peer: x_sum.at[peer[0] % group], lambda d: g_in.at[d], wg_send, wg_recv
    ):
        copy.wait_recv()
    total = x_sum[g]
    for d in range(group - 1):
        total = total + g_in[d]
    g_sum[...] = total
    for copy in exchange(
        z_peers, lambda d, peer: g_sum.at[peer[0] // group], lambda d: z_in.at[d], wz_send, wz_recv
    ):
        copy.wait_recv()
    total = g_sum[z]
    for d in range(planes - 1):
        total = total + z_in[d]
    piece[...] = total
    sum_ref[g, z] = total
    for copy in exchange(z_peers, lambda d, peer: piece, lambda d: sum_ref.at[g, z], bz_send, bz_recv):
        copy.wait_recv()
    for copy in exchange(g_peers, lambda d, peer: sum_ref.at[g], lambda d: sum_ref.at[g], bg_send, bg_recv):
        copy.wait_recv()
    for copy in sent:
        copy.wait_send()


def give_back(grads, dq, shared, features, norm_grad, in_weight, out_grad, asks, node_count):
    planes, group = torus(node_count)
    rows = 4 * HD * 2 // (planes * group)
    late = BLOCK - SHARED
    dma = lambda *shape: pltpu.SemaphoreType.DMA(shape)
    vmem = pl.BlockSpec(memory_space=pltpu.VMEM)
    low = lambda *shape: pltpu.VMEM(shape, jnp.bfloat16)
    high = lambda *shape: pltpu.VMEM(shape, jnp.float32)
    both = lambda *shape: [dma(*shape)] * 2
    feature_grad, total = pl.pallas_call(
        functools.partial(return_kernel, planes, group),
        out_shape=(
            jax.ShapeDtypeStruct((HEADS, BLOCK, WIDE), jnp.bfloat16),
            jax.ShapeDtypeStruct((group, planes, rows, 128), jnp.float32),
        ),
        in_specs=[vmem] * 7 + [pl.BlockSpec(memory_space=pltpu.SMEM)],
        out_specs=(vmem,) * 2,
        scratch_shapes=[
            low(WIDE, HEADS * PAIR),
            low(WIDE, HEADS * HD),
            low(HEADS, HEADS, BLOCK, PAIR),
            low(HEADS, HEADS, HD, PAIR),
            low(planes, HEADS, group * CAP, PART, PAIR),
            low(planes, group, CAP, PART, WIDE),
            low(planes, group, CAP, PART, WIDE),
            low(planes, group, CAP, late, PAIR),
            low(planes, BLK, PART, WIDE),
            low(planes, BLK, late, PAIR),
            low(2, planes // 2, BLK, PART, WIDE),
            low(2, planes // 2, BLK, late, PAIR),
            low(BLK, PART, WIDE),
            low(BLK, late, PAIR),
            low(HEADS, HEADS, PART, WIDE),
            high(HEADS * PAIR, WIDE),
            high(HEADS, BLOCK, WIDE),
            high(HEADS, 2 * HD, 128),
            high(HEADS, 2 * HD, 128),
            low(HEADS, 6 * HD, 128),
            low(HEADS, 6 * HD, 128),
            high(group, planes, rows, 128),
            high(group - 1, planes, rows, 128),
            high(planes, rows, 128),
            high(planes - 1, rows, 128),
            high(rows, 128),
            *both(6, 3), *both(planes, 3), *both(planes, group - 1), *both(planes, group - 1),
            *both(2, planes // 2), *both(2, planes // 2),
            *both(group - 1), *both(planes - 1), *both(planes - 1), *both(group - 1),
        ],
        compiler_params=pltpu.CompilerParams(
            collective_id=3, has_side_effects=True, vmem_limit_bytes=56 << 20
        ),
        name="give_back",
    )(grads, dq, shared, features.reshape(HEADS, BLOCK, WIDE), norm_grad, in_weight, out_grad, asks)
    total = total.reshape(4 * HD * 2, 128)
    in_total, out_total = total[: 6 * HD], total[6 * HD :]
    in_total = jnp.concatenate([in_total[: 3 * HD], in_total[3 * HD :]], axis=1)
    out_total = jnp.concatenate([out_total[:HD], out_total[HD:]], axis=1)
    return feature_grad.reshape(HEADS * BLOCK, WIDE), in_total.T, out_total


def on_device(features, in_weight, out_weight, cotangent, key_slots, block_count, wanted):
    node_count = lax.axis_size("node")
    node_rows = BLK * BLOCK
    total_nodes = node_rows * node_count
    queries, table, shared, asks = fetch(features, in_weight, wanted, node_count)
    slots = key_slots.reshape(-1)
    wide, stat = forward(slots, block_count, queries, table)
    attended = wide[:, HD:]
    attended_rows = lax.all_to_all(attended, "head", split_axis=0, concat_axis=1, tiled=True)
    summed = features.astype(jnp.float32) + jnp.dot(
        attended_rows, out_weight, preferred_element_type=jnp.float32
    )
    root_mean = jnp.sqrt(jnp.mean(summed * summed, axis=-1, keepdims=True) + 1e-06)
    normed = summed / root_mean
    output = normed.astype(jnp.bfloat16)
    upstream = cotangent.astype(jnp.float32)
    norm_grad = (
        upstream - normed * jnp.mean(upstream * normed, axis=-1, keepdims=True)
    ) / root_mean
    norm_grad_low = norm_grad.astype(jnp.bfloat16)
    out_weight_grad = jnp.dot(attended_rows.T, norm_grad_low, preferred_element_type=jnp.float32)
    attended_grad = jnp.dot(norm_grad_low, out_weight.T, preferred_element_type=jnp.float32).astype(
        jnp.bfloat16
    )
    attended_grad = lax.all_to_all(attended_grad, "head", split_axis=1, concat_axis=0, tiled=True)
    dq, grads = backward(slots, block_count, queries, attended_grad, wide, stat, table)
    feature_grad, in_weight_grad, out_weight_grad = give_back(
        grads, dq, shared, features, norm_grad, in_weight, out_weight_grad, asks, node_count
    )
    grad_factor = total_nodes ** (-0.5)
    return (
        output,
        feature_grad,
        in_weight_grad * grad_factor,
        out_weight_grad * grad_factor,
    )


def solution(mesh):
    placed = (
        P(("node", "head"), None),
        P(),
        P(),
        P(("node", "head"), None),
        P("node", None),
        P("node"),
        P("node", None, None),
    )
    return jax.shard_map(
        on_device,
        mesh=mesh,
        in_specs=placed,
        out_specs=(
            P(("node", "head"), None),
            P(("node", "head"), None),
            P(None, "head"),
            P("head", None),
        ),
        check_vma=False,
    )
```

```python
import functools

import jax
import jax.numpy as jnp
from jax import lax
from jax.experimental import pallas as pl
from jax.experimental.pallas import tpu as pltpu
from jax.sharding import PartitionSpec as P

HEADS = 4
HD = 64
BLOCK = 128
BLK = 16
PER = 12
CAP = 2
PAIR = 2 * HD
PAIRED = 2
WIDE = 2 * BLOCK
SHARED = BLOCK // 2
PART = SHARED // HEADS
LUMP = PART + (BLOCK - SHARED) // 2
SCALE = HD ** (-0.5)
NT = (((1,), (1,)), ((), ()))
TN = (((0,), (0,)), ((), ()))
MESH = pl.DeviceIdType.MESH


def dot(a, b, dims=(((1,), (0,)), ((), ()))):
    return lax.dot_general(a, b, dims, preferred_element_type=jnp.float32)


def unpack(packed):
    return jnp.concatenate([packed[..., :HD], packed[..., HD:]], axis=-2)


def pack(rows):
    return jnp.concatenate([rows[..., :HD, :], rows[..., HD:, :]], axis=-1)


def attend(query, chosen, count):
    query = jnp.concatenate([query, jnp.zeros_like(query)], axis=1)
    scores = []
    for j in range(0, PER, 2):
        pair = dot(query, jnp.concatenate(chosen[j : j + 2], axis=0), NT)
        for i in range(2):
            dead = jnp.where(j + i < count, 0.0, -1e30)
            scores.append(pair[:, i * BLOCK : (i + 1) * BLOCK] + dead)
    highest = scores[0]
    for part in scores[1:]:
        highest = jnp.maximum(highest, part)
    highest = jnp.max(highest, axis=1, keepdims=True)
    total = jnp.zeros((BLOCK, BLOCK), jnp.float32)
    result = jnp.zeros((BLOCK, PAIR), jnp.float32)
    for j in range(0, PER, 2):
        raised = [jnp.exp(part - highest) for part in scores[j : j + 2]]
        total = total + raised[0] + raised[1]
        result = result + dot(
            jnp.concatenate([x.astype(jnp.bfloat16) for x in raised], axis=1),
            jnp.concatenate(chosen[j : j + 2], axis=0),
        )
    total = jnp.sum(total, axis=1, keepdims=True)
    return (result / total).astype(jnp.bfloat16), highest, total


def backward_kernel(slots_ref, count_ref, both_ref, stat_ref, table_ref, dq_ref, grads_ref, acc_ref, keys_ref, terms_ref):
    step = pl.program_id(0)

    @pl.when(step == 0)
    def _():
        acc_ref[...] = jnp.zeros_like(acc_ref)

    stacks, slots = [], []
    for i in range(PAIRED):
        b = step * PAIRED + i
        count = count_ref[b]
        both = both_ref[i]
        lane = lax.broadcasted_iota(jnp.int32, both.shape, 1)
        zero = jnp.zeros_like(both)
        stacked = jnp.concatenate(
            [jnp.where(lane < HD, both, zero), jnp.where(lane < HD, zero, both)], axis=0
        )
        stacks.append(stacked)
        highest, dots, inverse = stat_ref[i, 0:1], stat_ref[i, 1:2], stat_ref[i, 2:3]
        slots.append([slots_ref[b * PER + j] for j in range(PER)])
        for j in range(PER):
            keys_ref[i, j * BLOCK : (j + 1) * BLOCK] = table_ref[slots[i][j]]
        for j in range(0, PER, 2):
            products = dot(keys_ref[i, j * BLOCK : (j + 2) * BLOCK], stacked, NT)
            for k in range(2):
                rows = slice(k * BLOCK, (k + 1) * BLOCK)
                top = highest + jnp.where(j + k < count, 0.0, 1e30)
                attention = jnp.exp(products[rows, :BLOCK] - top) * inverse
                score_grad = attention * (products[rows, BLOCK:] - dots)
                terms_ref[i, (j + k) * BLOCK : (j + k + 1) * BLOCK] = jnp.concatenate(
                    [score_grad.astype(jnp.bfloat16), attention.astype(jnp.bfloat16)], axis=1
                )
    for i in range(PAIRED):
        dq = dot(keys_ref[i], terms_ref[i, :, :BLOCK], TN)
        dq = (dq.T * SCALE).astype(jnp.bfloat16)
        dq_ref[i] = pack(dq[:, :HD])
        for j in range(0, PER, 2):
            grads = dot(terms_ref[i, j * BLOCK : (j + 2) * BLOCK], stacks[i])
            for k in range(2):
                acc_ref[slots[i][j + k]] += grads[k * BLOCK : (k + 1) * BLOCK]

    @pl.when(step == pl.num_programs(0) - 1)
    def _():
        grads_ref[...] = acc_ref[...].astype(jnp.bfloat16)


def backward(slots, count, both, stat, table):
    whole = lambda shape: pl.BlockSpec(shape, lambda b, *_: (0,) * len(shape))
    some = lambda *shape: pl.BlockSpec((PAIRED,) + shape, lambda b, *_: (b, 0, 0))
    grid_spec = pltpu.PrefetchScalarGridSpec(
        num_scalar_prefetch=2,
        grid=(BLK // PAIRED,),
        in_specs=[some(BLOCK, PAIR), some(8, BLOCK), whole(table.shape)],
        out_specs=[some(HD, PAIR), whole(table.shape)],
        scratch_shapes=[
            pltpu.VMEM(table.shape, jnp.float32),
            pltpu.VMEM((PAIRED, PER * BLOCK, PAIR), jnp.bfloat16),
            pltpu.VMEM((PAIRED, PER * BLOCK, 2 * BLOCK), jnp.bfloat16),
        ],
    )
    return pl.pallas_call(
        backward_kernel,
        grid_spec=grid_spec,
        out_shape=(
            jax.ShapeDtypeStruct((BLK, HD, PAIR), jnp.bfloat16),
            jax.ShapeDtypeStruct(table.shape, jnp.bfloat16),
        ),
        compiler_params=pltpu.CompilerParams(vmem_limit_bytes=56 << 20),
        cost_estimate=pl.CostEstimate(
            flops=10 * BLK * PER * BLOCK**3, bytes_accessed=16 << 20, transcendentals=BLK * PER * BLOCK**2
        ),
        name="attend_back",
    )(slots, count, both, stat, table)


def torus(node_count):
    rows = 4 if node_count >= 64 else 2
    return node_count // (2 * rows), rows * 2


def ring_order(planes):
    half = planes // 2
    return [0] + [s * k for k in range(1, half) for s in (-1, 1)] + [half]


def quarter(h):
    return pl.ds(pl.multiple_of(h * PART, PART), PART)


def remote(source, target, send, recv, peer):
    return pltpu.make_async_remote_copy(
        source, target, send, recv, device_id=peer, device_id_type=MESH
    )


def neighbours(planes, group):
    node, head = lax.axis_index("node"), lax.axis_index("head")
    z, g = node // group, node % group
    x_peers = [(node, (head + d) % HEADS) for d in range(1, HEADS)]
    g_peers = [(z * group + (g + d) % group, head) for d in range(1, group)]
    right = (((z + 1) % planes) * group + g, head)
    left = (((z + planes - 1) % planes) * group + g, head)
    return head, z, g, x_peers, g_peers, right, left


def greet(peers):
    barrier = pltpu.get_barrier_semaphore()
    for peer in peers:
        pl.semaphore_signal(barrier, inc=1, device_id=peer, device_id_type=MESH)
    return lambda: pl.semaphore_wait(barrier, len(peers))


def fetch_kernel(
    planes, group, own_ref, asked_ref, weight_ref, out_weight_ref, cotangent_ref, slots_ref, count_ref,
    table_ref, shared_ref, asks_ref, both_ref, stat_ref, output_ref, norm_ref, out_grad_ref,
    query_ref, packed, highs, sums, att_in, att_rows, low_grad, my_grads, grad_in,
    pairs, my_pairs, my_queries, ring_a, ring_b, chunk_a, chunk_b, picked_a, picked_b, landed, made, asks,
    o_send, o_recv, q_send, q_recv, ra_send, ra_recv, rb_send, rb_recv,
    ga_send, ga_recv, gb_send, gb_recv, x_send, x_recv, asks_sem,
):
    head, z, g, x_peers, g_peers, right, left = neighbours(planes, group)
    half = planes // 2
    width = group * CAP
    rows = HEADS * BLOCK
    late = pl.ds(SHARED, BLOCK - SHARED)
    own_blocks = pl.ds(head * HEADS, HEADS)
    arrive = greet(x_peers + g_peers + [right, left])

    ring_a[z, own_blocks] = own_ref[:, quarter(head)]
    weight = weight_ref[...]
    step = 3 * HD
    for h in range(HEADS):
        pairs[:, h * PAIR : (h + 1) * PAIR] = weight[:, h * step + HD : (h + 1) * step]
    own = own_ref[...].reshape(rows, WIDE)
    for h in range(HEADS):
        both = dot(own, pairs[:, h * PAIR : (h + 1) * PAIR]).astype(jnp.bfloat16)
        my_pairs[h] = both.reshape(HEADS, BLOCK, PAIR)
        queries = (dot(own, weight[:, h * step : h * step + HD]) * SCALE).astype(jnp.bfloat16)
        my_queries[h] = pack(queries.reshape(HEADS, BLOCK, HD))
    arrive()

    def own_copies(kind, source, target):
        return [
            remote(source(peer[1]), target, o_send.at[kind, d], o_recv.at[kind, d], peer)
            for d, peer in enumerate(x_peers)
        ]

    early = pl.ds(0, SHARED)
    corner = own_copies(0, lambda h: own_ref.at[:, quarter(h)], ring_a.at[z, own_blocks])
    lower = own_copies(1, lambda h: my_pairs.at[h, :, late], table_ref.at[own_blocks, late])
    upper = own_copies(2, lambda h: my_pairs.at[h, :, early], table_ref.at[own_blocks, early])
    asking = own_copies(3, lambda h: my_queries.at[h], query_ref.at[own_blocks])
    questions = [
        remote(asked_ref.at[peer[0] % group], asks_ref.at[g], q_send.at[d], q_recv.at[d], peer)
        for d, peer in enumerate(g_peers)
    ]
    sent = []

    def begin(copies):
        for copy in copies:
            copy.start()
            sent.append(copy)

    begin(corner + questions + lower + upper + asking)
    table_ref[own_blocks] = my_pairs[head]
    query_ref[own_blocks] = my_queries[head]
    asks_ref[g] = asked_ref[g]

    def hop(ring, send, recv, way, k):
        at = (z - k + planes) % planes if way == 0 else (z + k) % planes
        view = ring.at[at]
        if k == half - 1:
            view = view.at[pl.ds(way * (BLK // 2), BLK // 2)]
        return remote(view, view, send.at[way, k], recv.at[way, k], left if way else right)

    def hops(ring, send, recv):
        return {(way, k): hop(ring, send, recv, way, k) for way in range(2) for k in range(half)}

    hops_a = hops(ring_a, ra_send, ra_recv)
    hops_b = hops(ring_b, rb_send, rb_recv)
    order = ring_order(planes)
    place = lambda t: (z + order[t] + planes) % planes

    def bring(hops, t):
        offset = order[t]
        if offset == 0:
            begin([hops[0, 0], hops[1, 0]])
        elif offset == half:
            hops[0, half - 1].wait_recv()
            hops[1, half - 1].wait_recv()
        else:
            way, k = (0, -offset) if offset < 0 else (1, offset)
            hops[way, k - 1].wait_recv()
            begin([hops[way, k]])

    def spot(at, owner):
        return pl.ds(BLK + (at * group + owner) * CAP, CAP)

    def copies_a(at):
        return [
            remote(picked_a.at[at, d], landed.at[at, g], ga_send.at[at, d], ga_recv.at[at, d], peer)
            for d, peer in enumerate(g_peers)
        ]

    def copies_b(at):
        return [
            remote(
                picked_b.at[at, d], table_ref.at[spot(at, g), late], gb_send.at[at, d], gb_recv.at[at, d], peer
            )
            for d, peer in enumerate(g_peers)
        ]

    def bring_a(t):
        at = place(t)
        bring(hops_a, t)
        chunk_a[...] = ring_a[at]
        copies = copies_a(at)
        for d, peer in enumerate(g_peers):
            for c in range(CAP):
                picked_a[at, d, c] = chunk_a[asks[peer[0] % group, 0, at * CAP + c]]
            begin([copies[d]])
        for c in range(CAP):
            landed[at, g, c] = chunk_a[asks[g, 0, at * CAP + c]]

    def bring_b(t):
        at = place(t)
        bring(hops_b, t)
        chunk_b[...] = ring_b[at]
        copies = copies_b(at)
        for d, peer in enumerate(g_peers):
            for c in range(CAP):
                picked_b[at, d, c] = chunk_b[asks[peer[0] % group, 0, at * CAP + c]]
            begin([copies[d]])
        for c in range(CAP):
            table_ref[BLK + (at * group + g) * CAP + c, SHARED:] = chunk_b[asks[g, 0, at * CAP + c]]

    arriving = []

    def make(t):
        at = place(t)
        for copy in copies_a(at):
            copy.wait_recv()
        shared = landed[at].reshape(width * PART, WIDE)
        shared_ref[at] = shared
        both = dot(shared, pairs[...]).astype(jnp.bfloat16)
        for h in range(HEADS):
            made[at, h] = both[:, h * PAIR : (h + 1) * PAIR].reshape(width, PART, PAIR)
        slots = pl.ds(BLK + at * width, width)
        copies = [
            remote(
                made.at[at, peer[1]], table_ref.at[slots, quarter(head)], x_send.at[at, d], x_recv.at[at, d],
                peer,
            )
            for d, peer in enumerate(x_peers)
        ]
        begin(copies)
        arriving.extend(copies)
        table_ref[slots, quarter(head)] = made[at, head]

    for copy in corner:
        copy.wait_recv()
    for copy in questions:
        copy.wait_recv()
    answer = pltpu.make_async_copy(asks_ref, asks, asks_sem)
    answer.start()
    answer.wait()
    bring_a(0)
    for copy in lower:
        copy.wait_recv()
    ring_b[z] = table_ref[:BLK, SHARED:]
    bring_b(0)
    pairs_of = [[t, t + 1] for t in range(1, planes - 1, 2)] + [[planes - 1]]
    before = [0]
    for now in pairs_of:
        for t in now:
            bring_a(t)
        for t in before:
            make(t)
        for t in now:
            bring_b(t)
        before = now
    for t in before:
        make(t)
    for copy in upper + asking + arriving:
        copy.wait_recv()
    for t in range(planes):
        for copy in copies_b(place(t)):
            copy.wait_recv()

    attended = own_copies(
        4, lambda h: packed.at[pl.ds(h * HEADS, HEADS)], att_in.at[head]
    )
    for d in list(range(1, HEADS)) + [0]:
        base = (head + d) % HEADS * HEADS

        @pl.loop(0, HEADS)
        def _(i):
            b = base + i
            chosen = [table_ref[slots_ref[b, j]] for j in range(PER)]
            result, highest, total = attend(unpack(query_ref[b]), chosen, count_ref[b])
            packed[b] = pack(result[:, HD:])
            both_ref[b] = result
            highs[b] = jnp.broadcast_to(highest, (BLOCK, BLOCK))
            sums[b] = jnp.broadcast_to(total, (BLOCK, BLOCK))

        if d:
            begin([attended[d - 1]])
    att_in[head] = packed[own_blocks]
    for copy in attended:
        copy.wait_recv()

    @pl.loop(0, HEADS)
    def _(i):
        att = jnp.concatenate([unpack(att_in[h, i]) for h in range(HEADS)], axis=1)
        att_rows[i] = att
        summed = own_ref[i].astype(jnp.float32) + dot(att, out_weight_ref[...])
        root_mean = jnp.sqrt(jnp.mean(summed * summed, axis=-1, keepdims=True) + 1e-06)
        normed = summed / root_mean
        output_ref[i] = normed.astype(jnp.bfloat16)
        upstream = cotangent_ref[i].astype(jnp.float32)
        grad = (upstream - normed * jnp.mean(upstream * normed, axis=-1, keepdims=True)) / root_mean
        norm_ref[i] = grad
        low_grad[i] = grad.astype(jnp.bfloat16)
        back = dot(grad.astype(jnp.bfloat16), out_weight_ref[...], NT).astype(jnp.bfloat16)
        for h in range(HEADS):
            my_grads[h, i] = pack(back[:, h * HD : (h + 1) * HD])

    back = own_copies(5, lambda h: my_grads.at[h], grad_in.at[own_blocks])
    begin(back)
    grad_in[own_blocks] = my_grads[head]
    out_grad_ref[...] = dot(
        att_rows[...].reshape(rows, WIDE), low_grad[...].reshape(rows, WIDE), TN
    )
    for copy in back:
        copy.wait_recv()

    @pl.loop(0, BLK)
    def _(b):
        grad, result = unpack(grad_in[b]), both_ref[b][:, HD:]
        dots = jnp.sum(grad.astype(jnp.float32) * result.astype(jnp.float32), axis=1, keepdims=True)
        lane = lax.broadcasted_iota(jnp.int32, (BLOCK, BLOCK), 1)
        stat = jnp.where(lane == 0, highs[b], jnp.where(lane == 1, dots, 1.0 / sums[b]))
        stat_ref[b] = stat.T[:8]
        both_ref[b] = jnp.concatenate([unpack(query_ref[b]), grad], axis=1)

    for copy in sent:
        copy.wait_send()


def fetch(features, in_weight, out_weight, cotangent, key_slots, block_count, wanted, node_count):
    planes, group = torus(node_count)
    own = features.reshape(HEADS, BLOCK, WIDE)
    asked = wanted.reshape(planes, group, CAP).transpose(1, 0, 2).reshape(group, 1, planes * CAP)
    asked = jnp.pad(asked, ((0, 0), (0, 7), (0, 128 - planes * CAP)))
    dma = lambda *shape: pltpu.SemaphoreType.DMA(shape)
    vmem = pl.BlockSpec(memory_space=pltpu.VMEM)
    low = lambda *shape: pltpu.VMEM(shape, jnp.bfloat16)
    late = BLOCK - SHARED
    slots = BLK + planes * group * CAP
    return pl.pallas_call(
        functools.partial(fetch_kernel, planes, group),
        out_shape=(
            jax.ShapeDtypeStruct((slots, BLOCK, PAIR), jnp.bfloat16),
            jax.ShapeDtypeStruct((planes, group * CAP * PART, WIDE), jnp.bfloat16),
            jax.ShapeDtypeStruct((group, 8, 128), jnp.int32),
            jax.ShapeDtypeStruct((BLK, BLOCK, PAIR), jnp.bfloat16),
            jax.ShapeDtypeStruct((BLK, 8, BLOCK), jnp.float32),
            jax.ShapeDtypeStruct((HEADS, BLOCK, WIDE), jnp.bfloat16),
            jax.ShapeDtypeStruct((HEADS, BLOCK, WIDE), jnp.float32),
            jax.ShapeDtypeStruct((WIDE, WIDE), jnp.float32),
        ),
        in_specs=[vmem] * 5 + [pl.BlockSpec(memory_space=pltpu.SMEM)] * 2,
        out_specs=(vmem,) * 8,
        scratch_shapes=[
            low(BLK, HD, PAIR),
            low(BLK, HD, PAIR),
            pltpu.VMEM((BLK, BLOCK, BLOCK), jnp.float32),
            pltpu.VMEM((BLK, BLOCK, BLOCK), jnp.float32),
            low(HEADS, HEADS, HD, PAIR),
            low(HEADS, BLOCK, WIDE),
            low(HEADS, BLOCK, WIDE),
            low(HEADS, HEADS, HD, PAIR),
            low(BLK, HD, PAIR),
            low(WIDE, HEADS * PAIR),
            low(HEADS, HEADS, BLOCK, PAIR),
            low(HEADS, HEADS, HD, PAIR),
            low(planes, BLK, PART, WIDE),
            low(planes, BLK, late, PAIR),
            low(BLK, PART, WIDE),
            low(BLK, late, PAIR),
            low(planes, group - 1, CAP, PART, WIDE),
            low(planes, group - 1, CAP, late, PAIR),
            low(planes, group, CAP, PART, WIDE),
            low(planes, HEADS, group * CAP, PART, PAIR),
            pltpu.SMEM((group, 8, 128), jnp.int32),
            dma(6, 3), dma(6, 3), dma(group - 1), dma(group - 1),
            dma(2, planes // 2), dma(2, planes // 2), dma(2, planes // 2), dma(2, planes // 2),
            dma(planes, group - 1), dma(planes, group - 1), dma(planes, group - 1), dma(planes, group - 1),
            dma(planes, 3), dma(planes, 3),
            pltpu.SemaphoreType.DMA,
        ],
        compiler_params=pltpu.CompilerParams(
            collective_id=2, has_side_effects=True, vmem_limit_bytes=56 << 20
        ),
        name="fetch",
    )(own, asked, in_weight, out_weight, cotangent.reshape(own.shape), key_slots, block_count)


def return_kernel(
    planes, group, grads_ref, dq_ref, shared_ref, features_ref, norm_ref, weight_ref, out_ref, asks_ref,
    feature_ref, sum_ref,
    pairs, singles, own_pairs, own_queries, heads, leaving, answers_a, answers_b, partial_a, partial_b,
    ring_a, ring_b, summed, late_sums, quarters, acc, base,
    out_mine, out_in, in_mine, in_in, x_sum, g_in, g_sum, z_in, piece,
    o_send, o_recv, x_send, x_recv, ga_send, ga_recv, gb_send, gb_recv, ra_send, ra_recv, rb_send, rb_recv,
    wg_send, wg_recv, wz_send, wz_recv, bz_send, bz_recv, bg_send, bg_recv,
):
    head, z, g, x_peers, g_peers, right, left = neighbours(planes, group)
    z_peers = [(((z + d) % planes) * group + g, head) for d in range(1, planes)]
    half = planes // 2
    width = group * CAP
    low = BLOCK - SHARED
    early, late = pl.ds(0, SHARED), pl.ds(SHARED, low)
    own_blocks = pl.ds(head * HEADS, HEADS)
    arrive = greet(x_peers + g_peers + z_peers)

    weight = weight_ref[...]
    step = 3 * HD
    for h in range(HEADS):
        pairs[:, h * PAIR : (h + 1) * PAIR] = weight[:, h * step + HD : (h + 1) * step]
    singles[...] = jnp.concatenate(
        [weight[:, h * step : h * step + HD] for h in range(HEADS)], axis=1
    )
    for h in range(HEADS):
        some = out_ref[h * HD : (h + 1) * HD]
        out_mine[h] = jnp.concatenate([some[:, :BLOCK], some[:, BLOCK:]], axis=0)
    arrive()

    order = list(reversed(ring_order(planes)))
    places = [(z + offset + planes) % planes for offset in order]
    spot = lambda at, owner: pl.ds(BLK + (at * group + owner) * CAP, CAP)
    slots = lambda at: pl.ds(BLK + at * width, width)
    sent = []

    def begin(copies):
        for copy in copies:
            copy.start()
            sent.append(copy)

    def to_heads(kind, source, target):
        return [
            remote(source(peer[1]), target, o_send.at[kind, d], o_recv.at[kind, d], peer)
            for d, peer in enumerate(x_peers)
        ]

    blocks_of = lambda h: pl.ds(h * HEADS, HEADS)
    own = to_heads(0, lambda h: grads_ref.at[blocks_of(h), early], own_pairs.at[head, :, early])
    own += to_heads(1, lambda h: dq_ref.at[blocks_of(h)], own_queries.at[head])
    out_copies = to_heads(2, lambda h: out_mine.at[h], out_in.at[head])
    far = [
        [
            remote(
                grads_ref.at[slots(at), quarter(peer[1])], heads.at[at, head],
                x_send.at[at, d], x_recv.at[at, d], peer,
            )
            for d, peer in enumerate(x_peers)
        ]
        for at in places
    ]
    far_late = [
        [
            remote(
                grads_ref.at[spot(at, peer[0] % group), late], answers_b.at[at, g],
                gb_send.at[at, d], gb_recv.at[at, d], peer,
            )
            for d, peer in enumerate(g_peers)
        ]
        for at in places
    ]
    ahead = 3
    for t in range(min(ahead, planes)):
        begin(far[t])
        begin(far_late[t])
    acc[...] = jnp.zeros_like(acc)
    own_pairs[head, :, :SHARED] = grads_ref[own_blocks, :SHARED]
    own_queries[head] = dq_ref[own_blocks]

    def spread(t):
        at = places[t]
        heads[at, head] = grads_ref[slots(at), quarter(head)]
        for copy in far[t]:
            copy.wait_recv()
        if t + ahead < planes:
            begin(far[t + ahead])
            begin(far_late[t + ahead])
        if t + ahead == planes - 1:
            begin(own + out_copies)
        some = jnp.concatenate([heads[at, h].reshape(width * PART, PAIR) for h in range(HEADS)], axis=1)
        back = dot(some, pairs[...], NT).astype(jnp.bfloat16)
        leaving[at] = back.reshape(group, CAP, PART, WIDE)
        copies = [
            remote(
                leaving.at[at, peer[0] % group], answers_a.at[at, g], ga_send.at[at, d], ga_recv.at[at, d], peer
            )
            for d, peer in enumerate(g_peers)
        ]
        begin(copies)
        answers_a[at, g] = leaving[at, g]
        acc[...] += dot(some, shared_ref[at], TN)
        return copies

    def choose(t):
        at = places[t]
        side = width * PART
        column = lax.broadcasted_iota(jnp.int32, (1, side), 1)
        target = column % PART
        for j in range(width):
            block = asks_ref[j // CAP, 0, at * CAP + j % CAP]
            target = target + jnp.where(column // PART == j, block * PART, 0)
        row = lax.broadcasted_iota(jnp.int32, (BLK * PART, side), 0)
        return jnp.where(row == target, 1.0, 0.0).astype(jnp.bfloat16)

    def pass_on(t, total, partial, ring, send, recv):
        at, offset = places[t], order[t]
        mid = BLK // 2

        def hop(way, k):
            source, target = partial.at[at], ring.at[way, k]
            if k == 0:
                blocks = pl.ds(way * mid, mid)
                source, target = source.at[blocks], target.at[blocks]
            return remote(source, target, send.at[way, k], recv.at[way, k], left if way else right)

        if offset == half:
            partial[at] = total.astype(jnp.bfloat16)
            begin([hop(0, 0), hop(1, 0)])
            return None
        k = half - 1 - abs(offset)
        ways = [0] if offset > 0 else [1] if offset < 0 else [0, 1]
        for way in ways:
            hop(way, k).wait_recv()
            if k:
                total = total + ring[way, k].astype(jnp.float32)
            elif way:
                total = jnp.concatenate([total[:mid], total[mid:] + ring[way, k, mid:].astype(jnp.float32)], axis=0)
            else:
                total = jnp.concatenate([total[:mid] + ring[way, k, :mid].astype(jnp.float32), total[mid:]], axis=0)
        if offset:
            partial[at] = total.astype(jnp.bfloat16)
            begin([hop(ways[0], k + 1)])
            return None
        return total

    def gather_late(t, chosen):
        at = places[t]
        for copy in far_late[t]:
            copy.wait_recv()
        answers_b[at, g] = grads_ref[spot(at, g), SHARED:]
        total = [
            dot(chosen, answers_b[at, :, :, i * PART : (i + 1) * PART].reshape(width * PART, PAIR))
            for i in range(low // PART)
        ]
        total = jnp.concatenate([x.reshape(BLK, PART, PAIR) for x in total], axis=1)
        return pass_on(t, total, partial_b, ring_b, rb_send, rb_recv)

    def gather(t, chosen, copies):
        for copy in copies:
            copy.wait_recv()
        total = dot(chosen, answers_a[places[t]].reshape(width * PART, WIDE)).reshape(BLK, PART, WIDE)
        return pass_on(t, total, partial_a, ring_a, ra_send, ra_recv)

    before = None
    for t in range(planes):
        copies = spread(t)
        chosen = choose(t)
        if t == planes - 1:
            for copy in own:
                copy.wait_recv()
            some = jnp.concatenate(
                [own_pairs[h, :, :SHARED].reshape(HEADS * SHARED, PAIR) for h in range(HEADS)], axis=1
            )
            queries = jnp.concatenate(
                [
                    jnp.concatenate(
                        [own_queries[h, :, :, :HD], own_queries[h, :, :, HD:]], axis=1
                    ).reshape(HEADS * BLOCK, HD)
                    for h in range(HEADS)
                ],
                axis=1,
            )
            everything = features_ref[...].reshape(HEADS * BLOCK, WIDE)
            acc[...] += dot(some, features_ref[:, :SHARED].reshape(HEADS * SHARED, WIDE), TN)
            single_weight = dot(queries, everything, TN)
            base[...] = norm_ref[...] + dot(queries, singles[...], NT).reshape(HEADS, BLOCK, WIDE)
            base[:, :SHARED] += dot(some, pairs[...], NT).reshape(HEADS, SHARED, WIDE)
        total = gather_late(t, chosen)
        if t == planes - 1:
            late_sums[...] = (grads_ref[:BLK, SHARED:].astype(jnp.float32) + total).astype(jnp.bfloat16)
            tail = to_heads(3, lambda h: late_sums.at[blocks_of(h)], own_pairs.at[head, :, late])
            begin(tail)
            own_pairs[head, :, SHARED:] = late_sums[own_blocks]
        if t:
            gather(t - 1, *before)
        before = (chosen, copies)
    summed[...] = gather(planes - 1, *before).astype(jnp.bfloat16)
    final = to_heads(4, lambda h: summed.at[blocks_of(h)], quarters.at[head])
    begin(final)
    quarters[head] = summed[own_blocks]

    for copy in tail:
        copy.wait_recv()
    some = jnp.concatenate(
        [own_pairs[h, :, SHARED:].reshape(HEADS * low, PAIR) for h in range(HEADS)], axis=1
    )
    pair_weight = acc[...] + dot(some, features_ref[:, SHARED:].reshape(HEADS * low, WIDE), TN)
    for h in range(HEADS):
        terms = jnp.concatenate(
            [single_weight[h * HD : (h + 1) * HD], pair_weight[h * PAIR : (h + 1) * PAIR]], axis=0
        )
        terms = jnp.concatenate([terms[:, :BLOCK], terms[:, BLOCK:]], axis=0)
        in_mine[h] = terms.astype(jnp.bfloat16)
        if h == 0:
            in_own = jnp.where(head == 0, terms, 0.0)
        else:
            in_own = in_own + jnp.where(head == h, terms, 0.0)
    in_low = to_heads(5, lambda h: in_mine.at[h], in_in.at[head])
    begin(in_low)

    base[:, SHARED:] += dot(some, pairs[...], NT).reshape(HEADS, low, WIDE)
    feature_ref[:, SHARED:] = base[:, SHARED:].astype(jnp.bfloat16)
    for copy in final:
        copy.wait_recv()
    for h in range(HEADS):
        rows = slice(h * PART, (h + 1) * PART)
        feature_ref[:, rows] = (base[:, rows] + quarters[h].astype(jnp.float32)).astype(jnp.bfloat16)

    def exchange(peers, source, target, send, recv):
        copies = [
            remote(source(d, peer), target(d), send.at[d], recv.at[d], peer) for d, peer in enumerate(peers)
        ]
        begin(copies)
        return copies

    for copy in out_copies + in_low:
        copy.wait_recv()
    out_in[head] = out_mine[head]
    in_total = in_own
    for _, h in x_peers:
        in_total = in_total + in_in[h].astype(jnp.float32)
    out_total = out_in[0] + out_in[1] + out_in[2] + out_in[3]
    x_sum[...] = jnp.concatenate([in_total, out_total], axis=0).reshape(x_sum.shape)
    for copy in exchange(
        g_peers, lambda d, peer: x_sum.at[peer[0] % group], lambda d: g_in.at[d], wg_send, wg_recv
    ):
        copy.wait_recv()
    total = x_sum[g]
    for d in range(group - 1):
        total = total + g_in[d]
    g_sum[...] = total
    for copy in exchange(
        z_peers, lambda d, peer: g_sum.at[peer[0] // group], lambda d: z_in.at[d], wz_send, wz_recv
    ):
        copy.wait_recv()
    total = g_sum[z]
    for d in range(planes - 1):
        total = total + z_in[d]
    piece[...] = total
    sum_ref[g, z] = total
    for copy in exchange(z_peers, lambda d, peer: piece, lambda d: sum_ref.at[g, z], bz_send, bz_recv):
        copy.wait_recv()
    for copy in exchange(g_peers, lambda d, peer: sum_ref.at[g], lambda d: sum_ref.at[g], bg_send, bg_recv):
        copy.wait_recv()
    for copy in sent:
        copy.wait_send()


def give_back(grads, dq, shared, features, norm_grad, in_weight, out_grad, asks, node_count):
    planes, group = torus(node_count)
    rows = 4 * HD * 2 // (planes * group)
    late = BLOCK - SHARED
    dma = lambda *shape: pltpu.SemaphoreType.DMA(shape)
    vmem = pl.BlockSpec(memory_space=pltpu.VMEM)
    low = lambda *shape: pltpu.VMEM(shape, jnp.bfloat16)
    high = lambda *shape: pltpu.VMEM(shape, jnp.float32)
    both = lambda *shape: [dma(*shape)] * 2
    feature_grad, total = pl.pallas_call(
        functools.partial(return_kernel, planes, group),
        out_shape=(
            jax.ShapeDtypeStruct((HEADS, BLOCK, WIDE), jnp.bfloat16),
            jax.ShapeDtypeStruct((group, planes, rows, 128), jnp.float32),
        ),
        in_specs=[vmem] * 7 + [pl.BlockSpec(memory_space=pltpu.SMEM)],
        out_specs=(vmem,) * 2,
        scratch_shapes=[
            low(WIDE, HEADS * PAIR),
            low(WIDE, HEADS * HD),
            low(HEADS, HEADS, BLOCK, PAIR),
            low(HEADS, HEADS, HD, PAIR),
            low(planes, HEADS, group * CAP, PART, PAIR),
            low(planes, group, CAP, PART, WIDE),
            low(planes, group, CAP, PART, WIDE),
            low(planes, group, CAP, late, PAIR),
            low(planes, BLK, PART, WIDE),
            low(planes, BLK, late, PAIR),
            low(2, planes // 2, BLK, PART, WIDE),
            low(2, planes // 2, BLK, late, PAIR),
            low(BLK, PART, WIDE),
            low(BLK, late, PAIR),
            low(HEADS, HEADS, PART, WIDE),
            high(HEADS * PAIR, WIDE),
            high(HEADS, BLOCK, WIDE),
            high(HEADS, 2 * HD, 128),
            high(HEADS, 2 * HD, 128),
            low(HEADS, 6 * HD, 128),
            low(HEADS, 6 * HD, 128),
            high(group, planes, rows, 128),
            high(group - 1, planes, rows, 128),
            high(planes, rows, 128),
            high(planes - 1, rows, 128),
            high(rows, 128),
            *both(6, 3), *both(planes, 3), *both(planes, group - 1), *both(planes, group - 1),
            *both(2, planes // 2), *both(2, planes // 2),
            *both(group - 1), *both(planes - 1), *both(planes - 1), *both(group - 1),
        ],
        compiler_params=pltpu.CompilerParams(
            collective_id=3, has_side_effects=True, vmem_limit_bytes=56 << 20
        ),
        name="give_back",
    )(grads, dq, shared, features.reshape(HEADS, BLOCK, WIDE), norm_grad, in_weight, out_grad, asks)
    total = total.reshape(4 * HD * 2, 128)
    in_total, out_total = total[: 6 * HD], total[6 * HD :]
    in_total = jnp.concatenate([in_total[: 3 * HD], in_total[3 * HD :]], axis=1)
    out_total = jnp.concatenate([out_total[:HD], out_total[HD:]], axis=1)
    return feature_grad.reshape(HEADS * BLOCK, WIDE), in_total.T, out_total


def on_device(features, in_weight, out_weight, cotangent, key_slots, block_count, wanted):
    node_count = lax.axis_size("node")
    total_nodes = BLK * BLOCK * node_count
    table, shared, asks, both, stat, output, norm_grad, out_weight_grad = fetch(
        features, in_weight, out_weight, cotangent, key_slots, block_count, wanted, node_count
    )
    dq, grads = backward(key_slots.reshape(-1), block_count, both, stat, table)
    feature_grad, in_weight_grad, out_weight_grad = give_back(
        grads, dq, shared, features, norm_grad, in_weight, out_weight_grad, asks, node_count
    )
    grad_factor = total_nodes ** (-0.5)
    return (
        output.reshape(features.shape),
        feature_grad,
        in_weight_grad * grad_factor,
        out_weight_grad * grad_factor,
    )


def solution(mesh):
    placed = (
        P(("node", "head"), None),
        P(),
        P(),
        P(("node", "head"), None),
        P("node", None),
        P("node"),
        P("node", None, None),
    )
    return jax.shard_map(
        on_device,
        mesh=mesh,
        in_specs=placed,
        out_specs=(
            P(("node", "head"), None),
            P(("node", "head"), None),
            P(None, "head"),
            P("head", None),
        ),
        check_vma=False,
    )
```

```python
import functools

import jax
import jax.numpy as jnp
from jax import lax
from jax.experimental import pallas as pl
from jax.experimental.pallas import tpu as pltpu
from jax.sharding import PartitionSpec as P

HEADS = 4
HD = 64
BLOCK = 128
BLK = 16
PER = 12
CAP = 2
PAIR = 2 * HD
PAIRED = 2
WIDE = 2 * BLOCK
SHARED = BLOCK // 2
PART = SHARED // HEADS
LUMP = PART + (BLOCK - SHARED) // 2
SCALE = HD ** (-0.5)
NT = (((1,), (1,)), ((), ()))
TN = (((0,), (0,)), ((), ()))
MESH = pl.DeviceIdType.MESH


def dot(a, b, dims=(((1,), (0,)), ((), ()))):
    return lax.dot_general(a, b, dims, preferred_element_type=jnp.float32)


def unpack(packed):
    return jnp.concatenate([packed[..., :HD], packed[..., HD:]], axis=-2)


def pack(rows):
    return jnp.concatenate([rows[..., :HD, :], rows[..., HD:, :]], axis=-1)


def attend(query, chosen, count):
    query = jnp.concatenate([query, jnp.zeros_like(query)], axis=1)
    scores = []
    for j in range(0, PER, 2):
        pair = dot(query, jnp.concatenate(chosen[j : j + 2], axis=0), NT)
        for i in range(2):
            dead = jnp.where(j + i < count, 0.0, -1e30)
            scores.append(pair[:, i * BLOCK : (i + 1) * BLOCK] + dead)
    highest = scores[0]
    for part in scores[1:]:
        highest = jnp.maximum(highest, part)
    highest = jnp.max(highest, axis=1, keepdims=True)
    total = jnp.zeros((BLOCK, BLOCK), jnp.float32)
    result = jnp.zeros((BLOCK, PAIR), jnp.float32)
    for j in range(0, PER, 2):
        raised = [jnp.exp(part - highest) for part in scores[j : j + 2]]
        total = total + raised[0] + raised[1]
        result = result + dot(
            jnp.concatenate([x.astype(jnp.bfloat16) for x in raised], axis=1),
            jnp.concatenate(chosen[j : j + 2], axis=0),
        )
    total = jnp.sum(total, axis=1, keepdims=True)
    return (result / total).astype(jnp.bfloat16), highest, total


def backward_kernel(slots_ref, count_ref, both_ref, stat_ref, table_ref, dq_ref, grads_ref, acc_ref, keys_ref, terms_ref):
    step = pl.program_id(0)

    @pl.when(step == 0)
    def _():
        acc_ref[...] = jnp.zeros_like(acc_ref)

    stacks, slots = [], []
    for i in range(PAIRED):
        b = step * PAIRED + i
        count = count_ref[b]
        both = both_ref[i]
        lane = lax.broadcasted_iota(jnp.int32, both.shape, 1)
        zero = jnp.zeros_like(both)
        stacked = jnp.concatenate(
            [jnp.where(lane < HD, both, zero), jnp.where(lane < HD, zero, both)], axis=0
        )
        stacks.append(stacked)
        highest, dots, inverse = stat_ref[i, 0:1], stat_ref[i, 1:2], stat_ref[i, 2:3]
        slots.append([slots_ref[b * PER + j] for j in range(PER)])
        for j in range(PER):
            keys_ref[i, j * BLOCK : (j + 1) * BLOCK] = table_ref[slots[i][j]]
        for j in range(0, PER, 2):
            products = dot(keys_ref[i, j * BLOCK : (j + 2) * BLOCK], stacked, NT)
            for k in range(2):
                rows = slice(k * BLOCK, (k + 1) * BLOCK)
                top = highest + jnp.where(j + k < count, 0.0, 1e30)
                attention = jnp.exp(products[rows, :BLOCK] - top) * inverse
                score_grad = attention * (products[rows, BLOCK:] - dots)
                terms_ref[i, (j + k) * BLOCK : (j + k + 1) * BLOCK] = jnp.concatenate(
                    [score_grad.astype(jnp.bfloat16), attention.astype(jnp.bfloat16)], axis=1
                )
    for i in range(PAIRED):
        dq = dot(keys_ref[i], terms_ref[i, :, :BLOCK], TN)
        dq = (dq.T * SCALE).astype(jnp.bfloat16)
        dq_ref[i] = pack(dq[:, :HD])
        for j in range(0, PER, 2):
            grads = dot(terms_ref[i, j * BLOCK : (j + 2) * BLOCK], stacks[i])
            for k in range(2):
                acc_ref[slots[i][j + k]] += grads[k * BLOCK : (k + 1) * BLOCK]

    @pl.when(step == pl.num_programs(0) - 1)
    def _():
        grads_ref[...] = acc_ref[...].astype(jnp.bfloat16)


def backward(slots, count, both, stat, table):
    whole = lambda shape: pl.BlockSpec(shape, lambda b, *_: (0,) * len(shape))
    some = lambda *shape: pl.BlockSpec((PAIRED,) + shape, lambda b, *_: (b, 0, 0))
    grid_spec = pltpu.PrefetchScalarGridSpec(
        num_scalar_prefetch=2,
        grid=(BLK // PAIRED,),
        in_specs=[some(BLOCK, PAIR), some(8, BLOCK), whole(table.shape)],
        out_specs=[some(HD, PAIR), whole(table.shape)],
        scratch_shapes=[
            pltpu.VMEM(table.shape, jnp.float32),
            pltpu.VMEM((PAIRED, PER * BLOCK, PAIR), jnp.bfloat16),
            pltpu.VMEM((PAIRED, PER * BLOCK, 2 * BLOCK), jnp.bfloat16),
        ],
    )
    return pl.pallas_call(
        backward_kernel,
        grid_spec=grid_spec,
        out_shape=(
            jax.ShapeDtypeStruct((BLK, HD, PAIR), jnp.bfloat16),
            jax.ShapeDtypeStruct(table.shape, jnp.bfloat16),
        ),
        compiler_params=pltpu.CompilerParams(vmem_limit_bytes=56 << 20),
        cost_estimate=pl.CostEstimate(
            flops=10 * BLK * PER * BLOCK**3, bytes_accessed=16 << 20, transcendentals=BLK * PER * BLOCK**2
        ),
        name="attend_back",
    )(slots, count, both, stat, table)


def torus(node_count):
    rows = 4 if node_count >= 64 else 2
    return node_count // (2 * rows), rows * 2


def ring_order(planes):
    half = planes // 2
    return [0] + [s * k for k in range(1, half) for s in (-1, 1)] + [half]


def quarter(h):
    return pl.ds(pl.multiple_of(h * PART, PART), PART)


def remote(source, target, send, recv, peer):
    return pltpu.make_async_remote_copy(
        source, target, send, recv, device_id=peer, device_id_type=MESH
    )


def neighbours(planes, group):
    node, head = lax.axis_index("node"), lax.axis_index("head")
    z, g = node // group, node % group
    x_peers = [(node, (head + d) % HEADS) for d in range(1, HEADS)]
    g_peers = [(z * group + (g + d) % group, head) for d in range(1, group)]
    right = (((z + 1) % planes) * group + g, head)
    left = (((z + planes - 1) % planes) * group + g, head)
    return head, z, g, x_peers, g_peers, right, left


def greet(peers):
    barrier = pltpu.get_barrier_semaphore()
    for peer in peers:
        pl.semaphore_signal(barrier, inc=1, device_id=peer, device_id_type=MESH)
    return lambda: pl.semaphore_wait(barrier, len(peers))


def fetch_kernel(
    planes, group, own_ref, asked_ref, weight_ref, out_weight_ref, cotangent_ref, slots_ref, count_ref,
    table_ref, shared_ref, asks_ref, both_ref, stat_ref, output_ref, norm_ref, out_grad_ref,
    query_ref, packed, highs, sums, att_in, att_rows, low_grad, my_grads, grad_in,
    pairs, my_pairs, my_queries, ring_a, ring_b, chunk_a, chunk_b, picked_a, picked_b, landed, made, asks,
    o_send, o_recv, q_send, q_recv, ra_send, ra_recv, rb_send, rb_recv,
    ga_send, ga_recv, gb_send, gb_recv, x_send, x_recv, asks_sem,
):
    head, z, g, x_peers, g_peers, right, left = neighbours(planes, group)
    half = planes // 2
    width = group * CAP
    rows = HEADS * BLOCK
    late = pl.ds(SHARED, BLOCK - SHARED)
    own_blocks = pl.ds(head * HEADS, HEADS)
    arrive = greet(x_peers + g_peers + [right, left])

    ring_a[z, own_blocks] = own_ref[:, quarter(head)]
    weight = weight_ref[...]
    step = 3 * HD
    for h in range(HEADS):
        pairs[:, h * PAIR : (h + 1) * PAIR] = weight[:, h * step + HD : (h + 1) * step]
    own = own_ref[...].reshape(rows, WIDE)
    for h in range(HEADS):
        both = dot(own, pairs[:, h * PAIR : (h + 1) * PAIR]).astype(jnp.bfloat16)
        my_pairs[h] = both.reshape(HEADS, BLOCK, PAIR)
        queries = (dot(own, weight[:, h * step : h * step + HD]) * SCALE).astype(jnp.bfloat16)
        my_queries[h] = pack(queries.reshape(HEADS, BLOCK, HD))
    arrive()

    def own_copies(kind, source, target):
        return [
            remote(source(peer[1]), target, o_send.at[kind, d], o_recv.at[kind, d], peer)
            for d, peer in enumerate(x_peers)
        ]

    early = pl.ds(0, SHARED)
    corner = own_copies(0, lambda h: own_ref.at[:, quarter(h)], ring_a.at[z, own_blocks])
    lower = own_copies(1, lambda h: my_pairs.at[h, :, late], table_ref.at[own_blocks, late])
    upper = own_copies(2, lambda h: my_pairs.at[h, :, early], table_ref.at[own_blocks, early])
    asking = own_copies(3, lambda h: my_queries.at[h], query_ref.at[own_blocks])
    questions = [
        remote(asked_ref.at[peer[0] % group], asks_ref.at[g], q_send.at[d], q_recv.at[d], peer)
        for d, peer in enumerate(g_peers)
    ]
    sent = []

    def begin(copies):
        for copy in copies:
            copy.start()
            sent.append(copy)

    begin(corner + questions + lower + upper + asking)
    table_ref[own_blocks] = my_pairs[head]
    query_ref[own_blocks] = my_queries[head]
    asks_ref[g] = asked_ref[g]

    def hop(ring, send, recv, way, k):
        at = (z - k + planes) % planes if way == 0 else (z + k) % planes
        view = ring.at[at]
        if k == half - 1:
            view = view.at[pl.ds(way * (BLK // 2), BLK // 2)]
        return remote(view, view, send.at[way, k], recv.at[way, k], left if way else right)

    def hops(ring, send, recv):
        return {(way, k): hop(ring, send, recv, way, k) for way in range(2) for k in range(half)}

    hops_a = hops(ring_a, ra_send, ra_recv)
    hops_b = hops(ring_b, rb_send, rb_recv)
    order = ring_order(planes)
    place = lambda t: (z + order[t] + planes) % planes

    def bring(hops, t):
        offset = order[t]
        if offset == 0:
            begin([hops[0, 0], hops[1, 0]])
        elif offset == half:
            hops[0, half - 1].wait_recv()
            hops[1, half - 1].wait_recv()
        else:
            way, k = (0, -offset) if offset < 0 else (1, offset)
            hops[way, k - 1].wait_recv()
            begin([hops[way, k]])

    def spot(at, owner):
        return pl.ds(BLK + (at * group + owner) * CAP, CAP)

    def copies_a(at):
        return [
            remote(picked_a.at[at, d], landed.at[at, g], ga_send.at[at, d], ga_recv.at[at, d], peer)
            for d, peer in enumerate(g_peers)
        ]

    def copies_b(at):
        return [
            remote(
                picked_b.at[at, d], table_ref.at[spot(at, g), late], gb_send.at[at, d], gb_recv.at[at, d], peer
            )
            for d, peer in enumerate(g_peers)
        ]

    def bring_a(t):
        at = place(t)
        bring(hops_a, t)
        chunk_a[...] = ring_a[at]
        copies = copies_a(at)
        for d, peer in enumerate(g_peers):
            for c in range(CAP):
                picked_a[at, d, c] = chunk_a[asks[peer[0] % group, 0, at * CAP + c]]
            begin([copies[d]])
        for c in range(CAP):
            landed[at, g, c] = chunk_a[asks[g, 0, at * CAP + c]]

    def bring_b(t):
        at = place(t)
        bring(hops_b, t)
        chunk_b[...] = ring_b[at]
        copies = copies_b(at)
        for d, peer in enumerate(g_peers):
            for c in range(CAP):
                picked_b[at, d, c] = chunk_b[asks[peer[0] % group, 0, at * CAP + c]]
            begin([copies[d]])
        for c in range(CAP):
            table_ref[BLK + (at * group + g) * CAP + c, SHARED:] = chunk_b[asks[g, 0, at * CAP + c]]

    arriving = []

    def make(t):
        at = place(t)
        for copy in copies_a(at):
            copy.wait_recv()
        shared = landed[at].reshape(width * PART, WIDE)
        shared_ref[at] = shared
        both = dot(shared, pairs[...]).astype(jnp.bfloat16)
        for h in range(HEADS):
            made[at, h] = both[:, h * PAIR : (h + 1) * PAIR].reshape(width, PART, PAIR)
        slots = pl.ds(BLK + at * width, width)
        copies = [
            remote(
                made.at[at, peer[1]], table_ref.at[slots, quarter(head)], x_send.at[at, d], x_recv.at[at, d],
                peer,
            )
            for d, peer in enumerate(x_peers)
        ]
        begin(copies)
        arriving.extend(copies)
        table_ref[slots, quarter(head)] = made[at, head]

    for copy in corner:
        copy.wait_recv()
    for copy in questions:
        copy.wait_recv()
    answer = pltpu.make_async_copy(asks_ref, asks, asks_sem)
    answer.start()
    answer.wait()
    bring_a(0)
    for copy in lower:
        copy.wait_recv()
    ring_b[z] = table_ref[:BLK, SHARED:]
    bring_b(0)
    pairs_of = [[t, t + 1] for t in range(1, planes - 1, 2)] + [[planes - 1]]
    before = [0]
    for now in pairs_of:
        for t in now:
            bring_a(t)
        for t in before:
            make(t)
        for t in now:
            bring_b(t)
        before = now
    for t in before:
        make(t)
    for copy in upper + asking + arriving:
        copy.wait_recv()
    for t in range(planes):
        for copy in copies_b(place(t)):
            copy.wait_recv()

    attended = own_copies(
        4, lambda h: packed.at[pl.ds(h * HEADS, HEADS)], att_in.at[head]
    )
    for d in list(range(1, HEADS)) + [0]:
        base = (head + d) % HEADS * HEADS

        @pl.loop(0, HEADS // PAIRED)
        def _(i):
            blocks = [base + i * PAIRED + k for k in range(PAIRED)]
            chosen = [[table_ref[slots_ref[b, j]] for j in range(PER)] for b in blocks]
            results = [
                attend(unpack(query_ref[b]), some, count_ref[b]) for b, some in zip(blocks, chosen)
            ]
            for b, (result, highest, total) in zip(blocks, results):
                packed[b] = pack(result[:, HD:])
                both_ref[b] = result
                highs[b] = jnp.broadcast_to(highest, (BLOCK, BLOCK))
                sums[b] = jnp.broadcast_to(total, (BLOCK, BLOCK))

        if d:
            begin([attended[d - 1]])
    att_in[head] = packed[own_blocks]
    for copy in attended:
        copy.wait_recv()

    @pl.loop(0, HEADS)
    def _(i):
        att = jnp.concatenate([unpack(att_in[h, i]) for h in range(HEADS)], axis=1)
        att_rows[i] = att
        summed = own_ref[i].astype(jnp.float32) + dot(att, out_weight_ref[...])
        root_mean = jnp.sqrt(jnp.mean(summed * summed, axis=-1, keepdims=True) + 1e-06)
        normed = summed / root_mean
        output_ref[i] = normed.astype(jnp.bfloat16)
        upstream = cotangent_ref[i].astype(jnp.float32)
        grad = (upstream - normed * jnp.mean(upstream * normed, axis=-1, keepdims=True)) / root_mean
        norm_ref[i] = grad
        low_grad[i] = grad.astype(jnp.bfloat16)
        back = dot(grad.astype(jnp.bfloat16), out_weight_ref[...], NT).astype(jnp.bfloat16)
        for h in range(HEADS):
            my_grads[h, i] = pack(back[:, h * HD : (h + 1) * HD])

    back = own_copies(5, lambda h: my_grads.at[h], grad_in.at[own_blocks])
    begin(back)
    grad_in[own_blocks] = my_grads[head]
    out_grad_ref[...] = dot(
        att_rows[...].reshape(rows, WIDE), low_grad[...].reshape(rows, WIDE), TN
    )
    for copy in back:
        copy.wait_recv()

    @pl.loop(0, BLK // 4)
    def _(i):
        done = []
        for k in range(4):
            b = i * 4 + k
            grad, result = unpack(grad_in[b]), both_ref[b][:, HD:]
            dots = jnp.sum(grad.astype(jnp.float32) * result.astype(jnp.float32), axis=1, keepdims=True)
            lane = lax.broadcasted_iota(jnp.int32, (BLOCK, BLOCK), 1)
            stat = jnp.where(lane == 0, highs[b], jnp.where(lane == 1, dots, 1.0 / sums[b]))
            done.append((b, stat.T[:8], jnp.concatenate([unpack(query_ref[b]), grad], axis=1)))
        for b, stat, both in done:
            stat_ref[b] = stat
            both_ref[b] = both

    for copy in sent:
        copy.wait_send()


def fetch(features, in_weight, out_weight, cotangent, key_slots, block_count, wanted, node_count):
    planes, group = torus(node_count)
    own = features.reshape(HEADS, BLOCK, WIDE)
    asked = wanted.reshape(planes, group, CAP).transpose(1, 0, 2).reshape(group, 1, planes * CAP)
    asked = jnp.pad(asked, ((0, 0), (0, 7), (0, 128 - planes * CAP)))
    dma = lambda *shape: pltpu.SemaphoreType.DMA(shape)
    vmem = pl.BlockSpec(memory_space=pltpu.VMEM)
    low = lambda *shape: pltpu.VMEM(shape, jnp.bfloat16)
    late = BLOCK - SHARED
    slots = BLK + planes * group * CAP
    return pl.pallas_call(
        functools.partial(fetch_kernel, planes, group),
        out_shape=(
            jax.ShapeDtypeStruct((slots, BLOCK, PAIR), jnp.bfloat16),
            jax.ShapeDtypeStruct((planes, group * CAP * PART, WIDE), jnp.bfloat16),
            jax.ShapeDtypeStruct((group, 8, 128), jnp.int32),
            jax.ShapeDtypeStruct((BLK, BLOCK, PAIR), jnp.bfloat16),
            jax.ShapeDtypeStruct((BLK, 8, BLOCK), jnp.float32),
            jax.ShapeDtypeStruct((HEADS, BLOCK, WIDE), jnp.bfloat16),
            jax.ShapeDtypeStruct((HEADS, BLOCK, WIDE), jnp.float32),
            jax.ShapeDtypeStruct((WIDE, WIDE), jnp.float32),
        ),
        in_specs=[vmem] * 5 + [pl.BlockSpec(memory_space=pltpu.SMEM)] * 2,
        out_specs=(vmem,) * 8,
        scratch_shapes=[
            low(BLK, HD, PAIR),
            low(BLK, HD, PAIR),
            pltpu.VMEM((BLK, BLOCK, BLOCK), jnp.float32),
            pltpu.VMEM((BLK, BLOCK, BLOCK), jnp.float32),
            low(HEADS, HEADS, HD, PAIR),
            low(HEADS, BLOCK, WIDE),
            low(HEADS, BLOCK, WIDE),
            low(HEADS, HEADS, HD, PAIR),
            low(BLK, HD, PAIR),
            low(WIDE, HEADS * PAIR),
            low(HEADS, HEADS, BLOCK, PAIR),
            low(HEADS, HEADS, HD, PAIR),
            low(planes, BLK, PART, WIDE),
            low(planes, BLK, late, PAIR),
            low(BLK, PART, WIDE),
            low(BLK, late, PAIR),
            low(planes, group - 1, CAP, PART, WIDE),
            low(planes, group - 1, CAP, late, PAIR),
            low(planes, group, CAP, PART, WIDE),
            low(planes, HEADS, group * CAP, PART, PAIR),
            pltpu.SMEM((group, 8, 128), jnp.int32),
            dma(6, 3), dma(6, 3), dma(group - 1), dma(group - 1),
            dma(2, planes // 2), dma(2, planes // 2), dma(2, planes // 2), dma(2, planes // 2),
            dma(planes, group - 1), dma(planes, group - 1), dma(planes, group - 1), dma(planes, group - 1),
            dma(planes, 3), dma(planes, 3),
            pltpu.SemaphoreType.DMA,
        ],
        compiler_params=pltpu.CompilerParams(
            collective_id=2, has_side_effects=True, vmem_limit_bytes=56 << 20
        ),
        name="fetch",
    )(own, asked, in_weight, out_weight, cotangent.reshape(own.shape), key_slots, block_count)


def return_kernel(
    planes, group, grads_ref, dq_ref, shared_ref, features_ref, norm_ref, weight_ref, out_ref, asks_ref,
    feature_ref, sum_ref,
    pairs, singles, own_pairs, own_queries, heads, leaving, answers_a, answers_b, partial_a, partial_b,
    ring_a, ring_b, summed, late_sums, quarters, acc, base,
    out_mine, out_in, in_mine, in_in, x_sum, g_in, g_sum, z_in, piece,
    o_send, o_recv, x_send, x_recv, ga_send, ga_recv, gb_send, gb_recv, ra_send, ra_recv, rb_send, rb_recv,
    wg_send, wg_recv, wz_send, wz_recv, bz_send, bz_recv, bg_send, bg_recv,
):
    head, z, g, x_peers, g_peers, right, left = neighbours(planes, group)
    z_peers = [(((z + d) % planes) * group + g, head) for d in range(1, planes)]
    half = planes // 2
    width = group * CAP
    low = BLOCK - SHARED
    early, late = pl.ds(0, SHARED), pl.ds(SHARED, low)
    own_blocks = pl.ds(head * HEADS, HEADS)
    arrive = greet(x_peers + g_peers + z_peers)

    weight = weight_ref[...]
    step = 3 * HD
    for h in range(HEADS):
        pairs[:, h * PAIR : (h + 1) * PAIR] = weight[:, h * step + HD : (h + 1) * step]
    singles[...] = jnp.concatenate(
        [weight[:, h * step : h * step + HD] for h in range(HEADS)], axis=1
    )
    for h in range(HEADS):
        some = out_ref[h * HD : (h + 1) * HD]
        out_mine[h] = jnp.concatenate([some[:, :BLOCK], some[:, BLOCK:]], axis=0)
    arrive()

    order = list(reversed(ring_order(planes)))
    places = [(z + offset + planes) % planes for offset in order]
    spot = lambda at, owner: pl.ds(BLK + (at * group + owner) * CAP, CAP)
    slots = lambda at: pl.ds(BLK + at * width, width)
    sent = []

    def begin(copies):
        for copy in copies:
            copy.start()
            sent.append(copy)

    def to_heads(kind, source, target):
        return [
            remote(source(peer[1]), target, o_send.at[kind, d], o_recv.at[kind, d], peer)
            for d, peer in enumerate(x_peers)
        ]

    blocks_of = lambda h: pl.ds(h * HEADS, HEADS)
    own = to_heads(0, lambda h: grads_ref.at[blocks_of(h), early], own_pairs.at[head, :, early])
    own += to_heads(1, lambda h: dq_ref.at[blocks_of(h)], own_queries.at[head])
    out_copies = to_heads(2, lambda h: out_mine.at[h], out_in.at[head])
    far = [
        [
            remote(
                grads_ref.at[slots(at), quarter(peer[1])], heads.at[at, head],
                x_send.at[at, d], x_recv.at[at, d], peer,
            )
            for d, peer in enumerate(x_peers)
        ]
        for at in places
    ]
    far_late = [
        [
            remote(
                grads_ref.at[spot(at, peer[0] % group), late], answers_b.at[at, g],
                gb_send.at[at, d], gb_recv.at[at, d], peer,
            )
            for d, peer in enumerate(g_peers)
        ]
        for at in places
    ]
    ahead = 3
    for t in range(min(ahead, planes)):
        begin(far[t])
        begin(far_late[t])
    acc[...] = jnp.zeros_like(acc)
    own_pairs[head, :, :SHARED] = grads_ref[own_blocks, :SHARED]
    own_queries[head] = dq_ref[own_blocks]

    def spread(t):
        at = places[t]
        heads[at, head] = grads_ref[slots(at), quarter(head)]
        for copy in far[t]:
            copy.wait_recv()
        if t + ahead < planes:
            begin(far[t + ahead])
            begin(far_late[t + ahead])
        if t + ahead == planes - 1:
            begin(own + out_copies)
        some = jnp.concatenate([heads[at, h].reshape(width * PART, PAIR) for h in range(HEADS)], axis=1)
        back = dot(some, pairs[...], NT).astype(jnp.bfloat16)
        leaving[at] = back.reshape(group, CAP, PART, WIDE)
        copies = [
            remote(
                leaving.at[at, peer[0] % group], answers_a.at[at, g], ga_send.at[at, d], ga_recv.at[at, d], peer
            )
            for d, peer in enumerate(g_peers)
        ]
        begin(copies)
        answers_a[at, g] = leaving[at, g]
        acc[...] += dot(some, shared_ref[at], TN)
        return copies

    def choose(t):
        at = places[t]
        side = width * PART
        column = lax.broadcasted_iota(jnp.int32, (1, side), 1)
        target = column % PART
        for j in range(width):
            block = asks_ref[j // CAP, 0, at * CAP + j % CAP]
            target = target + jnp.where(column // PART == j, block * PART, 0)
        row = lax.broadcasted_iota(jnp.int32, (BLK * PART, side), 0)
        return jnp.where(row == target, 1.0, 0.0).astype(jnp.bfloat16)

    def pass_on(t, total, partial, ring, send, recv):
        at, offset = places[t], order[t]
        mid = BLK // 2

        def hop(way, k):
            source, target = partial.at[at], ring.at[way, k]
            if k == 0:
                blocks = pl.ds(way * mid, mid)
                source, target = source.at[blocks], target.at[blocks]
            return remote(source, target, send.at[way, k], recv.at[way, k], left if way else right)

        if offset == half:
            partial[at] = total.astype(jnp.bfloat16)
            begin([hop(0, 0), hop(1, 0)])
            return None
        k = half - 1 - abs(offset)
        ways = [0] if offset > 0 else [1] if offset < 0 else [0, 1]
        for way in ways:
            hop(way, k).wait_recv()
            if k:
                total = total + ring[way, k].astype(jnp.float32)
            elif way:
                total = jnp.concatenate([total[:mid], total[mid:] + ring[way, k, mid:].astype(jnp.float32)], axis=0)
            else:
                total = jnp.concatenate([total[:mid] + ring[way, k, :mid].astype(jnp.float32), total[mid:]], axis=0)
        if offset:
            partial[at] = total.astype(jnp.bfloat16)
            begin([hop(ways[0], k + 1)])
            return None
        return total

    def gather_late(t, chosen):
        at = places[t]
        for copy in far_late[t]:
            copy.wait_recv()
        answers_b[at, g] = grads_ref[spot(at, g), SHARED:]
        total = [
            dot(chosen, answers_b[at, :, :, i * PART : (i + 1) * PART].reshape(width * PART, PAIR))
            for i in range(low // PART)
        ]
        total = jnp.concatenate([x.reshape(BLK, PART, PAIR) for x in total], axis=1)
        return pass_on(t, total, partial_b, ring_b, rb_send, rb_recv)

    def gather(t, chosen, copies):
        for copy in copies:
            copy.wait_recv()
        total = dot(chosen, answers_a[places[t]].reshape(width * PART, WIDE)).reshape(BLK, PART, WIDE)
        return pass_on(t, total, partial_a, ring_a, ra_send, ra_recv)

    pending = []
    for t in range(planes):
        copies = spread(t)
        chosen = choose(t)
        if t == planes - 1:
            for copy in own:
                copy.wait_recv()
            some = jnp.concatenate(
                [own_pairs[h, :, :SHARED].reshape(HEADS * SHARED, PAIR) for h in range(HEADS)], axis=1
            )
            queries = jnp.concatenate(
                [
                    jnp.concatenate(
                        [own_queries[h, :, :, :HD], own_queries[h, :, :, HD:]], axis=1
                    ).reshape(HEADS * BLOCK, HD)
                    for h in range(HEADS)
                ],
                axis=1,
            )
            everything = features_ref[...].reshape(HEADS * BLOCK, WIDE)
            acc[...] += dot(some, features_ref[:, :SHARED].reshape(HEADS * SHARED, WIDE), TN)
            single_weight = dot(queries, everything, TN)
            base[...] = norm_ref[...] + dot(queries, singles[...], NT).reshape(HEADS, BLOCK, WIDE)
            base[:, :SHARED] += dot(some, pairs[...], NT).reshape(HEADS, SHARED, WIDE)
        total = gather_late(t, chosen)
        if t == planes - 1:
            late_sums[...] = (grads_ref[:BLK, SHARED:].astype(jnp.float32) + total).astype(jnp.bfloat16)
            tail = to_heads(3, lambda h: late_sums.at[blocks_of(h)], own_pairs.at[head, :, late])
            begin(tail)
            own_pairs[head, :, SHARED:] = late_sums[own_blocks]
        pending.append((t, chosen, copies))

    def gather_some(count):
        for _ in range(min(count, len(pending) - 1)):
            gather(*pending.pop(0))

    gather_some(1)
    for copy in tail:
        copy.wait_recv()
    some = jnp.concatenate(
        [own_pairs[h, :, SHARED:].reshape(HEADS * low, PAIR) for h in range(HEADS)], axis=1
    )
    pair_weight = acc[...] + dot(some, features_ref[:, SHARED:].reshape(HEADS * low, WIDE), TN)
    for h in range(HEADS):
        terms = jnp.concatenate(
            [single_weight[h * HD : (h + 1) * HD], pair_weight[h * PAIR : (h + 1) * PAIR]], axis=0
        )
        terms = jnp.concatenate([terms[:, :BLOCK], terms[:, BLOCK:]], axis=0)
        in_mine[h] = terms.astype(jnp.bfloat16)
        if h == 0:
            in_own = jnp.where(head == 0, terms, 0.0)
        else:
            in_own = in_own + jnp.where(head == h, terms, 0.0)
    in_low = to_heads(5, lambda h: in_mine.at[h], in_in.at[head])
    begin(in_low)

    def exchange(peers, source, target, send, recv):
        copies = [
            remote(source(d, peer), target(d), send.at[d], recv.at[d], peer) for d, peer in enumerate(peers)
        ]
        begin(copies)
        return copies

    gather_some(2)
    for copy in out_copies + in_low:
        copy.wait_recv()
    out_in[head] = out_mine[head]
    in_total = in_own
    for _, h in x_peers:
        in_total = in_total + in_in[h].astype(jnp.float32)
    out_total = out_in[0] + out_in[1] + out_in[2] + out_in[3]
    x_sum[...] = jnp.concatenate([in_total, out_total], axis=0).reshape(x_sum.shape)
    copies = exchange(
        g_peers, lambda d, peer: x_sum.at[peer[0] % group], lambda d: g_in.at[d], wg_send, wg_recv
    )
    gather_some(2)
    for copy in copies:
        copy.wait_recv()
    total = x_sum[g]
    for d in range(group - 1):
        total = total + g_in[d]
    g_sum[...] = total
    copies = exchange(
        z_peers, lambda d, peer: g_sum.at[peer[0] // group], lambda d: z_in.at[d], wz_send, wz_recv
    )
    gather_some(planes)
    for copy in copies:
        copy.wait_recv()
    total = g_sum[z]
    for d in range(planes - 1):
        total = total + z_in[d]
    piece[...] = total
    sum_ref[g, z] = total
    copies = exchange(z_peers, lambda d, peer: piece, lambda d: sum_ref.at[g, z], bz_send, bz_recv)
    summed[...] = gather(*pending.pop(0)).astype(jnp.bfloat16)
    final = to_heads(4, lambda h: summed.at[blocks_of(h)], quarters.at[head])
    begin(final)
    quarters[head] = summed[own_blocks]
    for copy in copies:
        copy.wait_recv()
    copies = exchange(g_peers, lambda d, peer: sum_ref.at[g], lambda d: sum_ref.at[g], bg_send, bg_recv)
    base[:, SHARED:] += dot(some, pairs[...], NT).reshape(HEADS, low, WIDE)
    feature_ref[:, SHARED:] = base[:, SHARED:].astype(jnp.bfloat16)
    for copy in final:
        copy.wait_recv()
    for h in range(HEADS):
        rows = slice(h * PART, (h + 1) * PART)
        feature_ref[:, rows] = (base[:, rows] + quarters[h].astype(jnp.float32)).astype(jnp.bfloat16)
    for copy in copies:
        copy.wait_recv()
    for copy in sent:
        copy.wait_send()


def give_back(grads, dq, shared, features, norm_grad, in_weight, out_grad, asks, node_count):
    planes, group = torus(node_count)
    rows = 4 * HD * 2 // (planes * group)
    late = BLOCK - SHARED
    dma = lambda *shape: pltpu.SemaphoreType.DMA(shape)
    vmem = pl.BlockSpec(memory_space=pltpu.VMEM)
    low = lambda *shape: pltpu.VMEM(shape, jnp.bfloat16)
    high = lambda *shape: pltpu.VMEM(shape, jnp.float32)
    both = lambda *shape: [dma(*shape)] * 2
    feature_grad, total = pl.pallas_call(
        functools.partial(return_kernel, planes, group),
        out_shape=(
            jax.ShapeDtypeStruct((HEADS, BLOCK, WIDE), jnp.bfloat16),
            jax.ShapeDtypeStruct((group, planes, rows, 128), jnp.float32),
        ),
        in_specs=[vmem] * 7 + [pl.BlockSpec(memory_space=pltpu.SMEM)],
        out_specs=(vmem,) * 2,
        scratch_shapes=[
            low(WIDE, HEADS * PAIR),
            low(WIDE, HEADS * HD),
            low(HEADS, HEADS, BLOCK, PAIR),
            low(HEADS, HEADS, HD, PAIR),
            low(planes, HEADS, group * CAP, PART, PAIR),
            low(planes, group, CAP, PART, WIDE),
            low(planes, group, CAP, PART, WIDE),
            low(planes, group, CAP, late, PAIR),
            low(planes, BLK, PART, WIDE),
            low(planes, BLK, late, PAIR),
            low(2, planes // 2, BLK, PART, WIDE),
            low(2, planes // 2, BLK, late, PAIR),
            low(BLK, PART, WIDE),
            low(BLK, late, PAIR),
            low(HEADS, HEADS, PART, WIDE),
            high(HEADS * PAIR, WIDE),
            high(HEADS, BLOCK, WIDE),
            high(HEADS, 2 * HD, 128),
            high(HEADS, 2 * HD, 128),
            low(HEADS, 6 * HD, 128),
            low(HEADS, 6 * HD, 128),
            high(group, planes, rows, 128),
            high(group - 1, planes, rows, 128),
            high(planes, rows, 128),
            high(planes - 1, rows, 128),
            high(rows, 128),
            *both(6, 3), *both(planes, 3), *both(planes, group - 1), *both(planes, group - 1),
            *both(2, planes // 2), *both(2, planes // 2),
            *both(group - 1), *both(planes - 1), *both(planes - 1), *both(group - 1),
        ],
        compiler_params=pltpu.CompilerParams(
            collective_id=3, has_side_effects=True, vmem_limit_bytes=56 << 20
        ),
        name="give_back",
    )(grads, dq, shared, features.reshape(HEADS, BLOCK, WIDE), norm_grad, in_weight, out_grad, asks)
    total = total.reshape(4 * HD * 2, 128)
    in_total, out_total = total[: 6 * HD], total[6 * HD :]
    in_total = jnp.concatenate([in_total[: 3 * HD], in_total[3 * HD :]], axis=1)
    out_total = jnp.concatenate([out_total[:HD], out_total[HD:]], axis=1)
    return feature_grad.reshape(HEADS * BLOCK, WIDE), in_total.T, out_total


def on_device(features, in_weight, out_weight, cotangent, key_slots, block_count, wanted):
    node_count = lax.axis_size("node")
    total_nodes = BLK * BLOCK * node_count
    table, shared, asks, both, stat, output, norm_grad, out_weight_grad = fetch(
        features, in_weight, out_weight, cotangent, key_slots, block_count, wanted, node_count
    )
    dq, grads = backward(key_slots.reshape(-1), block_count, both, stat, table)
    feature_grad, in_weight_grad, out_weight_grad = give_back(
        grads, dq, shared, features, norm_grad, in_weight, out_weight_grad, asks, node_count
    )
    grad_factor = total_nodes ** (-0.5)
    return (
        output.reshape(features.shape),
        feature_grad,
        in_weight_grad * grad_factor,
        out_weight_grad * grad_factor,
    )


def solution(mesh):
    placed = (
        P(("node", "head"), None),
        P(),
        P(),
        P(("node", "head"), None),
        P("node", None),
        P("node"),
        P("node", None, None),
    )
    return jax.shard_map(
        on_device,
        mesh=mesh,
        in_specs=placed,
        out_specs=(
            P(("node", "head"), None),
            P(("node", "head"), None),
            P(None, "head"),
            P("head", None),
        ),
        check_vma=False,
    )
```

```python
import functools

import jax
import jax.numpy as jnp
from jax import lax
from jax.experimental import pallas as pl
from jax.experimental.pallas import tpu as pltpu
from jax.sharding import PartitionSpec as P

HEADS = 4
HD = 64
BLOCK = 128
BLK = 16
PER = 12
CAP = 2
PAIR = 2 * HD
PAIRED = 2
WIDE = 2 * BLOCK
SHARED = BLOCK // 2
PART = SHARED // HEADS
LUMP = PART + (BLOCK - SHARED) // 2
SCALE = HD ** (-0.5)
NT = (((1,), (1,)), ((), ()))
TN = (((0,), (0,)), ((), ()))
MESH = pl.DeviceIdType.MESH


def dot(a, b, dims=(((1,), (0,)), ((), ()))):
    return lax.dot_general(a, b, dims, preferred_element_type=jnp.float32)


def unpack(packed):
    return jnp.concatenate([packed[..., :HD], packed[..., HD:]], axis=-2)


def pack(rows):
    return jnp.concatenate([rows[..., :HD, :], rows[..., HD:, :]], axis=-1)


def attend(query, chosen, count):
    query = jnp.concatenate([query, jnp.zeros_like(query)], axis=1)
    scores = []
    for j in range(0, PER, 2):
        pair = dot(query, jnp.concatenate(chosen[j : j + 2], axis=0), NT)
        for i in range(2):
            dead = jnp.where(j + i < count, 0.0, -1e30)
            scores.append(pair[:, i * BLOCK : (i + 1) * BLOCK] + dead)
    highest = scores[0]
    for part in scores[1:]:
        highest = jnp.maximum(highest, part)
    highest = jnp.max(highest, axis=1, keepdims=True)
    total = jnp.zeros((BLOCK, BLOCK), jnp.float32)
    result = jnp.zeros((BLOCK, PAIR), jnp.float32)
    for j in range(0, PER, 2):
        raised = [jnp.exp(part - highest) for part in scores[j : j + 2]]
        total = total + raised[0] + raised[1]
        result = result + dot(
            jnp.concatenate([x.astype(jnp.bfloat16) for x in raised], axis=1),
            jnp.concatenate(chosen[j : j + 2], axis=0),
        )
    total = jnp.sum(total, axis=1, keepdims=True)
    return (result / total).astype(jnp.bfloat16), highest, total


def backward_kernel(slots_ref, count_ref, both_ref, stat_ref, table_ref, dq_ref, grads_ref, acc_ref, keys_ref, terms_ref):
    step = pl.program_id(0)

    @pl.when(step == 0)
    def _():
        acc_ref[...] = jnp.zeros_like(acc_ref)

    stacks, slots = [], []
    for i in range(PAIRED):
        b = step * PAIRED + i
        count = count_ref[b]
        both = both_ref[i]
        lane = lax.broadcasted_iota(jnp.int32, both.shape, 1)
        zero = jnp.zeros_like(both)
        stacked = jnp.concatenate(
            [jnp.where(lane < HD, both, zero), jnp.where(lane < HD, zero, both)], axis=0
        )
        stacks.append(stacked)
        highest, dots, inverse = stat_ref[i, 0:1], stat_ref[i, 1:2], stat_ref[i, 2:3]
        slots.append([slots_ref[b, j] for j in range(PER)])
        for j in range(PER):
            keys_ref[i, j * BLOCK : (j + 1) * BLOCK] = table_ref[slots[i][j]]
        for j in range(0, PER, 2):
            products = dot(keys_ref[i, j * BLOCK : (j + 2) * BLOCK], stacked, NT)
            for k in range(2):
                rows = slice(k * BLOCK, (k + 1) * BLOCK)
                top = highest + jnp.where(j + k < count, 0.0, 1e30)
                attention = jnp.exp(products[rows, :BLOCK] - top) * inverse
                score_grad = attention * (products[rows, BLOCK:] - dots)
                terms_ref[i, (j + k) * BLOCK : (j + k + 1) * BLOCK] = jnp.concatenate(
                    [score_grad.astype(jnp.bfloat16), attention.astype(jnp.bfloat16)], axis=1
                )
    for i in range(PAIRED):
        dq = dot(keys_ref[i], terms_ref[i, :, :BLOCK], TN)
        dq = (dq.T * SCALE).astype(jnp.bfloat16)
        dq_ref[i] = pack(dq[:, :HD])
        for j in range(0, PER, 2):
            grads = dot(terms_ref[i, j * BLOCK : (j + 2) * BLOCK], stacks[i])
            for k in range(2):
                acc_ref[slots[i][j + k]] += grads[k * BLOCK : (k + 1) * BLOCK]

    @pl.when(step == pl.num_programs(0) - 1)
    def _():
        grads_ref[...] = acc_ref[...].astype(jnp.bfloat16)


def backward(slots, count, both, stat, table):
    whole = lambda shape: pl.BlockSpec(shape, lambda b, *_: (0,) * len(shape))
    some = lambda *shape: pl.BlockSpec((PAIRED,) + shape, lambda b, *_: (b, 0, 0))
    grid_spec = pltpu.PrefetchScalarGridSpec(
        num_scalar_prefetch=2,
        grid=(BLK // PAIRED,),
        in_specs=[some(BLOCK, PAIR), some(8, BLOCK), whole(table.shape)],
        out_specs=[some(HD, PAIR), whole(table.shape)],
        scratch_shapes=[
            pltpu.VMEM(table.shape, jnp.float32),
            pltpu.VMEM((PAIRED, PER * BLOCK, PAIR), jnp.bfloat16),
            pltpu.VMEM((PAIRED, PER * BLOCK, 2 * BLOCK), jnp.bfloat16),
        ],
    )
    return pl.pallas_call(
        backward_kernel,
        grid_spec=grid_spec,
        out_shape=(
            jax.ShapeDtypeStruct((BLK, HD, PAIR), jnp.bfloat16),
            jax.ShapeDtypeStruct(table.shape, jnp.bfloat16),
        ),
        compiler_params=pltpu.CompilerParams(vmem_limit_bytes=56 << 20),
        cost_estimate=pl.CostEstimate(
            flops=10 * BLK * PER * BLOCK**3, bytes_accessed=16 << 20, transcendentals=BLK * PER * BLOCK**2
        ),
        name="attend_back",
    )(slots, count, both, stat, table)


def torus(node_count):
    rows = 4 if node_count >= 64 else 2
    return node_count // (2 * rows), rows * 2


def ring_order(planes):
    half = planes // 2
    return [0] + [s * k for k in range(1, half) for s in (-1, 1)] + [half]


def quarter(h):
    return pl.ds(pl.multiple_of(h * PART, PART), PART)


def remote(source, target, send, recv, peer):
    return pltpu.make_async_remote_copy(
        source, target, send, recv, device_id=peer, device_id_type=MESH
    )


def neighbours(planes, group):
    node, head = lax.axis_index("node"), lax.axis_index("head")
    z, g = node // group, node % group
    x_peers = [(node, (head + d) % HEADS) for d in range(1, HEADS)]
    g_peers = [(z * group + (g + d) % group, head) for d in range(1, group)]
    right = (((z + 1) % planes) * group + g, head)
    left = (((z + planes - 1) % planes) * group + g, head)
    return head, z, g, x_peers, g_peers, right, left


def greet(peers):
    barrier = pltpu.get_barrier_semaphore()
    for peer in peers:
        pl.semaphore_signal(barrier, inc=1, device_id=peer, device_id_type=MESH)
    return lambda: pl.semaphore_wait(barrier, len(peers))


def fetch_kernel(
    planes, group, own_ref, asked_ref, weight_ref, out_weight_ref, cotangent_ref, slots_ref, count_ref,
    table_ref, shared_ref, asks_ref, both_ref, stat_ref, output_ref, norm_ref, out_grad_ref,
    query_ref, packed, highs, sums, att_in, att_rows, low_grad, my_grads, grad_in,
    pairs, my_pairs, my_queries, ring_a, ring_b, chunk_a, chunk_b, picked_a, picked_b, landed, made, asks,
    o_send, o_recv, q_send, q_recv, ra_send, ra_recv, rb_send, rb_recv,
    ga_send, ga_recv, gb_send, gb_recv, x_send, x_recv, asks_sem,
):
    head, z, g, x_peers, g_peers, right, left = neighbours(planes, group)
    half = planes // 2
    width = group * CAP
    rows = HEADS * BLOCK
    late = pl.ds(SHARED, BLOCK - SHARED)
    own_blocks = pl.ds(head * HEADS, HEADS)
    arrive = greet(x_peers + g_peers + [right, left])

    ring_a[z, own_blocks] = own_ref[:, quarter(head)]
    weight = weight_ref[...]
    step = 3 * HD
    for h in range(HEADS):
        pairs[:, h * PAIR : (h + 1) * PAIR] = weight[:, h * step + HD : (h + 1) * step]
    own = own_ref[...].reshape(rows, WIDE)
    for h in range(HEADS):
        both = dot(own, pairs[:, h * PAIR : (h + 1) * PAIR]).astype(jnp.bfloat16)
        my_pairs[h] = both.reshape(HEADS, BLOCK, PAIR)
        queries = (dot(own, weight[:, h * step : h * step + HD]) * SCALE).astype(jnp.bfloat16)
        my_queries[h] = pack(queries.reshape(HEADS, BLOCK, HD))
    arrive()

    def own_copies(kind, source, target):
        return [
            remote(source(peer[1]), target, o_send.at[kind, d], o_recv.at[kind, d], peer)
            for d, peer in enumerate(x_peers)
        ]

    early = pl.ds(0, SHARED)
    corner = own_copies(0, lambda h: own_ref.at[:, quarter(h)], ring_a.at[z, own_blocks])
    lower = own_copies(1, lambda h: my_pairs.at[h, :, late], table_ref.at[own_blocks, late])
    upper = own_copies(2, lambda h: my_pairs.at[h, :, early], table_ref.at[own_blocks, early])
    asking = own_copies(3, lambda h: my_queries.at[h], query_ref.at[own_blocks])
    questions = [
        remote(asked_ref.at[peer[0] % group], asks_ref.at[g], q_send.at[d], q_recv.at[d], peer)
        for d, peer in enumerate(g_peers)
    ]
    sent = []

    def begin(copies):
        for copy in copies:
            copy.start()
            sent.append(copy)

    begin(corner + questions + lower + upper + asking)
    table_ref[own_blocks] = my_pairs[head]
    query_ref[own_blocks] = my_queries[head]
    asks_ref[g] = asked_ref[g]

    def hop(ring, send, recv, way, k):
        at = (z - k + planes) % planes if way == 0 else (z + k) % planes
        view = ring.at[at]
        if k == half - 1:
            view = view.at[pl.ds(way * (BLK // 2), BLK // 2)]
        return remote(view, view, send.at[way, k], recv.at[way, k], left if way else right)

    def hops(ring, send, recv):
        return {(way, k): hop(ring, send, recv, way, k) for way in range(2) for k in range(half)}

    hops_a = hops(ring_a, ra_send, ra_recv)
    hops_b = hops(ring_b, rb_send, rb_recv)
    order = ring_order(planes)
    place = lambda t: (z + order[t] + planes) % planes

    def bring(hops, t):
        offset = order[t]
        if offset == 0:
            begin([hops[0, 0], hops[1, 0]])
        elif offset == half:
            hops[0, half - 1].wait_recv()
            hops[1, half - 1].wait_recv()
        else:
            way, k = (0, -offset) if offset < 0 else (1, offset)
            hops[way, k - 1].wait_recv()
            begin([hops[way, k]])

    def spot(at, owner):
        return pl.ds(BLK + (at * group + owner) * CAP, CAP)

    def copies_a(at):
        return [
            remote(picked_a.at[at, d], landed.at[at, g], ga_send.at[at, d], ga_recv.at[at, d], peer)
            for d, peer in enumerate(g_peers)
        ]

    def copies_b(at):
        return [
            remote(
                picked_b.at[at, d], table_ref.at[spot(at, g), late], gb_send.at[at, d], gb_recv.at[at, d], peer
            )
            for d, peer in enumerate(g_peers)
        ]

    def bring_a(t):
        at = place(t)
        bring(hops_a, t)
        chunk_a[...] = ring_a[at]
        copies = copies_a(at)
        for d, peer in enumerate(g_peers):
            for c in range(CAP):
                picked_a[at, d, c] = chunk_a[asks[peer[0] % group, 0, at * CAP + c]]
            begin([copies[d]])
        for c in range(CAP):
            landed[at, g, c] = chunk_a[asks[g, 0, at * CAP + c]]

    def bring_b(t):
        at = place(t)
        bring(hops_b, t)
        chunk_b[...] = ring_b[at]
        copies = copies_b(at)
        for d, peer in enumerate(g_peers):
            for c in range(CAP):
                picked_b[at, d, c] = chunk_b[asks[peer[0] % group, 0, at * CAP + c]]
            begin([copies[d]])
        for c in range(CAP):
            table_ref[BLK + (at * group + g) * CAP + c, SHARED:] = chunk_b[asks[g, 0, at * CAP + c]]

    arriving = []

    def make(t):
        at = place(t)
        for copy in copies_a(at):
            copy.wait_recv()
        shared = landed[at].reshape(width * PART, WIDE)
        shared_ref[at] = shared
        both = dot(shared, pairs[...]).astype(jnp.bfloat16)
        for h in range(HEADS):
            made[at, h] = both[:, h * PAIR : (h + 1) * PAIR].reshape(width, PART, PAIR)
        slots = pl.ds(BLK + at * width, width)
        copies = [
            remote(
                made.at[at, peer[1]], table_ref.at[slots, quarter(head)], x_send.at[at, d], x_recv.at[at, d],
                peer,
            )
            for d, peer in enumerate(x_peers)
        ]
        begin(copies)
        arriving.extend(copies)
        table_ref[slots, quarter(head)] = made[at, head]

    for copy in corner:
        copy.wait_recv()
    for copy in questions:
        copy.wait_recv()
    answer = pltpu.make_async_copy(asks_ref, asks, asks_sem)
    answer.start()
    answer.wait()
    bring_a(0)
    for copy in lower:
        copy.wait_recv()
    ring_b[z] = table_ref[:BLK, SHARED:]
    bring_b(0)
    pairs_of = [[t, t + 1] for t in range(1, planes - 1, 2)] + [[planes - 1]]
    before = [0]
    for now in pairs_of:
        for t in now:
            bring_a(t)
        for t in before:
            make(t)
        for t in now:
            bring_b(t)
        before = now
    for t in before:
        make(t)
    for copy in upper + asking + arriving:
        copy.wait_recv()
    for t in range(planes):
        for copy in copies_b(place(t)):
            copy.wait_recv()

    attended = own_copies(
        4, lambda h: packed.at[pl.ds(h * HEADS, HEADS)], att_in.at[head]
    )
    for d in list(range(1, HEADS)) + [0]:
        base = (head + d) % HEADS * HEADS

        @pl.loop(0, HEADS // PAIRED)
        def _(i):
            blocks = [base + i * PAIRED + k for k in range(PAIRED)]
            chosen = [[table_ref[slots_ref[b, j]] for j in range(PER)] for b in blocks]
            results = [
                attend(unpack(query_ref[b]), some, count_ref[b]) for b, some in zip(blocks, chosen)
            ]
            for b, (result, highest, total) in zip(blocks, results):
                packed[b] = pack(result[:, HD:])
                both_ref[b] = result
                highs[b] = jnp.broadcast_to(highest, (BLOCK, BLOCK))
                sums[b] = jnp.broadcast_to(total, (BLOCK, BLOCK))

        if d:
            begin([attended[d - 1]])
    att_in[head] = packed[own_blocks]
    for copy in attended:
        copy.wait_recv()

    @pl.loop(0, HEADS, unroll=True)
    def _(i):
        att = jnp.concatenate([unpack(att_in[h, i]) for h in range(HEADS)], axis=1)
        att_rows[i] = att
        summed = own_ref[i].astype(jnp.float32) + dot(att, out_weight_ref[...])
        root_mean = jnp.sqrt(jnp.mean(summed * summed, axis=-1, keepdims=True) + 1e-06)
        normed = summed / root_mean
        output_ref[i] = normed.astype(jnp.bfloat16)
        upstream = cotangent_ref[i].astype(jnp.float32)
        grad = (upstream - normed * jnp.mean(upstream * normed, axis=-1, keepdims=True)) / root_mean
        norm_ref[i] = grad
        low_grad[i] = grad.astype(jnp.bfloat16)
        back = dot(grad.astype(jnp.bfloat16), out_weight_ref[...], NT).astype(jnp.bfloat16)
        for h in range(HEADS):
            my_grads[h, i] = pack(back[:, h * HD : (h + 1) * HD])

    back = own_copies(5, lambda h: my_grads.at[h], grad_in.at[own_blocks])
    begin(back)
    grad_in[own_blocks] = my_grads[head]
    out_grad_ref[...] = dot(
        att_rows[...].reshape(rows, WIDE), low_grad[...].reshape(rows, WIDE), TN
    )
    for copy in back:
        copy.wait_recv()

    @pl.loop(0, BLK // 4)
    def _(i):
        done = []
        for k in range(4):
            b = i * 4 + k
            grad, result = unpack(grad_in[b]), both_ref[b][:, HD:]
            dots = jnp.sum(grad.astype(jnp.float32) * result.astype(jnp.float32), axis=1, keepdims=True)
            lane = lax.broadcasted_iota(jnp.int32, (BLOCK, BLOCK), 1)
            stat = jnp.where(lane == 0, highs[b], jnp.where(lane == 1, dots, 1.0 / sums[b]))
            done.append((b, stat.T[:8], jnp.concatenate([unpack(query_ref[b]), grad], axis=1)))
        for b, stat, both in done:
            stat_ref[b] = stat
            both_ref[b] = both

    for copy in sent:
        copy.wait_send()


def fetch(features, in_weight, out_weight, cotangent, key_slots, block_count, wanted, node_count):
    planes, group = torus(node_count)
    own = features.reshape(HEADS, BLOCK, WIDE)
    asked = wanted.reshape(planes, group, CAP).transpose(1, 0, 2).reshape(group, 1, planes * CAP)
    asked = jnp.pad(asked, ((0, 0), (0, 7), (0, 128 - planes * CAP)))
    dma = lambda *shape: pltpu.SemaphoreType.DMA(shape)
    vmem = pl.BlockSpec(memory_space=pltpu.VMEM)
    low = lambda *shape: pltpu.VMEM(shape, jnp.bfloat16)
    late = BLOCK - SHARED
    slots = BLK + planes * group * CAP
    return pl.pallas_call(
        functools.partial(fetch_kernel, planes, group),
        out_shape=(
            jax.ShapeDtypeStruct((slots, BLOCK, PAIR), jnp.bfloat16),
            jax.ShapeDtypeStruct((planes, group * CAP * PART, WIDE), jnp.bfloat16),
            jax.ShapeDtypeStruct((group, 8, 128), jnp.int32),
            jax.ShapeDtypeStruct((BLK, BLOCK, PAIR), jnp.bfloat16),
            jax.ShapeDtypeStruct((BLK, 8, BLOCK), jnp.float32),
            jax.ShapeDtypeStruct((HEADS, BLOCK, WIDE), jnp.bfloat16),
            jax.ShapeDtypeStruct((HEADS, BLOCK, WIDE), jnp.float32),
            jax.ShapeDtypeStruct((WIDE, WIDE), jnp.float32),
        ),
        in_specs=[vmem] * 5 + [pl.BlockSpec(memory_space=pltpu.SMEM)] * 2,
        out_specs=(vmem,) * 8,
        scratch_shapes=[
            low(BLK, HD, PAIR),
            low(BLK, HD, PAIR),
            pltpu.VMEM((BLK, BLOCK, BLOCK), jnp.float32),
            pltpu.VMEM((BLK, BLOCK, BLOCK), jnp.float32),
            low(HEADS, HEADS, HD, PAIR),
            low(HEADS, BLOCK, WIDE),
            low(HEADS, BLOCK, WIDE),
            low(HEADS, HEADS, HD, PAIR),
            low(BLK, HD, PAIR),
            low(WIDE, HEADS * PAIR),
            low(HEADS, HEADS, BLOCK, PAIR),
            low(HEADS, HEADS, HD, PAIR),
            low(planes, BLK, PART, WIDE),
            low(planes, BLK, late, PAIR),
            low(BLK, PART, WIDE),
            low(BLK, late, PAIR),
            low(planes, group - 1, CAP, PART, WIDE),
            low(planes, group - 1, CAP, late, PAIR),
            low(planes, group, CAP, PART, WIDE),
            low(planes, HEADS, group * CAP, PART, PAIR),
            pltpu.SMEM((group, 8, 128), jnp.int32),
            dma(6, 3), dma(6, 3), dma(group - 1), dma(group - 1),
            dma(2, planes // 2), dma(2, planes // 2), dma(2, planes // 2), dma(2, planes // 2),
            dma(planes, group - 1), dma(planes, group - 1), dma(planes, group - 1), dma(planes, group - 1),
            dma(planes, 3), dma(planes, 3),
            pltpu.SemaphoreType.DMA,
        ],
        compiler_params=pltpu.CompilerParams(
            collective_id=2, has_side_effects=True, vmem_limit_bytes=56 << 20
        ),
        name="fetch",
    )(own, asked, in_weight, out_weight, cotangent.reshape(own.shape), key_slots, block_count)


def return_kernel(
    planes, group, grads_ref, dq_ref, shared_ref, features_ref, norm_ref, weight_ref, out_ref, asks_ref,
    feature_ref, sum_ref,
    pairs, singles, own_pairs, own_queries, heads, leaving, answers_a, answers_b, partial_a, partial_b,
    ring_a, ring_b, summed, late_sums, quarters, acc, base,
    out_mine, out_in, in_mine, in_in, x_sum, g_in, g_sum, z_in, piece,
    o_send, o_recv, x_send, x_recv, ga_send, ga_recv, gb_send, gb_recv, ra_send, ra_recv, rb_send, rb_recv,
    wg_send, wg_recv, wz_send, wz_recv, bz_send, bz_recv, bg_send, bg_recv,
):
    head, z, g, x_peers, g_peers, right, left = neighbours(planes, group)
    z_peers = [(((z + d) % planes) * group + g, head) for d in range(1, planes)]
    half = planes // 2
    width = group * CAP
    low = BLOCK - SHARED
    early, late = pl.ds(0, SHARED), pl.ds(SHARED, low)
    own_blocks = pl.ds(head * HEADS, HEADS)
    arrive = greet(x_peers + g_peers + z_peers)

    weight = weight_ref[...]
    step = 3 * HD
    for h in range(HEADS):
        pairs[:, h * PAIR : (h + 1) * PAIR] = weight[:, h * step + HD : (h + 1) * step]
    singles[...] = jnp.concatenate(
        [weight[:, h * step : h * step + HD] for h in range(HEADS)], axis=1
    )
    for h in range(HEADS):
        some = out_ref[h * HD : (h + 1) * HD]
        out_mine[h] = jnp.concatenate([some[:, :BLOCK], some[:, BLOCK:]], axis=0)
    arrive()

    order = list(reversed(ring_order(planes)))
    places = [(z + offset + planes) % planes for offset in order]
    spot = lambda at, owner: pl.ds(BLK + (at * group + owner) * CAP, CAP)
    slots = lambda at: pl.ds(BLK + at * width, width)
    sent = []

    def begin(copies):
        for copy in copies:
            copy.start()
            sent.append(copy)

    def to_heads(kind, source, target):
        return [
            remote(source(peer[1]), target, o_send.at[kind, d], o_recv.at[kind, d], peer)
            for d, peer in enumerate(x_peers)
        ]

    blocks_of = lambda h: pl.ds(h * HEADS, HEADS)
    own = to_heads(0, lambda h: grads_ref.at[blocks_of(h), early], own_pairs.at[head, :, early])
    own += to_heads(1, lambda h: dq_ref.at[blocks_of(h)], own_queries.at[head])
    out_copies = to_heads(2, lambda h: out_mine.at[h], out_in.at[head])
    far = [
        [
            remote(
                grads_ref.at[slots(at), quarter(peer[1])], heads.at[at, head],
                x_send.at[at, d], x_recv.at[at, d], peer,
            )
            for d, peer in enumerate(x_peers)
        ]
        for at in places
    ]
    far_late = [
        [
            remote(
                grads_ref.at[spot(at, peer[0] % group), late], answers_b.at[at, g],
                gb_send.at[at, d], gb_recv.at[at, d], peer,
            )
            for d, peer in enumerate(g_peers)
        ]
        for at in places
    ]
    ahead = 3
    for t in range(min(ahead, planes)):
        begin(far[t])
        begin(far_late[t])
    acc[...] = jnp.zeros_like(acc)
    own_pairs[head, :, :SHARED] = grads_ref[own_blocks, :SHARED]
    own_queries[head] = dq_ref[own_blocks]

    def spread(t):
        at = places[t]
        heads[at, head] = grads_ref[slots(at), quarter(head)]
        for copy in far[t]:
            copy.wait_recv()
        if t + ahead < planes:
            begin(far[t + ahead])
            begin(far_late[t + ahead])
        if t + ahead == planes - 1:
            begin(own + out_copies)
        some = jnp.concatenate([heads[at, h].reshape(width * PART, PAIR) for h in range(HEADS)], axis=1)
        back = dot(some, pairs[...], NT).astype(jnp.bfloat16)
        leaving[at] = back.reshape(group, CAP, PART, WIDE)
        copies = [
            remote(
                leaving.at[at, peer[0] % group], answers_a.at[at, g], ga_send.at[at, d], ga_recv.at[at, d], peer
            )
            for d, peer in enumerate(g_peers)
        ]
        begin(copies)
        answers_a[at, g] = leaving[at, g]
        acc[...] += dot(some, shared_ref[at], TN)
        return copies

    def choose(t):
        at = places[t]
        side = width * PART
        column = lax.broadcasted_iota(jnp.int32, (1, side), 1)
        target = column % PART
        for j in range(width):
            block = asks_ref[j // CAP, 0, at * CAP + j % CAP]
            target = target + jnp.where(column // PART == j, block * PART, 0)
        row = lax.broadcasted_iota(jnp.int32, (BLK * PART, side), 0)
        return jnp.where(row == target, 1.0, 0.0).astype(jnp.bfloat16)

    def pass_on(t, total, partial, ring, send, recv):
        at, offset = places[t], order[t]
        mid = BLK // 2

        def hop(way, k):
            source, target = partial.at[at], ring.at[way, k]
            if k == 0:
                blocks = pl.ds(way * mid, mid)
                source, target = source.at[blocks], target.at[blocks]
            return remote(source, target, send.at[way, k], recv.at[way, k], left if way else right)

        if offset == half:
            partial[at] = total.astype(jnp.bfloat16)
            begin([hop(0, 0), hop(1, 0)])
            return None
        k = half - 1 - abs(offset)
        ways = [0] if offset > 0 else [1] if offset < 0 else [0, 1]
        for way in ways:
            hop(way, k).wait_recv()
            if k:
                total = total + ring[way, k].astype(jnp.float32)
            elif way:
                total = jnp.concatenate([total[:mid], total[mid:] + ring[way, k, mid:].astype(jnp.float32)], axis=0)
            else:
                total = jnp.concatenate([total[:mid] + ring[way, k, :mid].astype(jnp.float32), total[mid:]], axis=0)
        if offset:
            partial[at] = total.astype(jnp.bfloat16)
            begin([hop(ways[0], k + 1)])
            return None
        return total

    def gather_late(t, chosen):
        at = places[t]
        for copy in far_late[t]:
            copy.wait_recv()
        answers_b[at, g] = grads_ref[spot(at, g), SHARED:]
        total = [
            dot(chosen, answers_b[at, :, :, i * PART : (i + 1) * PART].reshape(width * PART, PAIR))
            for i in range(low // PART)
        ]
        total = jnp.concatenate([x.reshape(BLK, PART, PAIR) for x in total], axis=1)
        return pass_on(t, total, partial_b, ring_b, rb_send, rb_recv)

    def gather(t, chosen, copies):
        for copy in copies:
            copy.wait_recv()
        total = dot(chosen, answers_a[places[t]].reshape(width * PART, WIDE)).reshape(BLK, PART, WIDE)
        return pass_on(t, total, partial_a, ring_a, ra_send, ra_recv)

    pending = []
    for t in range(planes):
        copies = spread(t)
        chosen = choose(t)
        if t == planes - 1:
            for copy in own:
                copy.wait_recv()
            some = jnp.concatenate(
                [own_pairs[h, :, :SHARED].reshape(HEADS * SHARED, PAIR) for h in range(HEADS)], axis=1
            )
            queries = jnp.concatenate(
                [
                    jnp.concatenate(
                        [own_queries[h, :, :, :HD], own_queries[h, :, :, HD:]], axis=1
                    ).reshape(HEADS * BLOCK, HD)
                    for h in range(HEADS)
                ],
                axis=1,
            )
            everything = features_ref[...].reshape(HEADS * BLOCK, WIDE)
            acc[...] += dot(some, features_ref[:, :SHARED].reshape(HEADS * SHARED, WIDE), TN)
            single_weight = dot(queries, everything, TN)
            base[...] = norm_ref[...] + dot(queries, singles[...], NT).reshape(HEADS, BLOCK, WIDE)
            base[:, :SHARED] += dot(some, pairs[...], NT).reshape(HEADS, SHARED, WIDE)
        total = gather_late(t, chosen)
        if t == planes - 1:
            late_sums[...] = (grads_ref[:BLK, SHARED:].astype(jnp.float32) + total).astype(jnp.bfloat16)
            tail = to_heads(3, lambda h: late_sums.at[blocks_of(h)], own_pairs.at[head, :, late])
            begin(tail)
            own_pairs[head, :, SHARED:] = late_sums[own_blocks]
        pending.append((t, chosen, copies))

    def gather_some(count):
        for _ in range(min(count, len(pending) - 1)):
            gather(*pending.pop(0))

    gather_some(1)
    for copy in tail:
        copy.wait_recv()
    some = jnp.concatenate(
        [own_pairs[h, :, SHARED:].reshape(HEADS * low, PAIR) for h in range(HEADS)], axis=1
    )
    pair_weight = acc[...] + dot(some, features_ref[:, SHARED:].reshape(HEADS * low, WIDE), TN)
    for h in range(HEADS):
        terms = jnp.concatenate(
            [single_weight[h * HD : (h + 1) * HD], pair_weight[h * PAIR : (h + 1) * PAIR]], axis=0
        )
        terms = jnp.concatenate([terms[:, :BLOCK], terms[:, BLOCK:]], axis=0)
        in_mine[h] = terms.astype(jnp.bfloat16)
        if h == 0:
            in_own = jnp.where(head == 0, terms, 0.0)
        else:
            in_own = in_own + jnp.where(head == h, terms, 0.0)
    in_low = to_heads(5, lambda h: in_mine.at[h], in_in.at[head])
    begin(in_low)

    def exchange(peers, source, target, send, recv):
        copies = [
            remote(source(d, peer), target(d), send.at[d], recv.at[d], peer) for d, peer in enumerate(peers)
        ]
        begin(copies)
        return copies

    gather_some(2)
    for copy in out_copies + in_low:
        copy.wait_recv()
    out_in[head] = out_mine[head]
    in_total = in_own
    for _, h in x_peers:
        in_total = in_total + in_in[h].astype(jnp.float32)
    out_total = out_in[0] + out_in[1] + out_in[2] + out_in[3]
    x_sum[...] = jnp.concatenate([in_total, out_total], axis=0).reshape(x_sum.shape)
    copies = exchange(
        g_peers, lambda d, peer: x_sum.at[peer[0] % group], lambda d: g_in.at[d], wg_send, wg_recv
    )
    gather_some(2)
    for copy in copies:
        copy.wait_recv()
    total = x_sum[g]
    for d in range(group - 1):
        total = total + g_in[d]
    g_sum[...] = total
    copies = exchange(
        z_peers, lambda d, peer: g_sum.at[peer[0] // group], lambda d: z_in.at[d], wz_send, wz_recv
    )
    gather_some(planes)
    for copy in copies:
        copy.wait_recv()
    total = g_sum[z]
    for d in range(planes - 1):
        total = total + z_in[d]
    piece[...] = total
    sum_ref[g, z] = total
    copies = exchange(z_peers, lambda d, peer: piece, lambda d: sum_ref.at[g, z], bz_send, bz_recv)
    summed[...] = gather(*pending.pop(0)).astype(jnp.bfloat16)
    final = to_heads(4, lambda h: summed.at[blocks_of(h)], quarters.at[head])
    begin(final)
    quarters[head] = summed[own_blocks]
    for copy in copies:
        copy.wait_recv()
    copies = exchange(g_peers, lambda d, peer: sum_ref.at[g], lambda d: sum_ref.at[g], bg_send, bg_recv)
    base[:, SHARED:] += dot(some, pairs[...], NT).reshape(HEADS, low, WIDE)
    feature_ref[:, SHARED:] = base[:, SHARED:].astype(jnp.bfloat16)
    for copy in final:
        copy.wait_recv()
    for h in range(HEADS):
        rows = slice(h * PART, (h + 1) * PART)
        feature_ref[:, rows] = (base[:, rows] + quarters[h].astype(jnp.float32)).astype(jnp.bfloat16)
    for copy in copies:
        copy.wait_recv()
    for copy in sent:
        copy.wait_send()


def give_back(grads, dq, shared, features, norm_grad, in_weight, out_grad, asks, node_count):
    planes, group = torus(node_count)
    rows = 4 * HD * 2 // (planes * group)
    late = BLOCK - SHARED
    dma = lambda *shape: pltpu.SemaphoreType.DMA(shape)
    vmem = pl.BlockSpec(memory_space=pltpu.VMEM)
    low = lambda *shape: pltpu.VMEM(shape, jnp.bfloat16)
    high = lambda *shape: pltpu.VMEM(shape, jnp.float32)
    both = lambda *shape: [dma(*shape)] * 2
    feature_grad, total = pl.pallas_call(
        functools.partial(return_kernel, planes, group),
        out_shape=(
            jax.ShapeDtypeStruct((HEADS, BLOCK, WIDE), jnp.bfloat16),
            jax.ShapeDtypeStruct((group, planes, rows, 128), jnp.float32),
        ),
        in_specs=[vmem] * 7 + [pl.BlockSpec(memory_space=pltpu.SMEM)],
        out_specs=(vmem,) * 2,
        scratch_shapes=[
            low(WIDE, HEADS * PAIR),
            low(WIDE, HEADS * HD),
            low(HEADS, HEADS, BLOCK, PAIR),
            low(HEADS, HEADS, HD, PAIR),
            low(planes, HEADS, group * CAP, PART, PAIR),
            low(planes, group, CAP, PART, WIDE),
            low(planes, group, CAP, PART, WIDE),
            low(planes, group, CAP, late, PAIR),
            low(planes, BLK, PART, WIDE),
            low(planes, BLK, late, PAIR),
            low(2, planes // 2, BLK, PART, WIDE),
            low(2, planes // 2, BLK, late, PAIR),
            low(BLK, PART, WIDE),
            low(BLK, late, PAIR),
            low(HEADS, HEADS, PART, WIDE),
            high(HEADS * PAIR, WIDE),
            high(HEADS, BLOCK, WIDE),
            high(HEADS, 2 * HD, 128),
            high(HEADS, 2 * HD, 128),
            low(HEADS, 6 * HD, 128),
            low(HEADS, 6 * HD, 128),
            high(group, planes, rows, 128),
            high(group - 1, planes, rows, 128),
            high(planes, rows, 128),
            high(planes - 1, rows, 128),
            high(rows, 128),
            *both(6, 3), *both(planes, 3), *both(planes, group - 1), *both(planes, group - 1),
            *both(2, planes // 2), *both(2, planes // 2),
            *both(group - 1), *both(planes - 1), *both(planes - 1), *both(group - 1),
        ],
        compiler_params=pltpu.CompilerParams(
            collective_id=3, has_side_effects=True, vmem_limit_bytes=56 << 20
        ),
        name="give_back",
    )(grads, dq, shared, features.reshape(HEADS, BLOCK, WIDE), norm_grad, in_weight, out_grad, asks)
    total = total.reshape(4 * HD * 2, 128)
    in_total, out_total = total[: 6 * HD], total[6 * HD :]
    in_total = jnp.concatenate([in_total[: 3 * HD], in_total[3 * HD :]], axis=1)
    out_total = jnp.concatenate([out_total[:HD], out_total[HD:]], axis=1)
    return feature_grad.reshape(HEADS * BLOCK, WIDE), in_total.T, out_total


def on_device(features, in_weight, out_weight, cotangent, key_slots, block_count, wanted):
    node_count = lax.axis_size("node")
    total_nodes = BLK * BLOCK * node_count
    table, shared, asks, both, stat, output, norm_grad, out_weight_grad = fetch(
        features, in_weight, out_weight, cotangent, key_slots, block_count, wanted, node_count
    )
    dq, grads = backward(key_slots, block_count, both, stat, table)
    feature_grad, in_weight_grad, out_weight_grad = give_back(
        grads, dq, shared, features, norm_grad, in_weight, out_weight_grad, asks, node_count
    )
    grad_factor = total_nodes ** (-0.5)
    return (
        output.reshape(features.shape),
        feature_grad,
        in_weight_grad * grad_factor,
        out_weight_grad * grad_factor,
    )


def solution(mesh):
    placed = (
        P(("node", "head"), None),
        P(),
        P(),
        P(("node", "head"), None),
        P("node", None),
        P("node"),
        P("node", None, None),
    )
    return jax.shard_map(
        on_device,
        mesh=mesh,
        in_specs=placed,
        out_specs=(
            P(("node", "head"), None),
            P(("node", "head"), None),
            P(None, "head"),
            P("head", None),
        ),
        check_vma=False,
    )
```
